128 devices in a mesh: px: 16 (over z, x), py: 8 (over y, core).
Axes of the slice: x: 4, y: 4, z: 4, core: 2. Of those that a mesh axis runs over, the one named last changes fastest.
Arguments:
- state_old: float32 [5, 64, 131072], P(None, None, ('px', 'py'))
- level_old: int32 [131072], P(('px', 'py')), may hold values 0 or 1
- morton_old: int32 [131072], P(('px', 'py')), may hold values from -1 to 65535, as said below
- neighbours: int32 [6, 65536], P(None, ('px', 'py')), may hold values from 0 to 65535, as said below
Outputs:
- new_state: float32 [5, 64, 65536], P(None, None, ('px', 'py'))
- rate: float32 [5, 64, 65536], P(None, None, ('px', 'py'))
The draws below stay inside these ranges and needn't reach their ends.
Inputs may be any that keep to these rules, and one draw needn't show every extreme that they name: `morton_old`: every element 0 to 65535 stands in exactly one slot; the other slots hold -1. The element of old device d goes to new device d, d + 1 or d - 1 along the curve, which closes (device 0 follows the last). Every device sends 1 to 256 elements to the next device, always the lowest-ranked of that device's elements, and 1 to 255 to the previous one, always the highest-ranked of that device's elements; both bounds are reached on some device. `neighbours`: every neighbour of a device's element lies on that device or on a device 1, 2, 3 or 4 steps before or after it along the curve (the curve closes: device 0 follows the last). For each device, exactly 128 of its faces have their neighbour on the next device and exactly 128 on the previous one, and at most 128 on each device 2 to 4 steps away, reached on some device. A face whose neighbour is on the same device never has the element itself as neighbour.
All inputs are finite; a program needn't handle non-finite values. No bound on the sum of `level_old` on one device may be relied on, other than what follows from the above.
Results may differ from the reference program's by a relative error of at most 0.0003.
Values sent between devices are 32-bit elements; how exact they have to be, the bound alone decides.
No kernel may reach another device: no remote copies, remote signals or barrier semaphores. Data moves between devices by JAX's collectives and lax.ppermute only.
A program may use at most 128 MiB of HBM per device.

```python
import math
import jax
import jax.numpy as jnp
import numpy as np
from jax import lax

FIELDS = 5
DOFS = 64
NEW_DEV = 512
GHOST_CAP = 128
OLD_CAP = 1024
OLD_ALL = 131072
NEW_ALL = 65536
N_PX = 16
N_PY = 8


def draw_state_old(key, part):
    key = jax.random.fold_in(key, 11)
    subkeys = jax.random.split(key, 3)
    grid_shape = (DOFS, OLD_ALL)
    density = jnp.exp(jax.random.uniform(subkeys[0], grid_shape, jnp.float32, math.log(0.5), math.log(2.0)))
    velocity = 0.5 * jax.random.truncated_normal(subkeys[1], -3.0, 3.0, (3,) + grid_shape, jnp.float32)
    pressure = jnp.exp(jax.random.uniform(subkeys[2], grid_shape, jnp.float32, math.log(0.5), math.log(2.0)))
    momentum = density * velocity
    energy = pressure / 0.4 + 0.5 * density * (velocity[0] * velocity[0] + velocity[1] * velocity[1] + velocity[2] * velocity[2])
    return jnp.concatenate([density[None], momentum, energy[None]], axis=0).astype(jnp.float32)


def draw_morton_old(key, part):
    key = jax.random.fold_in(key, 12)
    devices = OLD_ALL // OLD_CAP
    half_dev = NEW_DEV // 2
    subkeys = jax.random.split(key, 5)
    ahead_counts = jax.random.randint(subkeys[0], (devices,), 1, half_dev + 1).astype(jnp.int32)
    behind_counts = jax.random.randint(subkeys[1], (devices,), 1, half_dev).astype(jnp.int32)
    ahead_counts = ahead_counts.at[jax.random.randint(subkeys[2], (), 0, devices)].set(half_dev)
    behind_counts = behind_counts.at[jax.random.randint(subkeys[3], (), 0, devices)].set(half_dev - 1)
    device_ids = jnp.arange(devices, dtype=jnp.int32)[:, None]
    next_ids = (device_ids + 1) % devices
    prior_ids = (device_ids + devices - 1) % devices
    half_cols = jnp.arange(half_dev, dtype=jnp.int32)[None, :]
    full_cols = jnp.arange(NEW_DEV, dtype=jnp.int32)[None, :]
    head_part = jnp.where(half_cols < ahead_counts[next_ids], next_ids * NEW_DEV + half_cols, -1)
    tail_part = jnp.where(half_cols < behind_counts[prior_ids], prior_ids * NEW_DEV + NEW_DEV - 1 - half_cols, -1)
    keep_mid = (full_cols >= ahead_counts[device_ids]) & (full_cols < NEW_DEV - behind_counts[device_ids])
    middle_part = jnp.where(keep_mid, device_ids * NEW_DEV + full_cols, -1)
    candidates = jnp.concatenate([head_part, middle_part, tail_part], axis=1).astype(jnp.int32)
    orders = jax.vmap(lambda subkey: jax.random.permutation(subkey, OLD_CAP))(jax.random.split(subkeys[4], devices)).astype(jnp.int32)
    return jnp.take_along_axis(candidates, orders, axis=1).reshape(-1).astype(jnp.int32)


def draw_neighbours(key, part):
    key = jax.random.fold_in(key, 13)
    devices = NEW_ALL // NEW_DEV
    face_slots = 6 * NEW_DEV
    subkeys = jax.random.split(key, 6)
    steps_table = jnp.array([-4, -3, -2, -1, 1, 2, 3, 4], jnp.int32)
    far_table = jnp.array([0, 1, 2, 5, 6, 7], jnp.int32)
    adjacent = jnp.abs(steps_table) == 1
    far_counts = jax.random.randint(subkeys[0], (devices, 8), 0, GHOST_CAP + 1).astype(jnp.int32)
    quotas = jnp.where(adjacent[None, :], GHOST_CAP, far_counts).astype(jnp.int32)
    chosen_device = jax.random.randint(subkeys[4], (), 0, devices)
    chosen_step = far_table[jax.random.randint(subkeys[5], (), 0, 6)]
    quotas = quotas.at[chosen_device, chosen_step].set(GHOST_CAP)
    bounds = jnp.cumsum(quotas, axis=1, dtype=jnp.int32)
    positions = jax.vmap(lambda subkey: jax.random.permutation(subkey, face_slots))(jax.random.split(subkeys[1], devices)).astype(jnp.int32)
    buckets = jax.vmap(lambda bounds_row, positions_row: jnp.searchsorted(bounds_row, positions_row, side='right'))(bounds, positions).astype(jnp.int32)
    device_ids = jnp.arange(devices, dtype=jnp.int32)[:, None]
    moved = (device_ids + steps_table[jnp.minimum(buckets, 7)] + devices) % devices
    peers = jnp.where(buckets < 8, moved, device_ids).astype(jnp.int32)
    far_slot = jax.random.randint(subkeys[2], (devices, face_slots), 0, NEW_DEV).astype(jnp.int32)
    own_slot = jnp.arange(face_slots, dtype=jnp.int32)[None, :] % NEW_DEV
    near_slot = (own_slot + 1 + jax.random.randint(subkeys[3], (devices, face_slots), 0, NEW_DEV - 1).astype(jnp.int32)) % NEW_DEV
    element_slots = jnp.where(peers == device_ids, near_slot, far_slot)
    global_ranks = peers * NEW_DEV + element_slots
    return jnp.transpose(global_ranks.reshape(devices, 6, NEW_DEV), (1, 0, 2)).reshape(6, NEW_ALL).astype(jnp.int32)


def touch_ends(result, key, least, top_value):
    extent = result.shape
    index_at = [jax.random.randint(jax.random.fold_in(key, axis), (), 0, extent[axis]) for axis in range(len(extent))]
    result = result.at[tuple(index_at)].set(least)
    longest = extent.index(max(extent))
    index_at[longest] = (index_at[longest] + 1) % extent[longest]
    return result.at[tuple(index_at)].set(top_value)


def setup_inputs(seed: int = 0) -> dict:
    key_of = jax.random.split(jax.random.key(seed), 5)
    return {
        "state_old": draw_state_old(jax.random.fold_in(key_of[4], 71), 0),
        "level_old": touch_ends((jax.random.randint(key_of[1], (OLD_ALL,), 0, 2) < 1).astype(jnp.int32), jax.random.fold_in(key_of[1], 1), 0, 1),
        "morton_old": draw_morton_old(jax.random.fold_in(key_of[4], 71), 0),
        "neighbours": draw_neighbours(jax.random.fold_in(key_of[4], 71), 0),
    }


heat_ratio = 1.4
speed_bound = 4.0
time_step = 0.0002
opposite_faces = (1, 0, 3, 2, 5, 4)

def node_tables():
    points = np.array([-1.0, -1.0 / np.sqrt(5.0), 1.0 / np.sqrt(5.0), 1.0])
    bary_weights = np.array([1.0 / np.prod([points[col_id] - points[other] for other in range(4) if other != col_id]) for col_id in range(4)])
    derivative = np.zeros((4, 4))
    for row_id in range(4):
        for col_id in range(4):
            if row_id != col_id:
                derivative[row_id, col_id] = bary_weights[col_id] / bary_weights[row_id] / (points[row_id] - points[col_id])
        derivative[row_id, row_id] = -np.sum(derivative[row_id])
    identity = np.eye(4)
    stacked = np.concatenate([np.kron(np.kron(derivative, identity), identity), np.kron(np.kron(identity, derivative), identity), np.kron(np.kron(identity, identity), derivative)], axis=1)
    lifting = np.zeros((64, 96))
    for face_id in range(6):
        direction = face_id // 2
        edge_index = 3 * (face_id % 2)
        for node_id in range(16):
            first_idx = node_id // 4
            second_idx = node_id % 4
            if direction == 0:
                node_spot = (edge_index, first_idx, second_idx)
            elif direction == 1:
                node_spot = (first_idx, edge_index, second_idx)
            else:
                node_spot = (first_idx, second_idx, edge_index)
            lifting[node_spot[0] * 16 + node_spot[1] * 4 + node_spot[2], face_id * 16 + node_id] = 1.0
    return (jnp.asarray(stacked, jnp.float32), jnp.asarray(lifting, jnp.float32))

def face_traces(fields):
    columns = fields.shape[-1]
    cube = fields.reshape(fields.shape[0], 4, 4, 4, columns)
    pieces = [cube[:, 0], cube[:, 3], cube[:, :, 0], cube[:, :, 3], cube[:, :, :, 0], cube[:, :, :, 3]]
    return jnp.stack([piece.reshape(fields.shape[0], 16, columns) for piece in pieces])

def axis_flux(state, direction):
    density = state[0]
    momentum = state[1:4]
    energy = state[4]
    velocity = momentum / density
    pressure = (heat_ratio - 1.0) * (energy - 0.5 * (momentum[0] * velocity[0] + momentum[1] * velocity[1] + momentum[2] * velocity[2]))
    normal_speed = velocity[direction]
    flux_rows = [momentum[direction]]
    for component in range(3):
        moment_flux = momentum[component] * normal_speed
        if component == direction:
            moment_flux = moment_flux + pressure
        flux_rows.append(moment_flux)
    flux_rows.append((energy + pressure) * normal_speed)
    return jnp.stack(flux_rows)

def rate_block(fields, level, outer_side):
    stacked, lifting = node_tables()
    metric = jnp.where(level > 0, 2.0, 1.0).astype(fields.dtype)
    volume_flux = jnp.concatenate([axis_flux(fields, direction) for direction in range(3)], axis=1)
    volume = jnp.einsum('pq,fqe->fpe', stacked.astype(fields.dtype), volume_flux, precision=lax.Precision.HIGHEST)
    inner_side = face_traces(fields)
    jump_terms = []
    for face_id in range(6):
        direction = face_id // 2
        normal_sign = 1.0 if face_id % 2 else -1.0
        flux_in = axis_flux(inner_side[face_id], direction)
        flux_out = axis_flux(outer_side[face_id], direction)
        jump_terms.append(normal_sign * (flux_out - flux_in) - speed_bound * (outer_side[face_id] - inner_side[face_id]))
    jump_all = jnp.stack(jump_terms, axis=1).reshape(fields.shape[0], 96, fields.shape[-1])
    surface = jnp.einsum('pg,fge->fpe', lifting.astype(fields.dtype), jump_all, precision=lax.Precision.HIGHEST)
    return -metric * (volume + 3.0 * surface)

def global_rate(fields, level, neighbours):
    devices = N_PX * N_PY
    traces = face_traces(fields)

    def one_block(block_id):
        first_col = block_id * NEW_DEV
        own_fields = lax.dynamic_slice_in_dim(fields, first_col, NEW_DEV, 2)
        own_level = lax.dynamic_slice_in_dim(level, first_col, NEW_DEV, 0)
        own_links = lax.dynamic_slice_in_dim(neighbours, first_col, NEW_DEV, 1)
        outer_side = jnp.stack([jnp.take(traces[opposite_faces[face_id]], own_links[face_id], axis=2) for face_id in range(6)])
        return rate_block(own_fields, own_level, outer_side)
    blocks = lax.map(one_block, jnp.arange(devices, dtype=jnp.int32))
    return jnp.transpose(blocks, (1, 2, 0, 3)).reshape(fields.shape)

def reference(state_old, level_old, morton_old, neighbours):
    occupied = morton_old >= 0
    curve_ranks = jnp.where(occupied, morton_old, NEW_ALL).astype(jnp.int32)
    start_fields = jnp.zeros((FIELDS, DOFS, NEW_ALL), state_old.dtype).at[:, :, curve_ranks].set(state_old, mode='drop')
    element_level = jnp.zeros((NEW_ALL,), jnp.int32).at[curve_ranks].set(level_old, mode='drop')
    rate_first = global_rate(start_fields, element_level, neighbours)
    section_fields = start_fields + time_step * rate_first
    rate_second = global_rate(section_fields, element_level, neighbours)
    new_state = 0.5 * start_fields + 0.5 * (section_fields + time_step * rate_second)
    return (new_state, rate_second)
```

```python
import jax
import jax.numpy as jnp
import numpy as np
from jax import lax
from jax.experimental import pallas as pl
from jax.experimental.pallas import tpu as pltpu
from jax.sharding import PartitionSpec as P

FIELDS = 5
DOFS = 64
ROWS = FIELDS * DOFS
NEW_DEV = 512
HALF = NEW_DEV // 2
OLD_CAP = 1024
CAP = 128
TRACE_ROWS = FIELDS * 16
MOVED_ROWS = ROWS + 8
BLOCKS = NEW_DEV // 128

HEAT = 1.4
SPEED = 4.0
DT = 0.0002
AXES = ("px", "py")
F32 = jnp.float32
BF16 = jnp.bfloat16
I32 = jnp.int32

STEPS = (2, 3, 4, 1, -1, -2, -3, -4)


def derivative_table():
    points = np.array([-1.0, -1.0 / np.sqrt(5.0), 1.0 / np.sqrt(5.0), 1.0])
    weights = np.array(
        [1.0 / np.prod([points[c] - points[o] for o in range(4) if o != c]) for c in range(4)]
    )
    table = np.zeros((4, 4))
    for r in range(4):
        for c in range(4):
            if r != c:
                table[r, c] = weights[c] / weights[r] / (points[r] - points[c])
        table[r, r] = -np.sum(table[r])
    return table


def stacked_table():
    d = derivative_table().astype(np.float32).astype(np.float64)
    one = np.eye(4)
    full = np.concatenate(
        [
            np.kron(np.kron(d, one), one),
            np.kron(np.kron(one, d), one),
            np.kron(np.kron(one, one), d),
        ],
        axis=1,
    ).astype(np.float32)
    high = full.astype(jnp.bfloat16)
    low = (full - high.astype(np.float32)).astype(jnp.bfloat16)
    return np.concatenate([high, low], axis=0)


def split(x):
    high = x.astype(BF16)
    low = (x - high.astype(F32)).astype(BF16)
    return high, low


def dot(a, b):
    return lax.dot_general(a, b, (((1,), (0,)), ((), ())), preferred_element_type=F32)


def dot_nt(a, b):
    return lax.dot_general(a, b, (((1,), (1,)), ((), ())), preferred_element_type=F32)


def one_hot_rows(size, row):
    spots = lax.broadcasted_iota(I32, (size, row.shape[1]), 0)
    return jnp.where(spots == row, 1.0, 0.0).astype(BF16)


def relay_slots(me, morton):
    occupied = morton >= 0
    owner = morton >> 9
    slot = morton & (NEW_DEV - 1)
    gap = (owner - me) & 127
    even = (me & 1) == 0
    to_next = occupied & (gap == 1)
    to_prior = occupied & (gap == 127)
    home = jnp.where(occupied & (gap == 0), slot, -1)
    ahead = jnp.where(to_next, slot, -1)
    behind = jnp.where(to_prior, slot - HALF, -1)
    sib = jnp.where(even, ahead, behind)
    far = jnp.where(even, behind, ahead)
    return sib, far, home


def stacked_rows(state, level):
    high, low = split(state)
    lev = jnp.broadcast_to(level.astype(F32), (16, OLD_CAP)).astype(BF16)
    return jnp.concatenate([high, low, lev], axis=0)


def store_moved(ref, got):
    ref[0:ROWS, :] = got[0:ROWS] + got[ROWS : 2 * ROWS]
    ref[ROWS : ROWS + 8, :] = got[2 * ROWS : 2 * ROWS + 8]


def pack_kernel(me_ref, state_ref, level_ref, morton_ref, far_ref, sib_ref):
    sib, far, _ = relay_slots(me_ref[0], morton_ref[...])
    lhs = stacked_rows(state_ref[...], level_ref[...])
    store_moved(far_ref, dot_nt(lhs, one_hot_rows(HALF, far)))
    store_moved(sib_ref, dot_nt(lhs, one_hot_rows(HALF, sib)))


def home_kernel(me_ref, state_ref, level_ref, morton_ref, home_ref):
    _, _, home = relay_slots(me_ref[0], morton_ref[...])
    lhs = stacked_rows(state_ref[...], level_ref[...])
    got = dot_nt(lhs, one_hot_rows(NEW_DEV, home))
    for c in range(BLOCKS):
        store_moved(home_ref.at[c], got[:, 128 * c : 128 * c + 128])


def request_kernel(me_ref, links_ref, ask_ref, near_ref, far_ref):
    me = me_ref[0]
    links = links_ref[...]
    owner = links >> 9
    slot = links & (NEW_DEV - 1)
    gap = ((owner - me + 192) & 127) - 64
    gap = jnp.where((me & 1) == 0, gap, -gap)
    near_ref[...] = jnp.where(gap == 0, slot, -1)
    b = lax.broadcasted_iota(I32, (8, NEW_DEV), 0)
    step_of = jnp.where(b < 3, b + 2, jnp.where(b == 3, 1, 3 - b))
    masks = [jnp.where(gap[f : f + 1, :] == step_of, 1.0, 0.0) for f in range(6)]
    k = lax.broadcasted_iota(I32, (NEW_DEV, NEW_DEV), 0)
    j = lax.broadcasted_iota(I32, (NEW_DEV, NEW_DEV), 1)
    upper = jnp.where(k <= j, 1.0, 0.0).astype(BF16)
    counts = dot(jnp.concatenate(masks, axis=0).astype(BF16), upper)
    offset = jnp.full((8, 1), -1.0, F32)
    bf = b.astype(F32)
    total = jnp.zeros((16, CAP), F32)
    for f in range(6):
        run = counts[8 * f : 8 * f + 8, :]
        here = gap[f : f + 1, :] != 0
        rank = jnp.sum(masks[f] * (run + offset), axis=0, keepdims=True)
        bucket = jnp.sum(masks[f] * bf, axis=0, keepdims=True)
        offset = offset + run[:, NEW_DEV - 1 : NEW_DEV]
        rank = jnp.where(here, rank.astype(I32), -1)
        far_ref[f : f + 1, :] = jnp.where(here, bucket.astype(I32) * CAP + rank, -1)
        s = slot[f : f + 1, :]
        low = (s & 255).astype(F32)
        high = ((s >> 8) + 2 * (f ^ 1)).astype(F32)
        lhs = jnp.concatenate([masks[f] * low, masks[f] * high], axis=0).astype(BF16)
        total = total + dot_nt(lhs, one_hot_rows(CAP, rank))
    ask_ref[...] = total[0:8].astype(I32) + 256 * total[8:16].astype(I32)


def lower_half(shape):
    return lax.broadcasted_iota(I32, shape, 0) < 4


def trace(ref, c, v, f):
    a, s = f // 2, f % 2
    at = v * DOFS
    if a == 0:
        return ref[c, at + 48 * s : at + 48 * s + 16, :]
    if a == 1:
        out = []
        for h in range(2):
            r = at + 32 * h + 8 * s
            x = ref[c, r : r + 8, :]
            y = ref[c, r + 16 : r + 24, :]
            low = lower_half(x.shape)
            if s == 0:
                out.append(jnp.where(low, x, pltpu.roll(y, 4, 0)))
            else:
                out.append(jnp.where(low, pltpu.roll(x, 4, 0), y))
        return jnp.concatenate(out, axis=0)
    return ref[c, pl.ds(at + 3 * s, 16, stride=4), :]


def add_on_face(ref, c, v, f, x):
    a, s = f // 2, f % 2
    at = v * DOFS
    if a == 0:
        ref[c, at + 48 * s : at + 48 * s + 16, :] += x
    elif a == 1:
        for h in range(2):
            y = x[8 * h : 8 * h + 8, :]
            low = lower_half(y.shape)
            keep = low if s == 0 else ~low
            turned = pltpu.roll(y, 4, 0)
            first, second = (y, turned) if s == 0 else (turned, y)
            r = at + 32 * h + 8 * s
            ref[c, r : r + 8, :] += jnp.where(keep, first, 0.0)
            ref[c, r + 16 : r + 24, :] += jnp.where(keep, second, 0.0)
    else:
        spot = (c, pl.ds(at + 3 * s, 16, stride=4), slice(None))
        ref[spot] = ref[spot] + x


def wide(ref, rows):
    return jnp.concatenate([ref[c, 0:rows, :] for c in range(ref.shape[0])], axis=1)


def pressure_of(w, u):
    return (HEAT - 1.0) * (w[4] - 0.5 * (w[1] * u[0] + w[2] * u[1] + w[3] * u[2]))


def axis_flux(w, u, p, a):
    un = u[a]
    out = [w[1 + a]]
    for c in range(3):
        m = w[1 + c] * un
        out.append(m + p if c == a else m)
    out.append((w[4] + p) * un)
    return out


def side_term(w, a, sign):
    u = [w[1 + c] / w[0] for c in range(3)]
    p = pressure_of(w, u)
    flux = axis_flux(w, u, p, a)
    return [(sign * flux[v]) - SPEED * w[v] for v in range(FIELDS)]


def reply(fields, ask_ref, got_ref, own_ref, swap_ref):
    ask = ask_ref[...]
    code = jnp.concatenate([ask[t : t + 1, :] for t in range(8)], axis=1)
    hot = one_hot_rows(NEW_DEV, code & (NEW_DEV - 1))
    high, low = split(fields)
    both = dot(jnp.concatenate([high, low], axis=0), hot)
    for t in range(8):
        spot = slice(CAP * t, CAP * t + CAP)
        got_ref[t] = both[0:ROWS, spot] + both[ROWS:, spot]
    for t in range(8):
        face = ask[t : t + 1, :] >> 9
        for v in range(FIELDS):
            x = trace(got_ref, t, v, 0)
            for f in range(1, 6):
                x = jnp.where(face == f, trace(got_ref, t, v, f), x)
            if t < 3:
                own_ref[t, 16 * v : 16 * v + 16, :] = x
            else:
                swap_ref[t - 3, 16 * v : 16 * v + 16, :] = x


def first_kernel(me_ref, home_ref, far_ref, sib_ref, ask_ref, start_ref, own_ref, swap_ref, got_ref):
    even = (me_ref[0] & 1) == 0
    for c in range(2):
        spot = slice(128 * c, 128 * c + 128)
        sib = sib_ref[:, spot]
        far = far_ref[:, spot]
        start_ref[c] = home_ref[c] + jnp.where(even, far, sib)
        start_ref[c + 2] = home_ref[c + 2] + jnp.where(even, sib, far)
    reply(wide(start_ref, ROWS), ask_ref, got_ref, own_ref, swap_ref)


def near_kernel(table_ref, fields_ref, near_ref, part_ref, high_ref, low_ref):
    for c in range(BLOCKS):
        spot = slice(128 * c, 128 * c + 128)
        w = [fields_ref[c, DOFS * v : DOFS * v + DOFS, :] for v in range(FIELDS)]
        u = [w[1 + i] / w[0] for i in range(3)]
        p = pressure_of(w, u)
        for a in range(3):
            flux = axis_flux(w, u, p, a)
            for v in range(FIELDS):
                high, low = split(flux[v])
                high_ref[v, DOFS * a : DOFS * a + DOFS, spot] = high
                low_ref[v, DOFS * a : DOFS * a + DOFS, spot] = low
    table = table_ref[...]
    for v in range(FIELDS):
        x = dot(table, high_ref[v])
        x = x[0:DOFS] + x[DOFS:] + dot(table[0:DOFS], low_ref[v])
        for c in range(BLOCKS):
            part_ref[c, DOFS * v : DOFS * v + DOFS, :] = x[:, 128 * c : 128 * c + 128]
    for f in range(6):
        a, sign = f // 2, 1.0 if f % 2 else -1.0
        mine = near_ref[f : f + 1, :]
        hot = one_hot_rows(NEW_DEV, mine)
        across = jnp.concatenate(
            [
                jnp.concatenate([trace(fields_ref, c, v, f ^ 1) for v in range(FIELDS)], axis=0)
                for c in range(BLOCKS)
            ],
            axis=1,
        )
        high, low = split(across)
        both = dot(jnp.concatenate([high, low], axis=0), hot)
        for c in range(BLOCKS):
            spot = slice(128 * c, 128 * c + 128)
            outer = both[0:TRACE_ROWS, spot] + both[TRACE_ROWS:, spot]
            there = mine[:, spot] >= 0
            plus = side_term(outer_fields(outer, there), a, sign)
            minus = side_term([trace(fields_ref, c, v, f) for v in range(FIELDS)], a, sign)
            for v in range(FIELDS):
                add_on_face(part_ref, c, v, f, 3.0 * (jnp.where(there, plus[v], 0.0) - minus[v]))


def outer_fields(outer, there):
    w = [outer[16 * v : 16 * v + 16] for v in range(FIELDS)]
    w[0] = jnp.where(there, w[0], 1.0)
    return w


def add_far(part_ref, far_ref, ghosts, sum_ref, lhs_ref):
    for t in range(8):
        high, low = split(ghosts[t])
        lhs_ref[0:TRACE_ROWS, CAP * t : CAP * t + CAP] = high
        lhs_ref[TRACE_ROWS:, CAP * t : CAP * t + CAP] = low
    sum_ref[...] = part_ref[...]
    lhs = lhs_ref[...]
    for f in range(6):
        a, sign = f // 2, 1.0 if f % 2 else -1.0
        place = far_ref[f : f + 1, :]
        both = dot(lhs, one_hot_rows(8 * CAP, place))
        for c in range(BLOCKS):
            spot = slice(128 * c, 128 * c + 128)
            outer = both[0:TRACE_ROWS, spot] + both[TRACE_ROWS:, spot]
            there = place[:, spot] >= 0
            plus = side_term(outer_fields(outer, there), a, sign)
            for v in range(FIELDS):
                add_on_face(sum_ref, c, v, f, 3.0 * jnp.where(there, plus[v], 0.0))


def metric_of(start_ref, c):
    return jnp.where(start_ref[c, ROWS : ROWS + 1, :] > 0.5, 2.0, 1.0)


def ghosts_of(a_ref, b_ref, swap_ref, post_ref):
    return [post_ref[1], post_ref[0], post_ref[2], swap_ref[0], a_ref[2], a_ref[0], b_ref[1], b_ref[0]]


def second_kernel(start_ref, part_ref, far_ref, ask_ref, a_ref, b_ref, swap_ref, post_ref,
                  section_ref, own_ref, out_ref, sum_ref, lhs_ref, got_ref):
    add_far(part_ref, far_ref, ghosts_of(a_ref, b_ref, swap_ref, post_ref), sum_ref, lhs_ref)
    for c in range(BLOCKS):
        section_ref[c] = start_ref[c, 0:ROWS, :] - (DT * metric_of(start_ref, c)) * sum_ref[c]
    reply(wide(section_ref, ROWS), ask_ref, got_ref, own_ref, out_ref)


def last_kernel(start_ref, section_ref, part_ref, far_ref, a_ref, b_ref, swap_ref, post_ref,
                state_ref, rate_ref, sum_ref, lhs_ref):
    add_far(part_ref, far_ref, ghosts_of(a_ref, b_ref, swap_ref, post_ref), sum_ref, lhs_ref)
    for c in range(BLOCKS):
        spot = slice(128 * c, 128 * c + 128)
        rate = -metric_of(start_ref, c) * sum_ref[c]
        rate_ref[:, spot] = rate
        state_ref[:, spot] = 0.5 * start_ref[c, 0:ROWS, :] + 0.5 * (section_ref[c] + DT * rate)


VM = pl.BlockSpec(memory_space=pltpu.VMEM)
SM = pl.BlockSpec(memory_space=pltpu.SMEM)


def call(kernel, outs, args, scalars=0, scratch=(), flops=0):
    return pl.pallas_call(
        kernel,
        out_shape=[jax.ShapeDtypeStruct(s, d) for s, d in outs],
        in_specs=[SM] * scalars + [VM] * (len(args) - scalars),
        out_specs=[VM] * len(outs),
        scratch_shapes=[pltpu.VMEM(s, d) for s, d in scratch],
        compiler_params=pltpu.CompilerParams(vmem_limit_bytes=40 * 2**20),
        cost_estimate=pl.CostEstimate(flops=flops, bytes_accessed=2**20, transcendentals=0),
    )(*args)


def swap_cores(x):
    n = lax.axis_size(AXES)
    return lax.ppermute(x, AXES, [(i, i ^ 1) for i in range(n)])


def swap_chips(x):
    n = lax.axis_size(AXES)
    return lax.ppermute(x, AXES, [(i, (i + (1 if i % 2 else -1)) % n) for i in range(n)])


def outward(x, by):
    n = lax.axis_size(AXES)
    return lax.ppermute(x, AXES, [(i, (i + (by if i % 2 == 0 else -by)) % n) for i in range(n)])


def exchange(own, swap):
    got = swap_cores(swap)
    b = outward(jnp.concatenate([own[2:3], got[3:5]], axis=0), 4)
    a = outward(jnp.concatenate([own[0:2], got[1:3]], axis=0), 2)
    post = swap_cores(jnp.concatenate([a[1:2], a[3:4], b[2:3]], axis=0))
    return a, b, got, post


def body(state_old, level_old, morton_old, neighbours):
    me = lax.axis_index(AXES).astype(I32).reshape(1)
    state = state_old.reshape(ROWS, OLD_CAP)
    level = level_old.reshape(1, OLD_CAP)
    morton = morton_old.reshape(1, OLD_CAP)

    ask, near, far = call(
        request_kernel,
        [((8, CAP), I32), ((6, NEW_DEV), I32), ((6, NEW_DEV), I32)],
        (me, neighbours),
        1,
    )
    ask = ask.reshape(8, 1, CAP)
    asked = jnp.concatenate(list(g for g in ghosts_of(*exchange(ask[0:3], ask[3:8]))), axis=0)

    to_far, to_sib = call(
        pack_kernel, [((MOVED_ROWS, HALF), F32)] * 2, (me, state, level, morton), 1
    )
    from_far = swap_chips(to_far)
    from_sib = swap_cores(to_sib)
    (home,) = call(home_kernel, [((BLOCKS, MOVED_ROWS, 128), F32)], (me, state, level, morton), 1)

    chunks = [((3, TRACE_ROWS, CAP), F32), ((5, TRACE_ROWS, CAP), F32)]
    got_scratch = ((8, ROWS, CAP), F32)
    sum_scratch = ((BLOCKS, ROWS, 128), F32)
    lhs_scratch = ((2 * TRACE_ROWS, 8 * CAP), BF16)
    table = jnp.asarray(stacked_table())

    def near_part(fields):
        return call(
            near_kernel,
            [((BLOCKS, ROWS, 128), F32)],
            (table, fields, near),
            0,
            [((FIELDS, 3 * DOFS, NEW_DEV), BF16)] * 2,
            flops=10**9,
        )[0]

    start, own, swap = call(
        first_kernel,
        [((BLOCKS, MOVED_ROWS, 128), F32)] + chunks,
        (me, home, from_far, from_sib, asked),
        1,
        [got_scratch],
    )
    came = exchange(own, swap)
    part = near_part(start)
    section, own, swap = call(
        second_kernel,
        [((BLOCKS, ROWS, 128), F32)] + chunks,
        (start, part, far, asked) + came,
        0,
        [sum_scratch, lhs_scratch, got_scratch],
    )
    came = exchange(own, swap)
    part = near_part(section)
    new_state, rate = call(
        last_kernel,
        [((ROWS, NEW_DEV), F32)] * 2,
        (start, section, part, far) + came,
        0,
        [sum_scratch, lhs_scratch],
    )
    shape = (FIELDS, DOFS, NEW_DEV)
    return new_state.reshape(shape), rate.reshape(shape)


def solution(mesh):
    wide = P(None, None, AXES)
    return jax.shard_map(
        body,
        mesh=mesh,
        in_specs=(wide, P(AXES), P(AXES), P(None, AXES)),
        out_specs=(wide, wide),
        check_vma=False,
    )
```

```python
import jax
import jax.numpy as jnp
import numpy as np
from jax import lax
from jax.experimental import pallas as pl
from jax.experimental.pallas import tpu as pltpu
from jax.sharding import PartitionSpec as P

FIELDS = 5
DOFS = 64
ROWS = FIELDS * DOFS
NEW_DEV = 512
HALF = NEW_DEV // 2
OLD_CAP = 1024
CAP = 128
TRACE_ROWS = FIELDS * 16
MOVED_ROWS = ROWS + 8
BLOCKS = NEW_DEV // 128

HEAT = 1.4
SPEED = 4.0
DT = 0.0002
AXES = ("px", "py")
F32 = jnp.float32
BF16 = jnp.bfloat16
I32 = jnp.int32

STEPS = (2, 3, 4, 1, -1, -2, -3, -4)


def derivative_table():
    points = np.array([-1.0, -1.0 / np.sqrt(5.0), 1.0 / np.sqrt(5.0), 1.0])
    weights = np.array(
        [1.0 / np.prod([points[c] - points[o] for o in range(4) if o != c]) for c in range(4)]
    )
    table = np.zeros((4, 4))
    for r in range(4):
        for c in range(4):
            if r != c:
                table[r, c] = weights[c] / weights[r] / (points[r] - points[c])
        table[r, r] = -np.sum(table[r])
    return table


def stacked_table():
    d = derivative_table().astype(np.float32).astype(np.float64)
    one = np.eye(4)
    full = np.concatenate(
        [
            np.kron(np.kron(d, one), one),
            np.kron(np.kron(one, d), one),
            np.kron(np.kron(one, one), d),
        ],
        axis=1,
    ).astype(np.float32)
    high = full.astype(jnp.bfloat16)
    low = (full - high.astype(np.float32)).astype(jnp.bfloat16)
    return np.concatenate([high, low], axis=0)


def split(x):
    high = x.astype(BF16)
    low = (x - high.astype(F32)).astype(BF16)
    return high, low


def dot(a, b):
    return lax.dot_general(a, b, (((1,), (0,)), ((), ())), preferred_element_type=F32)


def dot_nt(a, b):
    return lax.dot_general(a, b, (((1,), (1,)), ((), ())), preferred_element_type=F32)


def one_hot_rows(size, row):
    spots = lax.broadcasted_iota(I32, (size, row.shape[1]), 0)
    return jnp.where(spots == row, 1.0, 0.0).astype(BF16)


def relay_slots(me, morton):
    occupied = morton >= 0
    owner = morton >> 9
    slot = morton & (NEW_DEV - 1)
    gap = (owner - me) & 127
    even = (me & 1) == 0
    to_next = occupied & (gap == 1)
    to_prior = occupied & (gap == 127)
    home = jnp.where(occupied & (gap == 0), slot, -1)
    ahead = jnp.where(to_next, slot, -1)
    behind = jnp.where(to_prior, slot - HALF, -1)
    sib = jnp.where(even, ahead, behind)
    far = jnp.where(even, behind, ahead)
    return sib, far, home


def store_moved(ref, got):
    ref[0:ROWS, :] = got[0:ROWS] + got[ROWS : 2 * ROWS]
    ref[ROWS : ROWS + 8, :] = got[2 * ROWS : 2 * ROWS + 8]


def prepare_kernel(me_ref, links_hbm, state_hbm, level_hbm, morton_hbm, ask_ref, near_ref, far_ref,
                   slots_ref, rows_ref, links_ref, state_ref, level_ref, morton_ref, sems):
    pairs = ((links_hbm, links_ref), (morton_hbm, morton_ref), (level_hbm, level_ref), (state_hbm, state_ref))
    copies = [pltpu.make_async_copy(src, dst, sems.at[i]) for i, (src, dst) in enumerate(pairs)]
    for copy in copies:
        copy.start()
    copies[0].wait()
    requests(me_ref[0], links_ref[...], ask_ref, near_ref, far_ref)
    copies[1].wait()
    for i, row in enumerate(relay_slots(me_ref[0], morton_ref[...])):
        slots_ref[i : i + 1, :] = row
    copies[2].wait()
    rows_ref[2 * ROWS :, :] = jnp.broadcast_to(level_ref[...].astype(F32), (16, OLD_CAP)).astype(BF16)
    copies[3].wait()
    high, low = split(state_ref[...])
    rows_ref[0:ROWS, :] = high
    rows_ref[ROWS : 2 * ROWS, :] = low


def pack_kernel(rows_ref, slots_ref, far_ref, sib_ref):
    lhs = rows_ref[...]
    store_moved(far_ref, dot_nt(lhs, one_hot_rows(HALF, slots_ref[1:2, :])))
    store_moved(sib_ref, dot_nt(lhs, one_hot_rows(HALF, slots_ref[0:1, :])))


def home_kernel(rows_ref, slots_ref, home_ref):
    got = dot_nt(rows_ref[...], one_hot_rows(NEW_DEV, slots_ref[2:3, :]))
    for c in range(BLOCKS):
        store_moved(home_ref.at[c], got[:, 128 * c : 128 * c + 128])


def requests(me, links, ask_ref, near_ref, far_ref):
    owner = links >> 9
    slot = links & (NEW_DEV - 1)
    gap = ((owner - me + 192) & 127) - 64
    gap = jnp.where((me & 1) == 0, gap, -gap)
    near_ref[...] = jnp.where(gap == 0, slot, -1)
    b = lax.broadcasted_iota(I32, (8, NEW_DEV), 0)
    step_of = jnp.where(b < 3, b + 2, jnp.where(b == 3, 1, 3 - b))
    masks = [jnp.where(gap[f : f + 1, :] == step_of, 1.0, 0.0) for f in range(6)]
    k = lax.broadcasted_iota(I32, (NEW_DEV, NEW_DEV), 0)
    j = lax.broadcasted_iota(I32, (NEW_DEV, NEW_DEV), 1)
    upper = jnp.where(k <= j, 1.0, 0.0).astype(BF16)
    counts = dot(jnp.concatenate(masks, axis=0).astype(BF16), upper)
    offset = jnp.full((8, 1), -1.0, F32)
    bf = b.astype(F32)
    total = jnp.zeros((16, CAP), F32)
    for f in range(6):
        run = counts[8 * f : 8 * f + 8, :]
        here = gap[f : f + 1, :] != 0
        rank = jnp.sum(masks[f] * (run + offset), axis=0, keepdims=True)
        bucket = jnp.sum(masks[f] * bf, axis=0, keepdims=True)
        offset = offset + run[:, NEW_DEV - 1 : NEW_DEV]
        rank = jnp.where(here, rank.astype(I32), -1)
        far_ref[f : f + 1, :] = jnp.where(here, bucket.astype(I32) * CAP + rank, -1)
        s = slot[f : f + 1, :]
        low = (s & 255).astype(F32)
        high = ((s >> 8) + 2 * (f ^ 1)).astype(F32)
        lhs = jnp.concatenate([masks[f] * low, masks[f] * high], axis=0).astype(BF16)
        total = total + dot_nt(lhs, one_hot_rows(CAP, rank))
    ask_ref[...] = total[0:8].astype(I32) + 256 * total[8:16].astype(I32)


def lower_half(shape):
    return lax.broadcasted_iota(I32, shape, 0) < 4


def trace(ref, c, v, f):
    a, s = f // 2, f % 2
    at = v * DOFS
    if a == 0:
        return ref[c, at + 48 * s : at + 48 * s + 16, :]
    if a == 1:
        out = []
        for h in range(2):
            r = at + 32 * h + 8 * s
            x = ref[c, r : r + 8, :]
            y = ref[c, r + 16 : r + 24, :]
            low = lower_half(x.shape)
            if s == 0:
                out.append(jnp.where(low, x, pltpu.roll(y, 4, 0)))
            else:
                out.append(jnp.where(low, pltpu.roll(x, 4, 0), y))
        return jnp.concatenate(out, axis=0)
    return ref[c, pl.ds(at + 3 * s, 16, stride=4), :]


def add_on_face(ref, c, v, f, x):
    a, s = f // 2, f % 2
    at = v * DOFS
    if a == 0:
        ref[c, at + 48 * s : at + 48 * s + 16, :] += x
    elif a == 1:
        for h in range(2):
            y = x[8 * h : 8 * h + 8, :]
            low = lower_half(y.shape)
            keep = low if s == 0 else ~low
            turned = pltpu.roll(y, 4, 0)
            first, second = (y, turned) if s == 0 else (turned, y)
            r = at + 32 * h + 8 * s
            ref[c, r : r + 8, :] += jnp.where(keep, first, 0.0)
            ref[c, r + 16 : r + 24, :] += jnp.where(keep, second, 0.0)
    else:
        spot = (c, pl.ds(at + 3 * s, 16, stride=4), slice(None))
        ref[spot] = ref[spot] + x


def wide(ref, rows):
    return jnp.concatenate([ref[c, 0:rows, :] for c in range(ref.shape[0])], axis=1)


def pressure_of(w, u):
    return (HEAT - 1.0) * (w[4] - 0.5 * (w[1] * u[0] + w[2] * u[1] + w[3] * u[2]))


def axis_flux(w, u, p, a):
    un = u[a]
    out = [w[1 + a]]
    for c in range(3):
        m = w[1 + c] * un
        out.append(m + p if c == a else m)
    out.append((w[4] + p) * un)
    return out


def side_term(w, f):
    sign = 1.0 if f % 2 else -1.0
    u = [w[1 + c] / w[0] for c in range(3)]
    p = pressure_of(w, u)
    flux = axis_flux(w, u, p, f // 2)
    return [(sign * flux[v]) - SPEED * w[v] for v in range(FIELDS)]


def reply(fields, ask_ref, got_ref, own_ref, swap_ref):
    ask = ask_ref[...]
    code = jnp.concatenate([ask[t : t + 1, :] for t in range(8)], axis=1)
    hot = one_hot_rows(NEW_DEV, code & (NEW_DEV - 1))
    high, low = split(fields)
    both = dot(jnp.concatenate([high, low], axis=0), hot)
    for t in range(8):
        spot = slice(CAP * t, CAP * t + CAP)
        got_ref[t] = both[0:ROWS, spot] + both[ROWS:, spot]
    for t in range(8):
        face = ask[t : t + 1, :] >> 9
        for v in range(FIELDS):
            x = trace(got_ref, t, v, 0)
            for f in range(1, 6):
                x = jnp.where(face == f, trace(got_ref, t, v, f), x)
            if t < 3:
                own_ref[t, 16 * v : 16 * v + 16, :] = x
            else:
                swap_ref[t - 3, 16 * v : 16 * v + 16, :] = x


def first_kernel(me_ref, home_ref, far_ref, sib_ref, ask_ref, start_ref, own_ref, swap_ref, got_ref):
    even = (me_ref[0] & 1) == 0
    for c in range(2):
        spot = slice(128 * c, 128 * c + 128)
        sib = sib_ref[:, spot]
        far = far_ref[:, spot]
        start_ref[c] = home_ref[c] + jnp.where(even, far, sib)
        start_ref[c + 2] = home_ref[c + 2] + jnp.where(even, sib, far)
    reply(wide(start_ref, ROWS), ask_ref, got_ref, own_ref, swap_ref)


def near_kernel(table_ref, fields_ref, near_ref, part_ref, outer_ref, high_ref, low_ref):
    for c in range(BLOCKS):
        spot = slice(128 * c, 128 * c + 128)
        w = [fields_ref[c, DOFS * v : DOFS * v + DOFS, :] for v in range(FIELDS)]
        u = [w[1 + i] / w[0] for i in range(3)]
        p = pressure_of(w, u)
        for a in range(3):
            flux = axis_flux(w, u, p, a)
            for v in range(FIELDS):
                high, low = split(flux[v])
                high_ref[v, DOFS * a : DOFS * a + DOFS, spot] = high
                low_ref[v, DOFS * a : DOFS * a + DOFS, spot] = low
    table = table_ref[...]
    for v in range(FIELDS):
        x = dot(table, high_ref[v])
        x = x[0:DOFS] + x[DOFS:] + dot(table[0:DOFS], low_ref[v])
        for c in range(BLOCKS):
            part_ref[c, DOFS * v : DOFS * v + DOFS, :] = x[:, 128 * c : 128 * c + 128]
    for f in range(6):
        hot = one_hot_rows(NEW_DEV, near_ref[f : f + 1, :])
        across = jnp.concatenate(
            [
                jnp.concatenate([trace(fields_ref, c, v, f ^ 1) for v in range(FIELDS)], axis=0)
                for c in range(BLOCKS)
            ],
            axis=1,
        )
        high, low = split(across)
        both = dot(jnp.concatenate([high, low], axis=0), hot)
        outer_ref[f] = both[0:TRACE_ROWS] + both[TRACE_ROWS:]
    for c in range(BLOCKS):
        for f in range(6):
            minus = side_term([trace(fields_ref, c, v, f) for v in range(FIELDS)], f)
            for v in range(FIELDS):
                add_on_face(part_ref, c, v, f, -3.0 * minus[v])


def ghost_rows(ghosts):
    parts = [split(g) for g in ghosts]
    high = jnp.concatenate([p[0] for p in parts], axis=1)
    low = jnp.concatenate([p[1] for p in parts], axis=1)
    return jnp.concatenate([high, low], axis=0)


def direct_kernel(outer_ref, far_ref, a_ref, b_ref, swap_ref, sum_ref):
    lhs = ghost_rows([swap_ref[0], a_ref[2], a_ref[0], b_ref[1], b_ref[0]])
    for f in range(6):
        both = dot(lhs, one_hot_rows(5 * CAP, far_ref[f : f + 1, :] - 3 * CAP))
        sum_ref[f] = outer_ref[f] + both[0:TRACE_ROWS] + both[TRACE_ROWS:]


def add_outer(part_ref, outer_ref, far_ref, post_ref, sum_ref):
    lhs = ghost_rows([post_ref[1], post_ref[0], post_ref[2]])
    sum_ref[...] = part_ref[...]
    for f in range(6):
        both = dot(lhs, one_hot_rows(3 * CAP, far_ref[f : f + 1, :]))
        for c in range(BLOCKS):
            spot = slice(128 * c, 128 * c + 128)
            outer = outer_ref[f, :, spot] + both[0:TRACE_ROWS, spot] + both[TRACE_ROWS:, spot]
            plus = side_term([outer[16 * v : 16 * v + 16] for v in range(FIELDS)], f)
            for v in range(FIELDS):
                add_on_face(sum_ref, c, v, f, 3.0 * plus[v])


def metric_of(start_ref, c):
    return jnp.where(start_ref[c, ROWS : ROWS + 1, :] > 0.5, 2.0, 1.0)


def second_kernel(start_ref, part_ref, outer_ref, far_ref, ask_ref, post_ref,
                  section_ref, own_ref, out_ref, sum_ref, got_ref):
    add_outer(part_ref, outer_ref, far_ref, post_ref, sum_ref)
    for c in range(BLOCKS):
        section_ref[c] = start_ref[c, 0:ROWS, :] - (DT * metric_of(start_ref, c)) * sum_ref[c]
    reply(wide(section_ref, ROWS), ask_ref, got_ref, own_ref, out_ref)


def last_kernel(start_ref, section_ref, part_ref, outer_ref, far_ref, post_ref,
                state_ref, rate_ref, sum_ref):
    add_outer(part_ref, outer_ref, far_ref, post_ref, sum_ref)
    for c in range(BLOCKS):
        spot = slice(128 * c, 128 * c + 128)
        rate = -metric_of(start_ref, c) * sum_ref[c]
        rate_ref[:, spot] = rate
        state_ref[:, spot] = 0.5 * start_ref[c, 0:ROWS, :] + 0.5 * (section_ref[c] + DT * rate)


VM = pl.BlockSpec(memory_space=pltpu.VMEM)
SM = pl.BlockSpec(memory_space=pltpu.SMEM)
HB = pl.BlockSpec(memory_space=pltpu.HBM)


def call(kernel, outs, args, specs=None, scratch=(), flops=10**6):
    return pl.pallas_call(
        kernel,
        out_shape=[jax.ShapeDtypeStruct(s, d) for s, d in outs],
        in_specs=specs or [VM] * len(args),
        out_specs=[VM] * len(outs),
        scratch_shapes=[pltpu.VMEM(*s) if isinstance(s, tuple) else s for s in scratch],
        compiler_params=pltpu.CompilerParams(vmem_limit_bytes=40 * 2**20),
        cost_estimate=pl.CostEstimate(flops=flops, bytes_accessed=2**20, transcendentals=0),
    )(*args)


def swap_cores(x):
    n = lax.axis_size(AXES)
    return lax.ppermute(x, AXES, [(i, i ^ 1) for i in range(n)])


def swap_chips(x):
    n = lax.axis_size(AXES)
    return lax.ppermute(x, AXES, [(i, (i + (1 if i % 2 else -1)) % n) for i in range(n)])


def outward(x, by):
    n = lax.axis_size(AXES)
    return lax.ppermute(x, AXES, [(i, (i + (by if i % 2 == 0 else -by)) % n) for i in range(n)])


def outward_pair(own, got):
    b = outward(jnp.concatenate([own[2:3], got[3:5]], axis=0), 4)
    a = outward(jnp.concatenate([own[0:2], got[1:3]], axis=0), 2)
    return a, b


def swap_back(a, b):
    return swap_cores(jnp.concatenate([a[1:2], a[3:4], b[2:3]], axis=0))


def body(state_old, level_old, morton_old, neighbours):
    me = lax.axis_index(AXES).astype(I32).reshape(1)
    state = state_old.reshape(ROWS, OLD_CAP)
    level = level_old.reshape(1, OLD_CAP)
    morton = morton_old.reshape(1, OLD_CAP)

    ask, near, far, slots, rows = call(
        prepare_kernel,
        [
            ((8, CAP), I32),
            ((6, NEW_DEV), I32),
            ((6, NEW_DEV), I32),
            ((3, OLD_CAP), I32),
            ((2 * ROWS + 16, OLD_CAP), BF16),
        ],
        (me, neighbours, state, level, morton),
        [SM, HB, HB, HB, HB],
        [
            ((6, NEW_DEV), I32),
            ((ROWS, OLD_CAP), F32),
            ((1, OLD_CAP), I32),
            ((1, OLD_CAP), I32),
            pltpu.SemaphoreType.DMA((4,)),
        ],
    )
    ask = ask.reshape(8, 1, CAP)
    got = swap_cores(ask[3:8])
    to_far, to_sib = call(pack_kernel, [((MOVED_ROWS, HALF), F32)] * 2, (rows, slots))
    got, to_far = lax.optimization_barrier((got, to_far))
    a, b = outward_pair(ask[0:3], got)
    from_far = swap_chips(to_far)
    from_sib = swap_cores(to_sib)
    (home,) = call(home_kernel, [((BLOCKS, MOVED_ROWS, 128), F32)], (rows, slots))
    post = swap_back(a, b)
    asked = jnp.concatenate(
        [post[1], post[0], post[2], got[0], a[2], a[0], b[1], b[0]], axis=0
    )

    chunks = [((3, TRACE_ROWS, CAP), F32), ((5, TRACE_ROWS, CAP), F32)]
    got_scratch = ((8, ROWS, CAP), F32)
    blocks = ((BLOCKS, ROWS, 128), F32)
    sides = ((6, TRACE_ROWS, NEW_DEV), F32)
    table = jnp.asarray(stacked_table())

    def neighbours_of(fields, own, swap):
        got = swap_cores(swap)
        a, b = outward_pair(own, got)
        part, outer = call(
            near_kernel,
            [blocks, sides],
            (table, fields, near),
            None,
            [((FIELDS, 3 * DOFS, NEW_DEV), BF16)] * 2,
            flops=10**9,
        )
        a, b, outer = lax.optimization_barrier((a, b, outer))
        post = swap_back(a, b)
        (outer,) = call(direct_kernel, [sides], (outer, far, a, b, got), flops=10**9)
        return part, outer, far, post

    start, own, swap = call(
        first_kernel,
        [((BLOCKS, MOVED_ROWS, 128), F32)] + chunks,
        (me, home, from_far, from_sib, asked),
        [SM, VM, VM, VM, VM],
        [got_scratch],
    )
    part, outer, far, post = neighbours_of(start, own, swap)
    section, own, swap = call(
        second_kernel,
        [blocks] + chunks,
        (start, part, outer, far, asked, post),
        None,
        [blocks, got_scratch],
    )
    part, outer, far, post = neighbours_of(section, own, swap)
    new_state, rate = call(
        last_kernel,
        [((ROWS, NEW_DEV), F32)] * 2,
        (start, section, part, outer, far, post),
        None,
        [blocks],
    )
    shape = (FIELDS, DOFS, NEW_DEV)
    return new_state.reshape(shape), rate.reshape(shape)


def solution(mesh):
    wide = P(None, None, AXES)
    return jax.shard_map(
        body,
        mesh=mesh,
        in_specs=(wide, P(AXES), P(AXES), P(None, AXES)),
        out_specs=(wide, wide),
        check_vma=False,
    )
```

```python
import jax
import jax.numpy as jnp
import numpy as np
from jax import lax
from jax.experimental import pallas as pl
from jax.experimental.pallas import tpu as pltpu
from jax.sharding import PartitionSpec as P

FIELDS = 5
DOFS = 64
ROWS = FIELDS * DOFS
NEW_DEV = 512
HALF = NEW_DEV // 2
OLD_CAP = 1024
CAP = 128
TRACE_ROWS = FIELDS * 16
MOVED_ROWS = ROWS + 8
BLOCKS = NEW_DEV // 128

HEAT = 1.4
SPEED = 4.0
DT = 0.0002
AXES = ("px", "py")
F32 = jnp.float32
BF16 = jnp.bfloat16
I32 = jnp.int32

STEPS = (2, 3, 4, 1, -1, -2, -3, -4)

OPEN_VMEM = 54


def derivative_table():
    points = np.array([-1.0, -1.0 / np.sqrt(5.0), 1.0 / np.sqrt(5.0), 1.0])
    weights = np.array(
        [1.0 / np.prod([points[c] - points[o] for o in range(4) if o != c]) for c in range(4)]
    )
    table = np.zeros((4, 4))
    for r in range(4):
        for c in range(4):
            if r != c:
                table[r, c] = weights[c] / weights[r] / (points[r] - points[c])
        table[r, r] = -np.sum(table[r])
    return table


def stacked_table():
    d = derivative_table().astype(np.float32).astype(np.float64)
    one = np.eye(4)
    full = np.concatenate(
        [
            np.kron(np.kron(d, one), one),
            np.kron(np.kron(one, d), one),
            np.kron(np.kron(one, one), d),
        ],
        axis=1,
    ).astype(np.float32)
    high = full.astype(jnp.bfloat16)
    low = (full - high.astype(np.float32)).astype(jnp.bfloat16)
    return np.concatenate([high, low], axis=0)


def split(x):
    high = x.astype(BF16)
    low = (x - high.astype(F32)).astype(BF16)
    return high, low


def dot(a, b):
    return lax.dot_general(a, b, (((1,), (0,)), ((), ())), preferred_element_type=F32)


def dot_nt(a, b):
    return lax.dot_general(a, b, (((1,), (1,)), ((), ())), preferred_element_type=F32)


def one_hot_rows(size, row):
    spots = lax.broadcasted_iota(I32, (size, row.shape[1]), 0)
    return jnp.where(spots == row, 1.0, 0.0).astype(BF16)


def relay_slots(me, morton):
    occupied = morton >= 0
    owner = morton >> 9
    slot = morton & (NEW_DEV - 1)
    gap = (owner - me) & 127
    even = (me & 1) == 0
    to_next = occupied & (gap == 1)
    to_prior = occupied & (gap == 127)
    home = jnp.where(occupied & (gap == 0), slot, -1)
    ahead = jnp.where(to_next, slot, -1)
    behind = jnp.where(to_prior, slot - HALF, -1)
    sib = jnp.where(even, ahead, behind)
    far = jnp.where(even, behind, ahead)
    return sib, far, home


def store_moved(ref, got):
    ref[0:ROWS, :] = got[0:ROWS] + got[ROWS : 2 * ROWS]
    ref[ROWS : ROWS + 8, :] = got[2 * ROWS : 2 * ROWS + 8]


def relay_rows(state, level):
    high, low = split(state)
    lev = jnp.broadcast_to(level.astype(F32), (16, OLD_CAP)).astype(BF16)
    return jnp.concatenate([high, low, lev], axis=0)


def open_kernel(me_ref, links_hbm, state_hbm, level_hbm, morton_hbm, ask_ref, near_ref, far_ref,
                to_far_ref, to_sib_ref, links_ref, state_ref, level_ref, morton_ref, sems):
    pairs = ((links_hbm, links_ref), (morton_hbm, morton_ref), (level_hbm, level_ref), (state_hbm, state_ref))
    copies = [pltpu.make_async_copy(src, dst, sems.at[i]) for i, (src, dst) in enumerate(pairs)]
    for copy in copies:
        copy.start()
    copies[0].wait()
    requests(me_ref[0], links_ref[...], ask_ref, near_ref, far_ref)
    copies[1].wait()
    sib, far, _ = relay_slots(me_ref[0], morton_ref[...])
    copies[2].wait()
    copies[3].wait()
    lhs = relay_rows(state_ref[...], level_ref[...])
    store_moved(to_far_ref, dot_nt(lhs, one_hot_rows(HALF, far)))
    store_moved(to_sib_ref, dot_nt(lhs, one_hot_rows(HALF, sib)))


def home_kernel(me_ref, state_ref, level_ref, morton_ref, home_ref):
    _, _, home = relay_slots(me_ref[0], morton_ref[...])
    got = dot_nt(relay_rows(state_ref[...], level_ref[...]), one_hot_rows(NEW_DEV, home))
    for c in range(BLOCKS):
        store_moved(home_ref.at[c], got[:, 128 * c : 128 * c + 128])


def requests(me, links, ask_ref, near_ref, far_ref):
    owner = links >> 9
    slot = links & (NEW_DEV - 1)
    gap = ((owner - me + 192) & 127) - 64
    gap = jnp.where((me & 1) == 0, gap, -gap)
    near_ref[...] = jnp.where(gap == 0, slot, -1)
    b = lax.broadcasted_iota(I32, (8, NEW_DEV), 0)
    step_of = jnp.where(b < 3, b + 2, jnp.where(b == 3, 1, 3 - b))
    masks = [jnp.where(gap[f : f + 1, :] == step_of, 1.0, 0.0) for f in range(6)]
    k = lax.broadcasted_iota(I32, (NEW_DEV, NEW_DEV), 0)
    j = lax.broadcasted_iota(I32, (NEW_DEV, NEW_DEV), 1)
    upper = jnp.where(k <= j, 1.0, 0.0).astype(BF16)
    counts = dot(jnp.concatenate(masks, axis=0).astype(BF16), upper)
    offset = jnp.full((8, 1), -1.0, F32)
    bf = b.astype(F32)
    total = jnp.zeros((16, CAP), F32)
    for f in range(6):
        run = counts[8 * f : 8 * f + 8, :]
        here = gap[f : f + 1, :] != 0
        rank = jnp.sum(masks[f] * (run + offset), axis=0, keepdims=True)
        bucket = jnp.sum(masks[f] * bf, axis=0, keepdims=True)
        offset = offset + run[:, NEW_DEV - 1 : NEW_DEV]
        rank = jnp.where(here, rank.astype(I32), -1)
        far_ref[f : f + 1, :] = jnp.where(here, bucket.astype(I32) * CAP + rank, -1)
        s = slot[f : f + 1, :]
        low = (s & 255).astype(F32)
        high = ((s >> 8) + 2 * (f ^ 1)).astype(F32)
        lhs = jnp.concatenate([masks[f] * low, masks[f] * high], axis=0).astype(BF16)
        total = total + dot_nt(lhs, one_hot_rows(CAP, rank))
    ask_ref[...] = total[0:8].astype(I32) + 256 * total[8:16].astype(I32)


def lower_half(shape):
    return lax.broadcasted_iota(I32, shape, 0) < 4


def trace(ref, c, v, f):
    a, s = f // 2, f % 2
    at = v * DOFS
    if a == 0:
        return ref[c, at + 48 * s : at + 48 * s + 16, :]
    if a == 1:
        out = []
        for h in range(2):
            r = at + 32 * h + 8 * s
            x = ref[c, r : r + 8, :]
            y = ref[c, r + 16 : r + 24, :]
            low = lower_half(x.shape)
            if s == 0:
                out.append(jnp.where(low, x, pltpu.roll(y, 4, 0)))
            else:
                out.append(jnp.where(low, pltpu.roll(x, 4, 0), y))
        return jnp.concatenate(out, axis=0)
    return ref[c, pl.ds(at + 3 * s, 16, stride=4), :]


def add_on_face(ref, c, v, f, x):
    a, s = f // 2, f % 2
    at = v * DOFS
    if a == 0:
        ref[c, at + 48 * s : at + 48 * s + 16, :] += x
    elif a == 1:
        for h in range(2):
            y = x[8 * h : 8 * h + 8, :]
            low = lower_half(y.shape)
            keep = low if s == 0 else ~low
            turned = pltpu.roll(y, 4, 0)
            first, second = (y, turned) if s == 0 else (turned, y)
            r = at + 32 * h + 8 * s
            ref[c, r : r + 8, :] += jnp.where(keep, first, 0.0)
            ref[c, r + 16 : r + 24, :] += jnp.where(keep, second, 0.0)
    else:
        spot = (c, pl.ds(at + 3 * s, 16, stride=4), slice(None))
        ref[spot] = ref[spot] + x


def wide(ref, rows):
    return jnp.concatenate([ref[c, 0:rows, :] for c in range(ref.shape[0])], axis=1)


def pressure_of(w, u):
    return (HEAT - 1.0) * (w[4] - 0.5 * (w[1] * u[0] + w[2] * u[1] + w[3] * u[2]))


def axis_flux(w, u, p, a):
    un = u[a]
    out = [w[1 + a]]
    for c in range(3):
        m = w[1 + c] * un
        out.append(m + p if c == a else m)
    out.append((w[4] + p) * un)
    return out


def side_term(w, f):
    sign = 1.0 if f % 2 else -1.0
    u = [w[1 + c] / w[0] for c in range(3)]
    p = pressure_of(w, u)
    flux = axis_flux(w, u, p, f // 2)
    return [(sign * flux[v]) - SPEED * w[v] for v in range(FIELDS)]


def reply(fields, ask_ref, got_ref, own_ref, swap_ref):
    ask = ask_ref[...]
    code = jnp.concatenate([ask[t : t + 1, :] for t in range(8)], axis=1)
    hot = one_hot_rows(NEW_DEV, code & (NEW_DEV - 1))
    high, low = split(fields)
    both = dot(jnp.concatenate([high, low], axis=0), hot)
    for t in range(8):
        spot = slice(CAP * t, CAP * t + CAP)
        got_ref[t] = both[0:ROWS, spot] + both[ROWS:, spot]
    for t in range(8):
        face = ask[t : t + 1, :] >> 9
        for v in range(FIELDS):
            x = trace(got_ref, t, v, 0)
            for f in range(1, 6):
                x = jnp.where(face == f, trace(got_ref, t, v, f), x)
            if t < 3:
                own_ref[t, 16 * v : 16 * v + 16, :] = x
            else:
                swap_ref[t - 3, 16 * v : 16 * v + 16, :] = x


def first_kernel(me_ref, home_ref, far_ref, sib_ref, ask_ref, start_ref, own_ref, swap_ref, got_ref):
    even = (me_ref[0] & 1) == 0
    for c in range(2):
        spot = slice(128 * c, 128 * c + 128)
        sib = sib_ref[:, spot]
        far = far_ref[:, spot]
        start_ref[c] = home_ref[c] + jnp.where(even, far, sib)
        start_ref[c + 2] = home_ref[c + 2] + jnp.where(even, sib, far)
    reply(wide(start_ref, ROWS), ask_ref, got_ref, own_ref, swap_ref)


def near_kernel(table_ref, fields_ref, near_ref, part_ref, outer_ref, high_ref, low_ref):
    for c in range(BLOCKS):
        spot = slice(128 * c, 128 * c + 128)
        w = [fields_ref[c, DOFS * v : DOFS * v + DOFS, :] for v in range(FIELDS)]
        u = [w[1 + i] / w[0] for i in range(3)]
        p = pressure_of(w, u)
        for a in range(3):
            flux = axis_flux(w, u, p, a)
            for v in range(FIELDS):
                high, low = split(flux[v])
                high_ref[v, DOFS * a : DOFS * a + DOFS, spot] = high
                low_ref[v, DOFS * a : DOFS * a + DOFS, spot] = low
    table = table_ref[...]
    for v in range(FIELDS):
        x = dot(table, high_ref[v])
        x = x[0:DOFS] + x[DOFS:] + dot(table[0:DOFS], low_ref[v])
        for c in range(BLOCKS):
            part_ref[c, DOFS * v : DOFS * v + DOFS, :] = x[:, 128 * c : 128 * c + 128]
    for f in range(6):
        hot = one_hot_rows(NEW_DEV, near_ref[f : f + 1, :])
        across = jnp.concatenate(
            [
                jnp.concatenate([trace(fields_ref, c, v, f ^ 1) for v in range(FIELDS)], axis=0)
                for c in range(BLOCKS)
            ],
            axis=1,
        )
        high, low = split(across)
        both = dot(jnp.concatenate([high, low], axis=0), hot)
        outer_ref[f] = both[0:TRACE_ROWS] + both[TRACE_ROWS:]
    for c in range(BLOCKS):
        for f in range(6):
            minus = side_term([trace(fields_ref, c, v, f) for v in range(FIELDS)], f)
            for v in range(FIELDS):
                add_on_face(part_ref, c, v, f, -3.0 * minus[v])


def ghost_rows(ghosts):
    parts = [split(g) for g in ghosts]
    high = jnp.concatenate([p[0] for p in parts], axis=1)
    low = jnp.concatenate([p[1] for p in parts], axis=1)
    return jnp.concatenate([high, low], axis=0)


def direct_kernel(outer_ref, far_ref, a_ref, b_ref, swap_ref, sum_ref):
    lhs = ghost_rows([swap_ref[0], a_ref[2], a_ref[0], b_ref[1], b_ref[0]])
    for f in range(6):
        both = dot(lhs, one_hot_rows(5 * CAP, far_ref[f : f + 1, :] - 3 * CAP))
        sum_ref[f] = outer_ref[f] + both[0:TRACE_ROWS] + both[TRACE_ROWS:]


def add_outer(part_ref, outer_ref, far_ref, post_ref, sum_ref):
    lhs = ghost_rows([post_ref[1], post_ref[0], post_ref[2]])
    sum_ref[...] = part_ref[...]
    for f in range(6):
        both = dot(lhs, one_hot_rows(3 * CAP, far_ref[f : f + 1, :]))
        for c in range(BLOCKS):
            spot = slice(128 * c, 128 * c + 128)
            outer = outer_ref[f, :, spot] + both[0:TRACE_ROWS, spot] + both[TRACE_ROWS:, spot]
            plus = side_term([outer[16 * v : 16 * v + 16] for v in range(FIELDS)], f)
            for v in range(FIELDS):
                add_on_face(sum_ref, c, v, f, 3.0 * plus[v])


def metric_of(start_ref, c):
    return jnp.where(start_ref[c, ROWS : ROWS + 1, :] > 0.5, 2.0, 1.0)


def second_kernel(start_ref, part_ref, outer_ref, far_ref, ask_ref, post_ref,
                  section_ref, own_ref, out_ref, sum_ref, got_ref):
    add_outer(part_ref, outer_ref, far_ref, post_ref, sum_ref)
    for c in range(BLOCKS):
        section_ref[c] = start_ref[c, 0:ROWS, :] - (DT * metric_of(start_ref, c)) * sum_ref[c]
    reply(wide(section_ref, ROWS), ask_ref, got_ref, own_ref, out_ref)


def last_kernel(start_ref, section_ref, part_ref, outer_ref, far_ref, post_ref,
                state_ref, rate_ref, sum_ref):
    add_outer(part_ref, outer_ref, far_ref, post_ref, sum_ref)
    for c in range(BLOCKS):
        spot = slice(128 * c, 128 * c + 128)
        rate = -metric_of(start_ref, c) * sum_ref[c]
        rate_ref[:, spot] = rate
        state_ref[:, spot] = 0.5 * start_ref[c, 0:ROWS, :] + 0.5 * (section_ref[c] + DT * rate)


VM = pl.BlockSpec(memory_space=pltpu.VMEM)
SM = pl.BlockSpec(memory_space=pltpu.SMEM)
HB = pl.BlockSpec(memory_space=pltpu.HBM)


def call(kernel, outs, args, specs=None, scratch=(), flops=10**6, vmem=40):
    return pl.pallas_call(
        kernel,
        out_shape=[jax.ShapeDtypeStruct(s, d) for s, d in outs],
        in_specs=specs or [VM] * len(args),
        out_specs=[VM] * len(outs),
        scratch_shapes=[pltpu.VMEM(*s) if isinstance(s, tuple) else s for s in scratch],
        compiler_params=pltpu.CompilerParams(vmem_limit_bytes=vmem * 2**20),
        cost_estimate=pl.CostEstimate(flops=flops, bytes_accessed=2**20, transcendentals=0),
    )(*args)


def swap_cores(x):
    n = lax.axis_size(AXES)
    return lax.ppermute(x, AXES, [(i, i ^ 1) for i in range(n)])


def swap_chips(x):
    n = lax.axis_size(AXES)
    return lax.ppermute(x, AXES, [(i, (i + (1 if i % 2 else -1)) % n) for i in range(n)])


def outward(x, by):
    n = lax.axis_size(AXES)
    return lax.ppermute(x, AXES, [(i, (i + (by if i % 2 == 0 else -by)) % n) for i in range(n)])


def outward_pair(own, got):
    b = outward(jnp.concatenate([own[2:3], got[3:5]], axis=0), 4)
    a = outward(jnp.concatenate([own[0:2], got[1:3]], axis=0), 2)
    return a, b


def swap_back(a, b):
    return swap_cores(jnp.concatenate([a[1:2], a[3:4], b[2:3]], axis=0))


def body(state_old, level_old, morton_old, neighbours):
    me = lax.axis_index(AXES).astype(I32).reshape(1)
    state = state_old.reshape(ROWS, OLD_CAP)
    level = level_old.reshape(1, OLD_CAP)
    morton = morton_old.reshape(1, OLD_CAP)

    ask, near, far, to_far, to_sib = call(
        open_kernel,
        [
            ((8, CAP), I32),
            ((6, NEW_DEV), I32),
            ((6, NEW_DEV), I32),
            ((MOVED_ROWS, HALF), F32),
            ((MOVED_ROWS, HALF), F32),
        ],
        (me, neighbours, state, level, morton),
        [SM, HB, HB, HB, HB],
        [
            ((6, NEW_DEV), I32),
            ((ROWS, OLD_CAP), F32),
            ((1, OLD_CAP), I32),
            ((1, OLD_CAP), I32),
            pltpu.SemaphoreType.DMA((4,)),
        ],
        vmem=OPEN_VMEM,
    )
    from_far = swap_chips(to_far)
    from_sib = swap_cores(to_sib)
    ask = ask.reshape(8, 1, CAP)
    got = swap_cores(ask[3:8])
    (home,) = call(
        home_kernel,
        [((BLOCKS, MOVED_ROWS, 128), F32)],
        (me, state, level, morton),
        [SM, VM, VM, VM],
    )
    a, b = outward_pair(ask[0:3], got)
    post = swap_back(a, b)
    asked = jnp.concatenate(
        [post[1], post[0], post[2], got[0], a[2], a[0], b[1], b[0]], axis=0
    )

    chunks = [((3, TRACE_ROWS, CAP), F32), ((5, TRACE_ROWS, CAP), F32)]
    got_scratch = ((8, ROWS, CAP), F32)
    blocks = ((BLOCKS, ROWS, 128), F32)
    sides = ((6, TRACE_ROWS, NEW_DEV), F32)
    table = jnp.asarray(stacked_table())

    def neighbours_of(fields, own, swap):
        got = swap_cores(swap)
        a, b = outward_pair(own, got)
        part, outer = call(
            near_kernel,
            [blocks, sides],
            (table, fields, near),
            None,
            [((FIELDS, 3 * DOFS, NEW_DEV), BF16)] * 2,
            flops=10**9,
        )
        a, b, outer = lax.optimization_barrier((a, b, outer))
        post = swap_back(a, b)
        (outer,) = call(direct_kernel, [sides], (outer, far, a, b, got), flops=10**9)
        return part, outer, far, post

    start, own, swap = call(
        first_kernel,
        [((BLOCKS, MOVED_ROWS, 128), F32)] + chunks,
        (me, home, from_far, from_sib, asked),
        [SM, VM, VM, VM, VM],
        [got_scratch],
    )
    part, outer, far, post = neighbours_of(start, own, swap)
    section, own, swap = call(
        second_kernel,
        [blocks] + chunks,
        (start, part, outer, far, asked, post),
        None,
        [blocks, got_scratch],
    )
    part, outer, far, post = neighbours_of(section, own, swap)
    new_state, rate = call(
        last_kernel,
        [((ROWS, NEW_DEV), F32)] * 2,
        (start, section, part, outer, far, post),
        None,
        [blocks],
    )
    shape = (FIELDS, DOFS, NEW_DEV)
    return new_state.reshape(shape), rate.reshape(shape)


def solution(mesh):
    wide = P(None, None, AXES)
    return jax.shard_map(
        body,
        mesh=mesh,
        in_specs=(wide, P(AXES), P(AXES), P(None, AXES)),
        out_specs=(wide, wide),
        check_vma=False,
    )
```

```python
import jax
import jax.numpy as jnp
import numpy as np
from jax import lax
from jax.experimental import pallas as pl
from jax.experimental.pallas import tpu as pltpu
from jax.sharding import PartitionSpec as P

FIELDS = 5
DOFS = 64
ROWS = FIELDS * DOFS
NEW_DEV = 512
HALF = NEW_DEV // 2
OLD_CAP = 1024
CAP = 128
TRACE_ROWS = FIELDS * 16
MOVED_ROWS = ROWS + 8
BLOCKS = NEW_DEV // 128

HEAT = 1.4
SPEED = 4.0
DT = 0.0002
AXES = ("px", "py")
F32 = jnp.float32
BF16 = jnp.bfloat16
I32 = jnp.int32

STEPS = (2, 3, 4, 1, -1, -2, -3, -4)


def derivative_table():
    points = np.array([-1.0, -1.0 / np.sqrt(5.0), 1.0 / np.sqrt(5.0), 1.0])
    weights = np.array(
        [1.0 / np.prod([points[c] - points[o] for o in range(4) if o != c]) for c in range(4)]
    )
    table = np.zeros((4, 4))
    for r in range(4):
        for c in range(4):
            if r != c:
                table[r, c] = weights[c] / weights[r] / (points[r] - points[c])
        table[r, r] = -np.sum(table[r])
    return table


def stacked_table():
    d = derivative_table().astype(np.float32).astype(np.float64)
    one = np.eye(4)
    full = np.concatenate(
        [
            np.kron(np.kron(d, one), one),
            np.kron(np.kron(one, d), one),
            np.kron(np.kron(one, one), d),
        ],
        axis=1,
    ).astype(np.float32)
    high = full.astype(jnp.bfloat16)
    low = (full - high.astype(np.float32)).astype(jnp.bfloat16)
    return np.concatenate([high, low], axis=0)


def split(x):
    high = x.astype(BF16)
    low = (x - high.astype(F32)).astype(BF16)
    return high, low


def dot(a, b):
    return lax.dot_general(a, b, (((1,), (0,)), ((), ())), preferred_element_type=F32)


def dot_nt(a, b):
    return lax.dot_general(a, b, (((1,), (1,)), ((), ())), preferred_element_type=F32)


def one_hot_rows(size, row):
    spots = lax.broadcasted_iota(I32, (size, row.shape[1]), 0)
    return jnp.where(spots == row, 1.0, 0.0).astype(BF16)


def relay_slots(me, morton):
    occupied = morton >= 0
    owner = morton >> 9
    slot = morton & (NEW_DEV - 1)
    gap = (owner - me) & 127
    even = (me & 1) == 0
    to_next = occupied & (gap == 1)
    to_prior = occupied & (gap == 127)
    home = jnp.where(occupied & (gap == 0), slot, -1)
    ahead = jnp.where(to_next, slot, -1)
    behind = jnp.where(to_prior, slot - HALF, -1)
    sib = jnp.where(even, ahead, behind)
    far = jnp.where(even, behind, ahead)
    return sib, far, home


def store_moved(ref, got):
    ref[0:ROWS, :] = got[0:ROWS] + got[ROWS : 2 * ROWS]
    ref[ROWS : ROWS + 8, :] = got[2 * ROWS : 2 * ROWS + 8]


def relay_rows(state, level):
    high, low = split(state)
    lev = jnp.broadcast_to(level.astype(F32), (16, OLD_CAP)).astype(BF16)
    return jnp.concatenate([high, low, lev], axis=0)


def open_kernel(me_ref, links_hbm, state_hbm, level_hbm, morton_hbm, own_ask_ref, swap_ask_ref, near_ref, far_ref,
                state_ref, level_ref, morton_ref, links_ref, sems):
    pairs = ((links_hbm, links_ref), (morton_hbm, morton_ref), (level_hbm, level_ref), (state_hbm, state_ref))
    copies = [pltpu.make_async_copy(src, dst, sems.at[i]) for i, (src, dst) in enumerate(pairs)]
    for copy in copies:
        copy.start()
    copies[0].wait()
    ask = requests(me_ref[0], links_ref[...], near_ref, far_ref)
    for t in range(8):
        if t < 3:
            own_ask_ref[t] = ask[t : t + 1]
        else:
            swap_ask_ref[t - 3] = ask[t : t + 1]
    for copy in copies[1:]:
        copy.wait()


def pack_kernel(me_ref, state_ref, level_ref, morton_ref, far_ref, sib_ref):
    sib, far, _ = relay_slots(me_ref[0], morton_ref[...])
    lhs = relay_rows(state_ref[...], level_ref[...])
    store_moved(far_ref, dot_nt(lhs, one_hot_rows(HALF, far)))
    store_moved(sib_ref, dot_nt(lhs, one_hot_rows(HALF, sib)))


def home_kernel(me_ref, state_ref, level_ref, morton_ref, home_ref):
    _, _, home = relay_slots(me_ref[0], morton_ref[...])
    got = dot_nt(relay_rows(state_ref[...], level_ref[...]), one_hot_rows(NEW_DEV, home))
    for c in range(BLOCKS):
        store_moved(home_ref.at[c], got[:, 128 * c : 128 * c + 128])


def requests(me, links, near_ref, far_ref):
    owner = links >> 9
    slot = links & (NEW_DEV - 1)
    gap = ((owner - me + 192) & 127) - 64
    gap = jnp.where((me & 1) == 0, gap, -gap)
    near_ref[...] = jnp.where(gap == 0, slot, -1)
    b = lax.broadcasted_iota(I32, (8, NEW_DEV), 0)
    step_of = jnp.where(b < 3, b + 2, jnp.where(b == 3, 1, 3 - b))
    masks = [jnp.where(gap[f : f + 1, :] == step_of, 1.0, 0.0) for f in range(6)]
    k = lax.broadcasted_iota(I32, (NEW_DEV, NEW_DEV), 0)
    j = lax.broadcasted_iota(I32, (NEW_DEV, NEW_DEV), 1)
    upper = jnp.where(k <= j, 1.0, 0.0).astype(BF16)
    counts = dot(jnp.concatenate(masks, axis=0).astype(BF16), upper)
    offset = jnp.full((8, 1), -1.0, F32)
    bf = b.astype(F32)
    total = jnp.zeros((16, CAP), F32)
    for f in range(6):
        run = counts[8 * f : 8 * f + 8, :]
        here = gap[f : f + 1, :] != 0
        rank = jnp.sum(masks[f] * (run + offset), axis=0, keepdims=True)
        bucket = jnp.sum(masks[f] * bf, axis=0, keepdims=True)
        offset = offset + run[:, NEW_DEV - 1 : NEW_DEV]
        rank = jnp.where(here, rank.astype(I32), -1)
        far_ref[f : f + 1, :] = jnp.where(here, bucket.astype(I32) * CAP + rank, -1)
        s = slot[f : f + 1, :]
        low = (s & 255).astype(F32)
        high = ((s >> 8) + 2 * (f ^ 1)).astype(F32)
        lhs = jnp.concatenate([masks[f] * low, masks[f] * high], axis=0).astype(BF16)
        total = total + dot_nt(lhs, one_hot_rows(CAP, rank))
    return total[0:8].astype(I32) + 256 * total[8:16].astype(I32)


def lower_half(shape):
    return lax.broadcasted_iota(I32, shape, 0) < 4


def trace(ref, c, v, f):
    a, s = f // 2, f % 2
    at = v * DOFS
    if a == 0:
        return ref[c, at + 48 * s : at + 48 * s + 16, :]
    if a == 1:
        out = []
        for h in range(2):
            r = at + 32 * h + 8 * s
            x = ref[c, r : r + 8, :]
            y = ref[c, r + 16 : r + 24, :]
            low = lower_half(x.shape)
            if s == 0:
                out.append(jnp.where(low, x, pltpu.roll(y, 4, 0)))
            else:
                out.append(jnp.where(low, pltpu.roll(x, 4, 0), y))
        return jnp.concatenate(out, axis=0)
    return ref[c, pl.ds(at + 3 * s, 16, stride=4), :]


def add_on_face(ref, c, v, f, x):
    a, s = f // 2, f % 2
    at = v * DOFS
    if a == 0:
        ref[c, at + 48 * s : at + 48 * s + 16, :] += x
    elif a == 1:
        for h in range(2):
            y = x[8 * h : 8 * h + 8, :]
            low = lower_half(y.shape)
            keep = low if s == 0 else ~low
            turned = pltpu.roll(y, 4, 0)
            first, second = (y, turned) if s == 0 else (turned, y)
            r = at + 32 * h + 8 * s
            ref[c, r : r + 8, :] += jnp.where(keep, first, 0.0)
            ref[c, r + 16 : r + 24, :] += jnp.where(keep, second, 0.0)
    else:
        spot = (c, pl.ds(at + 3 * s, 16, stride=4), slice(None))
        ref[spot] = ref[spot] + x


def wide(ref, rows):
    return jnp.concatenate([ref[c, 0:rows, :] for c in range(ref.shape[0])], axis=1)


def pressure_of(w, u):
    return (HEAT - 1.0) * (w[4] - 0.5 * (w[1] * u[0] + w[2] * u[1] + w[3] * u[2]))


def axis_flux(w, u, p, a):
    un = u[a]
    out = [w[1 + a]]
    for c in range(3):
        m = w[1 + c] * un
        out.append(m + p if c == a else m)
    out.append((w[4] + p) * un)
    return out


def side_term(w, f):
    sign = 1.0 if f % 2 else -1.0
    u = [w[1 + c] / w[0] for c in range(3)]
    p = pressure_of(w, u)
    flux = axis_flux(w, u, p, f // 2)
    return [(sign * flux[v]) - SPEED * w[v] for v in range(FIELDS)]


def reply(fields, ask, got_ref, out_ref):
    chunks = ask.shape[0]
    code = jnp.concatenate([ask[t : t + 1, :] for t in range(chunks)], axis=1)
    hot = one_hot_rows(NEW_DEV, code & (NEW_DEV - 1))
    high, low = split(fields)
    both = dot(jnp.concatenate([high, low], axis=0), hot)
    for t in range(chunks):
        spot = slice(CAP * t, CAP * t + CAP)
        got_ref[t] = both[0:ROWS, spot] + both[ROWS:, spot]
    for t in range(chunks):
        face = ask[t : t + 1, :] >> 9
        for v in range(FIELDS):
            x = trace(got_ref, t, v, 0)
            for f in range(1, 6):
                x = jnp.where(face == f, trace(got_ref, t, v, f), x)
            out_ref[t, 16 * v : 16 * v + 16, :] = x


def own_kernel(fields_ref, ask_ref, own_ref, got_ref):
    reply(wide(fields_ref, ROWS), ask_ref[0:3, :], got_ref, own_ref)


def first_kernel(me_ref, home_ref, far_ref, sib_ref, ask_ref, start_ref, swap_ref, got_ref):
    even = (me_ref[0] & 1) == 0
    for c in range(2):
        spot = slice(128 * c, 128 * c + 128)
        sib = sib_ref[:, spot]
        far = far_ref[:, spot]
        start_ref[c] = home_ref[c] + jnp.where(even, far, sib)
        start_ref[c + 2] = home_ref[c + 2] + jnp.where(even, sib, far)
    reply(wide(start_ref, ROWS), ask_ref[3:8, :], got_ref, swap_ref)


def near_kernel(table_ref, fields_ref, near_ref, part_ref, outer_ref, high_ref, low_ref):
    for c in range(BLOCKS):
        spot = slice(128 * c, 128 * c + 128)
        w = [fields_ref[c, DOFS * v : DOFS * v + DOFS, :] for v in range(FIELDS)]
        u = [w[1 + i] / w[0] for i in range(3)]
        p = pressure_of(w, u)
        for a in range(3):
            flux = axis_flux(w, u, p, a)
            for v in range(FIELDS):
                high, low = split(flux[v])
                high_ref[v, DOFS * a : DOFS * a + DOFS, spot] = high
                low_ref[v, DOFS * a : DOFS * a + DOFS, spot] = low
    table = table_ref[...]
    for v in range(FIELDS):
        x = dot(table, high_ref[v])
        x = x[0:DOFS] + x[DOFS:] + dot(table[0:DOFS], low_ref[v])
        for c in range(BLOCKS):
            part_ref[c, DOFS * v : DOFS * v + DOFS, :] = x[:, 128 * c : 128 * c + 128]
    for f in range(6):
        hot = one_hot_rows(NEW_DEV, near_ref[f : f + 1, :])
        across = jnp.concatenate(
            [
                jnp.concatenate([trace(fields_ref, c, v, f ^ 1) for v in range(FIELDS)], axis=0)
                for c in range(BLOCKS)
            ],
            axis=1,
        )
        high, low = split(across)
        both = dot(jnp.concatenate([high, low], axis=0), hot)
        outer_ref[f] = both[0:TRACE_ROWS] + both[TRACE_ROWS:]
    for c in range(BLOCKS):
        for f in range(6):
            minus = side_term([trace(fields_ref, c, v, f) for v in range(FIELDS)], f)
            for v in range(FIELDS):
                add_on_face(part_ref, c, v, f, -3.0 * minus[v])


def ghost_rows(ghosts):
    parts = [split(g) for g in ghosts]
    high = jnp.concatenate([p[0] for p in parts], axis=1)
    low = jnp.concatenate([p[1] for p in parts], axis=1)
    return jnp.concatenate([high, low], axis=0)


def direct_kernel(outer_ref, far_ref, a_ref, b_ref, swap_ref, sum_ref):
    lhs = ghost_rows([swap_ref[0], a_ref[2], a_ref[0], b_ref[1], b_ref[0]])
    for f in range(6):
        both = dot(lhs, one_hot_rows(5 * CAP, far_ref[f : f + 1, :] - 3 * CAP))
        sum_ref[f] = outer_ref[f] + both[0:TRACE_ROWS] + both[TRACE_ROWS:]


def place_rest(outer_ref, far_ref, post_ref, side_ref):
    lhs = ghost_rows([post_ref[1], post_ref[0], post_ref[2]])
    for f in range(6):
        both = dot(lhs, one_hot_rows(3 * CAP, far_ref[f : f + 1, :]))
        side_ref[f] = outer_ref[f] + both[0:TRACE_ROWS] + both[TRACE_ROWS:]


def add_outer(part_ref, side_ref, sum_ref, c):
    sum_ref[c] = part_ref[c]
    for f in range(6):
        outer = side_ref[f, :, 128 * c : 128 * c + 128]
        plus = side_term([outer[16 * v : 16 * v + 16] for v in range(FIELDS)], f)
        for v in range(FIELDS):
            add_on_face(sum_ref, c, v, f, 3.0 * plus[v])


def metric_of(start_ref, c):
    return jnp.where(start_ref[c, ROWS : ROWS + 1, :] > 0.5, 2.0, 1.0)


def second_kernel(start_ref, part_ref, outer_ref, far_ref, ask_ref, post_ref,
                  section_ref, swap_ref, side_ref, sum_ref, got_ref):
    place_rest(outer_ref, far_ref, post_ref, side_ref)
    for c in range(BLOCKS):
        add_outer(part_ref, side_ref, sum_ref, c)
        section_ref[c] = start_ref[c, 0:ROWS, :] - (DT * metric_of(start_ref, c)) * sum_ref[c]
    reply(wide(section_ref, ROWS), ask_ref[3:8, :], got_ref, swap_ref)


def last_kernel(start_ref, section_ref, part_ref, outer_ref, far_ref, post_ref,
                state_hbm, rate_hbm, side_ref, sum_ref, state_ref, rate_ref, sems):
    place_rest(outer_ref, far_ref, post_ref, side_ref)
    copies = []
    for c in range(BLOCKS):
        add_outer(part_ref, side_ref, sum_ref, c)
        rate = -metric_of(start_ref, c) * sum_ref[c]
        rate_ref[c] = rate
        state_ref[c] = 0.5 * start_ref[c, 0:ROWS, :] + 0.5 * (section_ref[c] + DT * rate)
        for i, (src, dst) in enumerate(((rate_ref, rate_hbm), (state_ref, state_hbm))):
            copy = pltpu.make_async_copy(src.at[c], dst.at[:, pl.ds(128 * c, 128)], sems.at[i, c])
            copy.start()
            copies.append(copy)
    for copy in copies:
        copy.wait()


VM = pl.BlockSpec(memory_space=pltpu.VMEM)
SM = pl.BlockSpec(memory_space=pltpu.SMEM)
HB = pl.BlockSpec(memory_space=pltpu.HBM)


def call(kernel, outs, args, specs=None, scratch=(), flops=10**6, outs_in=None):
    return pl.pallas_call(
        kernel,
        out_shape=[jax.ShapeDtypeStruct(s, d) for s, d in outs],
        in_specs=specs or [VM] * len(args),
        out_specs=[outs_in or VM] * len(outs),
        scratch_shapes=[pltpu.VMEM(*s) if isinstance(s, tuple) else s for s in scratch],
        compiler_params=pltpu.CompilerParams(vmem_limit_bytes=40 * 2**20),
        cost_estimate=pl.CostEstimate(flops=flops, bytes_accessed=2**20, transcendentals=0),
    )(*args)


def swap_cores(x):
    n = lax.axis_size(AXES)
    return lax.ppermute(x, AXES, [(i, i ^ 1) for i in range(n)])


def swap_chips(x):
    n = lax.axis_size(AXES)
    return lax.ppermute(x, AXES, [(i, (i + (1 if i % 2 else -1)) % n) for i in range(n)])


def outward(x, by):
    n = lax.axis_size(AXES)
    return lax.ppermute(x, AXES, [(i, (i + (by if i % 2 == 0 else -by)) % n) for i in range(n)])


def outward_pair(own, got):
    b = outward(jnp.concatenate([own[2:3], got[3:5]], axis=0), 4)
    a = outward(jnp.concatenate([own[0:2], got[1:3]], axis=0), 2)
    return a, b


def swap_back(a, b):
    return swap_cores(jnp.concatenate([a[1:2], a[3:4], b[2:3]], axis=0))


def body(state_old, level_old, morton_old, neighbours):
    me = lax.axis_index(AXES).astype(I32).reshape(1)
    inputs = [
        pltpu.with_memory_space_constraint(x, pltpu.HBM)
        for x in (
            neighbours,
            state_old.reshape(ROWS, OLD_CAP),
            level_old.reshape(1, OLD_CAP),
            morton_old.reshape(1, OLD_CAP),
        )
    ]
    own_ask, swap_ask, near, far, state, level, morton = call(
        open_kernel,
        [
            ((3, 1, CAP), I32),
            ((5, 1, CAP), I32),
            ((6, NEW_DEV), I32),
            ((6, NEW_DEV), I32),
            ((ROWS, OLD_CAP), F32),
            ((1, OLD_CAP), I32),
            ((1, OLD_CAP), I32),
        ],
        (me, *inputs),
        [SM, HB, HB, HB, HB],
        [((6, NEW_DEV), I32), pltpu.SemaphoreType.DMA((4,))],
    )
    got = swap_cores(swap_ask)
    relay = [SM, VM, VM, VM]
    to_far, to_sib = call(pack_kernel, [((MOVED_ROWS, HALF), F32)] * 2, (me, state, level, morton), relay)
    got, to_far, to_sib, morton = lax.optimization_barrier((got, to_far, to_sib, morton))
    a, b = outward_pair(own_ask, got)
    from_far = swap_chips(to_far)
    from_sib = swap_cores(to_sib)
    (home,) = call(home_kernel, [((BLOCKS, MOVED_ROWS, 128), F32)], (me, state, level, morton), relay)
    post = swap_back(a, b)
    asked = jnp.concatenate(
        [post[1], post[0], post[2], got[0], a[2], a[0], b[1], b[0]], axis=0
    )

    swapped = ((5, TRACE_ROWS, CAP), F32)
    got_scratch = ((5, ROWS, CAP), F32)
    blocks = ((BLOCKS, ROWS, 128), F32)
    sides = ((6, TRACE_ROWS, NEW_DEV), F32)
    table = jnp.asarray(stacked_table())

    def neighbours_of(fields, swap):
        got = swap_cores(swap)
        (own,) = call(
            own_kernel,
            [((3, TRACE_ROWS, CAP), F32)],
            (fields, asked),
            None,
            [((3, ROWS, CAP), F32)],
        )
        a, b = outward_pair(own, got)
        part, outer = call(
            near_kernel,
            [blocks, sides],
            (table, fields, near),
            None,
            [((FIELDS, 3 * DOFS, NEW_DEV), BF16)] * 2,
            flops=10**9,
        )
        a, b, outer = lax.optimization_barrier((a, b, outer))
        post = swap_back(a, b)
        (outer,) = call(direct_kernel, [sides], (outer, far, a, b, got), flops=10**9)
        return part, outer, far, post

    start, swap = call(
        first_kernel,
        [((BLOCKS, MOVED_ROWS, 128), F32), swapped],
        (me, home, from_far, from_sib, asked),
        [SM, VM, VM, VM, VM],
        [got_scratch],
    )
    part, outer, far, post = neighbours_of(start, swap)
    section, swap = call(
        second_kernel,
        [blocks, swapped],
        (start, part, outer, far, asked, post),
        None,
        [sides, blocks, got_scratch],
    )
    part, outer, far, post = neighbours_of(section, swap)
    new_state, rate = call(
        last_kernel,
        [((ROWS, NEW_DEV), F32)] * 2,
        (start, section, part, outer, far, post),
        None,
        [sides, blocks, blocks, blocks, pltpu.SemaphoreType.DMA((2, BLOCKS))],
        outs_in=HB,
    )
    shape = (FIELDS, DOFS, NEW_DEV)
    return new_state.reshape(shape), rate.reshape(shape)


def solution(mesh):
    wide = P(None, None, AXES)
    return jax.shard_map(
        body,
        mesh=mesh,
        in_specs=(wide, P(AXES), P(AXES), P(None, AXES)),
        out_specs=(wide, wide),
        check_vma=False,
    )
```

```python
import jax
import jax.numpy as jnp
import numpy as np
from jax import lax
from jax.experimental import pallas as pl
from jax.experimental.pallas import tpu as pltpu
from jax.sharding import PartitionSpec as P

FIELDS = 5
DOFS = 64
ROWS = FIELDS * DOFS
NEW_DEV = 512
HALF = NEW_DEV // 2
OLD_CAP = 1024
CAP = 128
TRACE_ROWS = FIELDS * 16
MOVED_ROWS = ROWS + 8
BLOCKS = NEW_DEV // 128

HEAT = 1.4
SPEED = 4.0
DT = 0.0002
AXES = ("px", "py")
F32 = jnp.float32
BF16 = jnp.bfloat16
I32 = jnp.int32

STEPS = (2, 3, 4, 1, -1, -2, -3, -4)


def derivative_table():
    points = np.array([-1.0, -1.0 / np.sqrt(5.0), 1.0 / np.sqrt(5.0), 1.0])
    weights = np.array(
        [1.0 / np.prod([points[c] - points[o] for o in range(4) if o != c]) for c in range(4)]
    )
    table = np.zeros((4, 4))
    for r in range(4):
        for c in range(4):
            if r != c:
                table[r, c] = weights[c] / weights[r] / (points[r] - points[c])
        table[r, r] = -np.sum(table[r])
    return table


def stacked_table():
    d = derivative_table().astype(np.float32).astype(np.float64)
    one = np.eye(4)
    full = np.concatenate(
        [
            np.kron(np.kron(d, one), one),
            np.kron(np.kron(one, d), one),
            np.kron(np.kron(one, one), d),
        ],
        axis=1,
    ).astype(np.float32)
    high = full.astype(jnp.bfloat16)
    low = (full - high.astype(np.float32)).astype(jnp.bfloat16)
    return np.concatenate([high, low], axis=0)


def split(x):
    high = x.astype(BF16)
    low = (x - high.astype(F32)).astype(BF16)
    return high, low


def dot(a, b):
    return lax.dot_general(a, b, (((1,), (0,)), ((), ())), preferred_element_type=F32)


def dot_nt(a, b):
    return lax.dot_general(a, b, (((1,), (1,)), ((), ())), preferred_element_type=F32)


def one_hot_rows(size, row):
    spots = lax.broadcasted_iota(I32, (size, row.shape[1]), 0)
    return jnp.where(spots == row, 1.0, 0.0).astype(BF16)


def relay_slots(me, morton):
    occupied = morton >= 0
    owner = morton >> 9
    slot = morton & (NEW_DEV - 1)
    gap = (owner - me) & 127
    even = (me & 1) == 0
    to_next = occupied & (gap == 1)
    to_prior = occupied & (gap == 127)
    home = jnp.where(occupied & (gap == 0), slot, -1)
    ahead = jnp.where(to_next, slot, -1)
    behind = jnp.where(to_prior, slot - HALF, -1)
    sib = jnp.where(even, ahead, behind)
    far = jnp.where(even, behind, ahead)
    return sib, far, home


def store_moved(ref, got):
    ref[0:ROWS, :] = got[0:ROWS] + got[ROWS : 2 * ROWS]
    ref[ROWS : ROWS + 8, :] = got[2 * ROWS : 2 * ROWS + 8]


def relay_rows(state, level):
    high, low = split(state)
    lev = jnp.broadcast_to(level.astype(F32), (16, OLD_CAP)).astype(BF16)
    return jnp.concatenate([high, low, lev], axis=0)


def open_kernel(me_ref, links_hbm, state_hbm, level_hbm, morton_hbm, own_ask_ref, swap_ask_ref, near_ref, far_ref,
                state_ref, level_ref, morton_ref, links_ref, sems):
    pairs = ((links_hbm, links_ref), (morton_hbm, morton_ref), (level_hbm, level_ref), (state_hbm, state_ref))
    copies = [pltpu.make_async_copy(src, dst, sems.at[i]) for i, (src, dst) in enumerate(pairs)]
    for copy in copies:
        copy.start()
    copies[0].wait()
    ask = requests(me_ref[0], links_ref[...], near_ref, far_ref)
    for t in range(8):
        if t < 3:
            own_ask_ref[t] = ask[t : t + 1]
        else:
            swap_ask_ref[t - 3] = ask[t : t + 1]
    for copy in copies[1:]:
        copy.wait()


def pack_kernel(me_ref, state_ref, level_ref, morton_ref, far_ref, sib_ref):
    sib, far, _ = relay_slots(me_ref[0], morton_ref[...])
    lhs = relay_rows(state_ref[...], level_ref[...])
    store_moved(far_ref, dot_nt(lhs, one_hot_rows(HALF, far)))
    store_moved(sib_ref, dot_nt(lhs, one_hot_rows(HALF, sib)))


def home_kernel(me_ref, state_ref, level_ref, morton_ref, home_ref):
    _, _, home = relay_slots(me_ref[0], morton_ref[...])
    got = dot_nt(relay_rows(state_ref[...], level_ref[...]), one_hot_rows(NEW_DEV, home))
    for c in range(BLOCKS):
        store_moved(home_ref.at[c], got[:, 128 * c : 128 * c + 128])


def requests(me, links, near_ref, far_ref):
    owner = links >> 9
    slot = links & (NEW_DEV - 1)
    gap = ((owner - me + 192) & 127) - 64
    gap = jnp.where((me & 1) == 0, gap, -gap)
    near_ref[...] = jnp.where(gap == 0, slot, -1)
    b = lax.broadcasted_iota(I32, (8, NEW_DEV), 0)
    step_of = jnp.where(b < 3, b + 2, jnp.where(b == 3, 1, 3 - b))
    masks = [jnp.where(gap[f : f + 1, :] == step_of, 1.0, 0.0) for f in range(6)]
    k = lax.broadcasted_iota(I32, (NEW_DEV, NEW_DEV), 0)
    j = lax.broadcasted_iota(I32, (NEW_DEV, NEW_DEV), 1)
    upper = jnp.where(k <= j, 1.0, 0.0).astype(BF16)
    counts = dot(jnp.concatenate(masks, axis=0).astype(BF16), upper)
    offset = jnp.full((8, 1), -1.0, F32)
    bf = b.astype(F32)
    total = jnp.zeros((16, CAP), F32)
    for f in range(6):
        run = counts[8 * f : 8 * f + 8, :]
        here = gap[f : f + 1, :] != 0
        rank = jnp.sum(masks[f] * (run + offset), axis=0, keepdims=True)
        bucket = jnp.sum(masks[f] * bf, axis=0, keepdims=True)
        offset = offset + run[:, NEW_DEV - 1 : NEW_DEV]
        rank = jnp.where(here, rank.astype(I32), -1)
        far_ref[f : f + 1, :] = jnp.where(here, bucket.astype(I32) * CAP + rank, -1)
        s = slot[f : f + 1, :]
        low = (s & 255).astype(F32)
        high = ((s >> 8) + 2 * (f ^ 1)).astype(F32)
        lhs = jnp.concatenate([masks[f] * low, masks[f] * high], axis=0).astype(BF16)
        total = total + dot_nt(lhs, one_hot_rows(CAP, rank))
    return total[0:8].astype(I32) + 256 * total[8:16].astype(I32)


def lower_half(shape):
    return lax.broadcasted_iota(I32, shape, 0) < 4


def trace(ref, c, v, f):
    a, s = f // 2, f % 2
    at = v * DOFS
    if a == 0:
        return ref[c, at + 48 * s : at + 48 * s + 16, :]
    if a == 1:
        out = []
        for h in range(2):
            r = at + 32 * h + 8 * s
            x = ref[c, r : r + 8, :]
            y = ref[c, r + 16 : r + 24, :]
            low = lower_half(x.shape)
            if s == 0:
                out.append(jnp.where(low, x, pltpu.roll(y, 4, 0)))
            else:
                out.append(jnp.where(low, pltpu.roll(x, 4, 0), y))
        return jnp.concatenate(out, axis=0)
    return ref[c, pl.ds(at + 3 * s, 16, stride=4), :]


def add_on_face(ref, c, v, f, x):
    a, s = f // 2, f % 2
    at = v * DOFS
    if a == 0:
        ref[c, at + 48 * s : at + 48 * s + 16, :] += x
    elif a == 1:
        for h in range(2):
            y = x[8 * h : 8 * h + 8, :]
            low = lower_half(y.shape)
            keep = low if s == 0 else ~low
            turned = pltpu.roll(y, 4, 0)
            first, second = (y, turned) if s == 0 else (turned, y)
            r = at + 32 * h + 8 * s
            ref[c, r : r + 8, :] += jnp.where(keep, first, 0.0)
            ref[c, r + 16 : r + 24, :] += jnp.where(keep, second, 0.0)
    else:
        spot = (c, pl.ds(at + 3 * s, 16, stride=4), slice(None))
        ref[spot] = ref[spot] + x


def wide(ref, rows):
    return jnp.concatenate([ref[c, 0:rows, :] for c in range(ref.shape[0])], axis=1)


def pressure_of(w, u):
    return (HEAT - 1.0) * (w[4] - 0.5 * (w[1] * u[0] + w[2] * u[1] + w[3] * u[2]))


def axis_flux(w, u, p, a):
    un = u[a]
    out = [w[1 + a]]
    for c in range(3):
        m = w[1 + c] * un
        out.append(m + p if c == a else m)
    out.append((w[4] + p) * un)
    return out


def side_term(w, f):
    sign = 1.0 if f % 2 else -1.0
    u = [w[1 + c] / w[0] for c in range(3)]
    p = pressure_of(w, u)
    flux = axis_flux(w, u, p, f // 2)
    return [(sign * flux[v]) - SPEED * w[v] for v in range(FIELDS)]


def asked_code(ask):
    return jnp.concatenate([ask[t : t + 1, :] for t in range(ask.shape[0])], axis=1)


def reply(fields, ask, hot, got_ref, out_ref):
    chunks = ask.shape[0]
    high, low = split(fields)
    both = dot(jnp.concatenate([high, low], axis=0), hot)
    for t in range(chunks):
        spot = slice(CAP * t, CAP * t + CAP)
        got_ref[t] = both[0:ROWS, spot] + both[ROWS:, spot]
    for t in range(chunks):
        face = ask[t : t + 1, :] >> 9
        for v in range(FIELDS):
            x = trace(got_ref, t, v, 0)
            for f in range(1, 6):
                x = jnp.where(face == f, trace(got_ref, t, v, f), x)
            out_ref[t, 16 * v : 16 * v + 16, :] = x


def hot_kernel(far_ref, ask_ref, rest_ref, reply_ref):
    for f in range(6):
        rest_ref[f] = one_hot_rows(3 * CAP, far_ref[f : f + 1, :])
    reply_ref[...] = one_hot_rows(NEW_DEV, asked_code(ask_ref[3:8, :]) & (NEW_DEV - 1))


def own_kernel(fields_ref, ask_ref, own_ref, got_ref):
    ask = ask_ref[0:3, :]
    hot = one_hot_rows(NEW_DEV, asked_code(ask) & (NEW_DEV - 1))
    reply(wide(fields_ref, ROWS), ask, hot, got_ref, own_ref)


def first_kernel(me_ref, home_ref, far_ref, sib_ref, ask_ref, hot_ref, start_ref, swap_ref, got_ref):
    even = (me_ref[0] & 1) == 0
    for c in range(2):
        spot = slice(128 * c, 128 * c + 128)
        sib = sib_ref[:, spot]
        far = far_ref[:, spot]
        start_ref[c] = home_ref[c] + jnp.where(even, far, sib)
        start_ref[c + 2] = home_ref[c + 2] + jnp.where(even, sib, far)
    reply(wide(start_ref, ROWS), ask_ref[3:8, :], hot_ref[...], got_ref, swap_ref)


def near_kernel(table_ref, fields_ref, near_ref, part_ref, high_ref, low_ref):
    for c in range(BLOCKS):
        spot = slice(128 * c, 128 * c + 128)
        w = [fields_ref[c, DOFS * v : DOFS * v + DOFS, :] for v in range(FIELDS)]
        u = [w[1 + i] / w[0] for i in range(3)]
        p = pressure_of(w, u)
        for a in range(3):
            flux = axis_flux(w, u, p, a)
            for v in range(FIELDS):
                high, low = split(flux[v])
                high_ref[v, DOFS * a : DOFS * a + DOFS, spot] = high
                low_ref[v, DOFS * a : DOFS * a + DOFS, spot] = low
    table = table_ref[...]
    for v in range(FIELDS):
        x = dot(table, high_ref[v])
        x = x[0:DOFS] + x[DOFS:] + dot(table[0:DOFS], low_ref[v])
        for c in range(BLOCKS):
            part_ref[c, DOFS * v : DOFS * v + DOFS, :] = x[:, 128 * c : 128 * c + 128]
    for f in range(6):
        hot = one_hot_rows(NEW_DEV, near_ref[f : f + 1, :])
        across = jnp.concatenate(
            [
                jnp.concatenate([trace(fields_ref, c, v, f ^ 1) for v in range(FIELDS)], axis=0)
                for c in range(BLOCKS)
            ],
            axis=1,
        )
        high, low = split(across)
        both = dot(jnp.concatenate([high, low], axis=0), hot)
        for c in range(BLOCKS):
            spot = slice(128 * c, 128 * c + 128)
            outer = both[0:TRACE_ROWS, spot] + both[TRACE_ROWS:, spot]
            there = near_ref[f : f + 1, spot] >= 0
            w = [outer[16 * v : 16 * v + 16] for v in range(FIELDS)]
            w[0] = jnp.where(there, w[0], 1.0)
            plus = side_term(w, f)
            minus = side_term([trace(fields_ref, c, v, f) for v in range(FIELDS)], f)
            for v in range(FIELDS):
                add_on_face(part_ref, c, v, f, 3.0 * (jnp.where(there, plus[v], 0.0) - minus[v]))


def ghost_terms(ghost, ask):
    face = (ask >> 9) ^ 1
    axis = face >> 1
    sign = jnp.where((face & 1) == 1, 3.0, -3.0)
    w = [ghost[16 * v : 16 * v + 16] for v in range(FIELDS)]
    u = [w[1 + c] / w[0] for c in range(3)]
    p = pressure_of(w, u)

    def along(x):
        return jnp.where(axis == 0, x[0], jnp.where(axis == 1, x[1], x[2]))

    un = along(u)
    flux = [along(w[1:4])]
    for c in range(3):
        flux.append(w[1 + c] * un + jnp.where(axis == c, p, 0.0))
    flux.append((w[4] + p) * un)
    return jnp.concatenate([sign * flux[v] - (3.0 * SPEED) * w[v] for v in range(FIELDS)], axis=0)


def ghost_rows(ghosts, ask_ref):
    parts = [split(ghost_terms(g, ask_ref[t])) for t, g in enumerate(ghosts)]
    high = jnp.concatenate([p[0] for p in parts], axis=1)
    low = jnp.concatenate([p[1] for p in parts], axis=1)
    return jnp.concatenate([high, low], axis=0)


def add_ghosts(sum_ref, lhs, hot_of):
    for f in range(6):
        both = dot(lhs, hot_of(f))
        for c in range(BLOCKS):
            spot = slice(128 * c, 128 * c + 128)
            term = both[0:TRACE_ROWS, spot] + both[TRACE_ROWS:, spot]
            for v in range(FIELDS):
                add_on_face(sum_ref, c, v, f, term[16 * v : 16 * v + 16])


def direct_kernel(part_ref, far_ref, ask_ref, a_ref, b_ref, swap_ref, sum_ref):
    lhs = ghost_rows([swap_ref[0], a_ref[2], a_ref[0], b_ref[1], b_ref[0]], ask_ref)
    sum_ref[...] = part_ref[...]
    add_ghosts(sum_ref, lhs, lambda f: one_hot_rows(5 * CAP, far_ref[f : f + 1, :] - 3 * CAP))


def add_rest(part_ref, rest_ref, ask_ref, post_ref, sum_ref):
    lhs = ghost_rows([post_ref[1], post_ref[0], post_ref[2]], ask_ref)
    sum_ref[...] = part_ref[...]
    add_ghosts(sum_ref, lhs, lambda f: rest_ref[f])


def metric_of(start_ref, c):
    return jnp.where(start_ref[c, ROWS : ROWS + 1, :] > 0.5, 2.0, 1.0)


def second_kernel(start_ref, part_ref, rest_ref, own_ask_ref, post_ref, ask_ref, hot_ref,
                  section_ref, swap_ref, sum_ref, got_ref):
    add_rest(part_ref, rest_ref, own_ask_ref, post_ref, sum_ref)
    for c in range(BLOCKS):
        section_ref[c] = start_ref[c, 0:ROWS, :] - (DT * metric_of(start_ref, c)) * sum_ref[c]
    reply(wide(section_ref, ROWS), ask_ref[3:8, :], hot_ref[...], got_ref, swap_ref)


def last_kernel(start_ref, section_ref, part_ref, rest_ref, own_ask_ref, post_ref,
                state_hbm, rate_hbm, sum_ref, state_ref, rate_ref, sems):
    add_rest(part_ref, rest_ref, own_ask_ref, post_ref, sum_ref)
    copies = []
    for c in range(BLOCKS):
        rate = -metric_of(start_ref, c) * sum_ref[c]
        rate_ref[c] = rate
        state_ref[c] = 0.5 * start_ref[c, 0:ROWS, :] + 0.5 * (section_ref[c] + DT * rate)
        for i, (src, dst) in enumerate(((rate_ref, rate_hbm), (state_ref, state_hbm))):
            copy = pltpu.make_async_copy(src.at[c], dst.at[:, pl.ds(128 * c, 128)], sems.at[i, c])
            copy.start()
            copies.append(copy)
    for copy in copies:
        copy.wait()


VM = pl.BlockSpec(memory_space=pltpu.VMEM)
SM = pl.BlockSpec(memory_space=pltpu.SMEM)
HB = pl.BlockSpec(memory_space=pltpu.HBM)


def call(kernel, outs, args, specs=None, scratch=(), flops=10**6, outs_in=None):
    return pl.pallas_call(
        kernel,
        out_shape=[jax.ShapeDtypeStruct(s, d) for s, d in outs],
        in_specs=specs or [VM] * len(args),
        out_specs=[outs_in or VM] * len(outs),
        scratch_shapes=[pltpu.VMEM(*s) if isinstance(s, tuple) else s for s in scratch],
        compiler_params=pltpu.CompilerParams(vmem_limit_bytes=24 * 2**20),
        cost_estimate=pl.CostEstimate(flops=flops, bytes_accessed=2**20, transcendentals=0),
    )(*args)


def swap_cores(x):
    n = lax.axis_size(AXES)
    return lax.ppermute(x, AXES, [(i, i ^ 1) for i in range(n)])


def swap_chips(x):
    n = lax.axis_size(AXES)
    return lax.ppermute(x, AXES, [(i, (i + (1 if i % 2 else -1)) % n) for i in range(n)])


def outward(x, by):
    n = lax.axis_size(AXES)
    return lax.ppermute(x, AXES, [(i, (i + (by if i % 2 == 0 else -by)) % n) for i in range(n)])


def outward_pair(own, got):
    b = outward(jnp.concatenate([own[2:3], got[3:5]], axis=0), 4)
    a = outward(jnp.concatenate([own[0:2], got[1:3]], axis=0), 2)
    return a, b


def swap_back(a, b):
    return swap_cores(jnp.concatenate([a[1:2], a[3:4], b[2:3]], axis=0))


def body(state_old, level_old, morton_old, neighbours):
    me = lax.axis_index(AXES).astype(I32).reshape(1)
    inputs = [
        pltpu.with_memory_space_constraint(x, pltpu.HBM)
        for x in (
            neighbours,
            state_old.reshape(ROWS, OLD_CAP),
            level_old.reshape(1, OLD_CAP),
            morton_old.reshape(1, OLD_CAP),
        )
    ]
    own_ask, swap_ask, near, far, state, level, morton = call(
        open_kernel,
        [
            ((3, 1, CAP), I32),
            ((5, 1, CAP), I32),
            ((6, NEW_DEV), I32),
            ((6, NEW_DEV), I32),
            ((ROWS, OLD_CAP), F32),
            ((1, OLD_CAP), I32),
            ((1, OLD_CAP), I32),
        ],
        (me, *inputs),
        [SM, HB, HB, HB, HB],
        [((6, NEW_DEV), I32), pltpu.SemaphoreType.DMA((4,))],
    )
    got = swap_cores(swap_ask)
    relay = [SM, VM, VM, VM]
    to_far, to_sib = call(pack_kernel, [((MOVED_ROWS, HALF), F32)] * 2, (me, state, level, morton), relay)
    got, to_far, to_sib, morton = lax.optimization_barrier((got, to_far, to_sib, morton))
    a, b = outward_pair(own_ask, got)
    from_far = swap_chips(to_far)
    from_sib = swap_cores(to_sib)
    (home,) = call(home_kernel, [((BLOCKS, MOVED_ROWS, 128), F32)], (me, state, level, morton), relay)
    post = swap_back(a, b)
    asked = jnp.concatenate(
        [post[1], post[0], post[2], got[0], a[2], a[0], b[1], b[0]], axis=0
    )

    rest_hot, reply_hot = call(
        hot_kernel,
        [((6, 3 * CAP, NEW_DEV), BF16), ((NEW_DEV, 5 * CAP), BF16)],
        (far, asked),
        flops=10**9,
    )
    swapped = ((5, TRACE_ROWS, CAP), F32)
    got_scratch = ((5, ROWS, CAP), F32)
    blocks = ((BLOCKS, ROWS, 128), F32)
    table = jnp.asarray(stacked_table())

    def neighbours_of(fields, swap):
        got = swap_cores(swap)
        (own,) = call(
            own_kernel,
            [((3, TRACE_ROWS, CAP), F32)],
            (fields, asked),
            None,
            [((3, ROWS, CAP), F32)],
        )
        a, b = outward_pair(own, got)
        (part,) = call(
            near_kernel,
            [blocks],
            (table, fields, near),
            None,
            [((FIELDS, 3 * DOFS, NEW_DEV), BF16)] * 2,
            flops=10**9,
        )
        a, b, part = lax.optimization_barrier((a, b, part))
        post = swap_back(a, b)
        (part,) = call(direct_kernel, [blocks], (part, far, swap_ask, a, b, got), flops=10**9)
        return part, rest_hot, own_ask, post

    start, swap = call(
        first_kernel,
        [((BLOCKS, MOVED_ROWS, 128), F32), swapped],
        (me, home, from_far, from_sib, asked, reply_hot),
        [SM, VM, VM, VM, VM, VM],
        [got_scratch],
    )
    ghosts = neighbours_of(start, swap)
    section, swap = call(
        second_kernel,
        [blocks, swapped],
        (start, *ghosts, asked, reply_hot),
        None,
        [blocks, got_scratch],
    )
    ghosts = neighbours_of(section, swap)
    new_state, rate = call(
        last_kernel,
        [((ROWS, NEW_DEV), F32)] * 2,
        (start, section, *ghosts),
        None,
        [blocks, blocks, blocks, pltpu.SemaphoreType.DMA((2, BLOCKS))],
        outs_in=HB,
    )
    shape = (FIELDS, DOFS, NEW_DEV)
    return new_state.reshape(shape), rate.reshape(shape)


def solution(mesh):
    wide = P(None, None, AXES)
    return jax.shard_map(
        body,
        mesh=mesh,
        in_specs=(wide, P(AXES), P(AXES), P(None, AXES)),
        out_specs=(wide, wide),
        check_vma=False,
    )
```

```python
import jax
import jax.numpy as jnp
import numpy as np
from jax import lax
from jax.experimental import pallas as pl
from jax.experimental.pallas import tpu as pltpu
from jax.sharding import PartitionSpec as P

FIELDS = 5
DOFS = 64
ROWS = FIELDS * DOFS
NEW_DEV = 512
HALF = NEW_DEV // 2
OLD_CAP = 1024
CAP = 128
TRACE_ROWS = FIELDS * 16
MOVED_ROWS = ROWS + 8
BLOCKS = NEW_DEV // 128

HEAT = 1.4
SPEED = 4.0
DT = 0.0002
AXES = ("px", "py")
F32 = jnp.float32
BF16 = jnp.bfloat16
I32 = jnp.int32

STEPS = (2, 3, 4, 1, -1, -2, -3, -4)


def derivative_table():
    points = np.array([-1.0, -1.0 / np.sqrt(5.0), 1.0 / np.sqrt(5.0), 1.0])
    weights = np.array(
        [1.0 / np.prod([points[c] - points[o] for o in range(4) if o != c]) for c in range(4)]
    )
    table = np.zeros((4, 4))
    for r in range(4):
        for c in range(4):
            if r != c:
                table[r, c] = weights[c] / weights[r] / (points[r] - points[c])
        table[r, r] = -np.sum(table[r])
    return table


def stacked_table():
    d = derivative_table().astype(np.float32).astype(np.float64)
    one = np.eye(4)
    full = np.concatenate(
        [
            np.kron(np.kron(d, one), one),
            np.kron(np.kron(one, d), one),
            np.kron(np.kron(one, one), d),
        ],
        axis=1,
    ).astype(np.float32)
    high = full.astype(jnp.bfloat16)
    low = (full - high.astype(np.float32)).astype(jnp.bfloat16)
    return np.concatenate([high, low], axis=0)


def split(x):
    high = x.astype(BF16)
    low = (x - high.astype(F32)).astype(BF16)
    return high, low


def dot(a, b):
    return lax.dot_general(a, b, (((1,), (0,)), ((), ())), preferred_element_type=F32)


def dot_nt(a, b):
    return lax.dot_general(a, b, (((1,), (1,)), ((), ())), preferred_element_type=F32)


def one_hot_rows(size, row):
    spots = lax.broadcasted_iota(I32, (size, row.shape[1]), 0)
    return jnp.where(spots == row, 1.0, 0.0).astype(BF16)


def relay_slots(me, morton):
    occupied = morton >= 0
    owner = morton >> 9
    slot = morton & (NEW_DEV - 1)
    gap = (owner - me) & 127
    even = (me & 1) == 0
    to_next = occupied & (gap == 1)
    to_prior = occupied & (gap == 127)
    home = jnp.where(occupied & (gap == 0), slot, -1)
    ahead = jnp.where(to_next, slot, -1)
    behind = jnp.where(to_prior, slot - HALF, -1)
    sib = jnp.where(even, ahead, behind)
    far = jnp.where(even, behind, ahead)
    return sib, far, home


def store_moved(ref, got):
    ref[0:ROWS, :] = got[0:ROWS] + got[ROWS : 2 * ROWS]
    ref[ROWS : ROWS + 8, :] = got[2 * ROWS : 2 * ROWS + 8]


def relay_rows(state, level):
    high, low = split(state)
    lev = jnp.broadcast_to(level.astype(F32), (16, OLD_CAP)).astype(BF16)
    return jnp.concatenate([high, low, lev], axis=0)


def open_kernel(me_ref, links_hbm, state_hbm, level_hbm, morton_hbm, own_ask_ref, swap_ask_ref, near_ref, far_ref,
                state_ref, level_ref, morton_ref, links_ref, sems):
    pairs = ((links_hbm, links_ref), (morton_hbm, morton_ref), (level_hbm, level_ref), (state_hbm, state_ref))
    copies = [pltpu.make_async_copy(src, dst, sems.at[i]) for i, (src, dst) in enumerate(pairs)]
    for copy in copies:
        copy.start()
    copies[0].wait()
    ask = requests(me_ref[0], links_ref[...], near_ref, far_ref)
    for t in range(8):
        if t < 3:
            own_ask_ref[t] = ask[t : t + 1]
        else:
            swap_ask_ref[t - 3] = ask[t : t + 1]
    for copy in copies[1:]:
        copy.wait()


def far_kernel(me_ref, state_ref, level_ref, morton_ref, far_ref):
    _, far, _ = relay_slots(me_ref[0], morton_ref[...])
    lhs = relay_rows(state_ref[...], level_ref[...])
    store_moved(far_ref, dot_nt(lhs, one_hot_rows(HALF, far)))


def sib_kernel(me_ref, state_ref, level_ref, morton_ref, sib_ref):
    sib, _, _ = relay_slots(me_ref[0], morton_ref[...])
    lhs = relay_rows(state_ref[...], level_ref[...])
    store_moved(sib_ref, dot_nt(lhs, one_hot_rows(HALF, sib)))


def home_kernel(me_ref, state_ref, level_ref, morton_ref, home_ref):
    _, _, home = relay_slots(me_ref[0], morton_ref[...])
    got = dot_nt(relay_rows(state_ref[...], level_ref[...]), one_hot_rows(NEW_DEV, home))
    for c in range(BLOCKS):
        store_moved(home_ref.at[c], got[:, 128 * c : 128 * c + 128])


def requests(me, links, near_ref, far_ref):
    owner = links >> 9
    slot = links & (NEW_DEV - 1)
    gap = ((owner - me + 192) & 127) - 64
    gap = jnp.where((me & 1) == 0, gap, -gap)
    near_ref[...] = jnp.where(gap == 0, slot, -1)
    b = lax.broadcasted_iota(I32, (8, NEW_DEV), 0)
    step_of = jnp.where(b < 3, b + 2, jnp.where(b == 3, 1, 3 - b))
    masks = [jnp.where(gap[f : f + 1, :] == step_of, 1.0, 0.0) for f in range(6)]
    k = lax.broadcasted_iota(I32, (NEW_DEV, NEW_DEV), 0)
    j = lax.broadcasted_iota(I32, (NEW_DEV, NEW_DEV), 1)
    upper = jnp.where(k <= j, 1.0, 0.0).astype(BF16)
    counts = dot(jnp.concatenate(masks, axis=0).astype(BF16), upper)
    offset = jnp.full((8, 1), -1.0, F32)
    bf = b.astype(F32)
    total = jnp.zeros((16, CAP), F32)
    for f in range(6):
        run = counts[8 * f : 8 * f + 8, :]
        here = gap[f : f + 1, :] != 0
        rank = jnp.sum(masks[f] * (run + offset), axis=0, keepdims=True)
        bucket = jnp.sum(masks[f] * bf, axis=0, keepdims=True)
        offset = offset + run[:, NEW_DEV - 1 : NEW_DEV]
        rank = jnp.where(here, rank.astype(I32), -1)
        far_ref[f : f + 1, :] = jnp.where(here, bucket.astype(I32) * CAP + rank, -1)
        s = slot[f : f + 1, :]
        low = (s & 255).astype(F32)
        high = ((s >> 8) + 2 * (f ^ 1)).astype(F32)
        lhs = jnp.concatenate([masks[f] * low, masks[f] * high], axis=0).astype(BF16)
        total = total + dot_nt(lhs, one_hot_rows(CAP, rank))
    return total[0:8].astype(I32) + 256 * total[8:16].astype(I32)


def lower_half(shape):
    return lax.broadcasted_iota(I32, shape, 0) < 4


def trace(ref, c, v, f):
    a, s = f // 2, f % 2
    at = v * DOFS
    if a == 0:
        return ref[c, at + 48 * s : at + 48 * s + 16, :]
    if a == 1:
        out = []
        for h in range(2):
            r = at + 32 * h + 8 * s
            x = ref[c, r : r + 8, :]
            y = ref[c, r + 16 : r + 24, :]
            low = lower_half(x.shape)
            if s == 0:
                out.append(jnp.where(low, x, pltpu.roll(y, 4, 0)))
            else:
                out.append(jnp.where(low, pltpu.roll(x, 4, 0), y))
        return jnp.concatenate(out, axis=0)
    return ref[c, pl.ds(at + 3 * s, 16, stride=4), :]


def add_on_face(ref, c, v, f, x):
    a, s = f // 2, f % 2
    at = v * DOFS
    if a == 0:
        ref[c, at + 48 * s : at + 48 * s + 16, :] += x
    elif a == 1:
        for h in range(2):
            y = x[8 * h : 8 * h + 8, :]
            low = lower_half(y.shape)
            keep = low if s == 0 else ~low
            turned = pltpu.roll(y, 4, 0)
            first, second = (y, turned) if s == 0 else (turned, y)
            r = at + 32 * h + 8 * s
            ref[c, r : r + 8, :] += jnp.where(keep, first, 0.0)
            ref[c, r + 16 : r + 24, :] += jnp.where(keep, second, 0.0)
    else:
        spot = (c, pl.ds(at + 3 * s, 16, stride=4), slice(None))
        ref[spot] = ref[spot] + x


def wide(ref, rows):
    return jnp.concatenate([ref[c, 0:rows, :] for c in range(ref.shape[0])], axis=1)


def pressure_of(w, u):
    return (HEAT - 1.0) * (w[4] - 0.5 * (w[1] * u[0] + w[2] * u[1] + w[3] * u[2]))


def axis_flux(w, u, p, a):
    un = u[a]
    out = [w[1 + a]]
    for c in range(3):
        m = w[1 + c] * un
        out.append(m + p if c == a else m)
    out.append((w[4] + p) * un)
    return out


def side_term(w, f):
    sign = 1.0 if f % 2 else -1.0
    u = [w[1 + c] / w[0] for c in range(3)]
    p = pressure_of(w, u)
    flux = axis_flux(w, u, p, f // 2)
    return [(sign * flux[v]) - SPEED * w[v] for v in range(FIELDS)]


def asked_code(ask):
    return jnp.concatenate([ask[t : t + 1, :] for t in range(ask.shape[0])], axis=1)


def reply(fields, ask, hot, got_ref, outs):
    chunks = ask.shape[0]
    high, low = split(fields)
    both = dot(jnp.concatenate([high, low], axis=0), hot)
    for t in range(chunks):
        spot = slice(CAP * t, CAP * t + CAP)
        got_ref[t] = both[0:ROWS, spot] + both[ROWS:, spot]
    for t in range(chunks):
        face = ask[t : t + 1, :] >> 9
        for v in range(FIELDS):
            x = trace(got_ref, t, v, 0)
            for f in range(1, 6):
                x = jnp.where(face == f, trace(got_ref, t, v, f), x)
            outs[t][16 * v : 16 * v + 16, :] = x


def hot_kernel(far_ref, ask_ref, rest_ref, reply_ref):
    for f in range(6):
        rest_ref[f] = one_hot_rows(3 * CAP, far_ref[f : f + 1, :])
    reply_ref[...] = one_hot_rows(NEW_DEV, asked_code(ask_ref[4:8, :]) & (NEW_DEV - 1))


def own_kernel(fields_ref, ask_ref, a_ref, b_ref, sib_ref, got_ref):
    ask = ask_ref[0:4, :]
    hot = one_hot_rows(NEW_DEV, asked_code(ask) & (NEW_DEV - 1))
    outs = [a_ref.at[0], a_ref.at[1], b_ref.at[0], sib_ref.at[0]]
    reply(wide(fields_ref, ROWS), ask, hot, got_ref, outs)


def first_kernel(me_ref, home_ref, far_ref, sib_ref, ask_ref, hot_ref, start_ref, swap_ref, got_ref):
    even = (me_ref[0] & 1) == 0
    for c in range(2):
        spot = slice(128 * c, 128 * c + 128)
        sib = sib_ref[:, spot]
        far = far_ref[:, spot]
        start_ref[c] = home_ref[c] + jnp.where(even, far, sib)
        start_ref[c + 2] = home_ref[c + 2] + jnp.where(even, sib, far)
    reply(wide(start_ref, ROWS), ask_ref[4:8, :], hot_ref[...], got_ref, [swap_ref.at[t] for t in range(4)])


def near_kernel(table_ref, fields_ref, near_ref, part_ref, high_ref, low_ref):
    for c in range(BLOCKS):
        spot = slice(128 * c, 128 * c + 128)
        w = [fields_ref[c, DOFS * v : DOFS * v + DOFS, :] for v in range(FIELDS)]
        u = [w[1 + i] / w[0] for i in range(3)]
        p = pressure_of(w, u)
        for a in range(3):
            flux = axis_flux(w, u, p, a)
            for v in range(FIELDS):
                high, low = split(flux[v])
                high_ref[v, DOFS * a : DOFS * a + DOFS, spot] = high
                low_ref[v, DOFS * a : DOFS * a + DOFS, spot] = low
    table = table_ref[...]
    for v in range(FIELDS):
        x = dot(table, high_ref[v])
        x = x[0:DOFS] + x[DOFS:] + dot(table[0:DOFS], low_ref[v])
        for c in range(BLOCKS):
            part_ref[c, DOFS * v : DOFS * v + DOFS, :] = x[:, 128 * c : 128 * c + 128]
    for f in range(6):
        hot = one_hot_rows(NEW_DEV, near_ref[f : f + 1, :])
        across = jnp.concatenate(
            [
                jnp.concatenate([trace(fields_ref, c, v, f ^ 1) for v in range(FIELDS)], axis=0)
                for c in range(BLOCKS)
            ],
            axis=1,
        )
        high, low = split(across)
        both = dot(jnp.concatenate([high, low], axis=0), hot)
        for c in range(BLOCKS):
            spot = slice(128 * c, 128 * c + 128)
            outer = both[0:TRACE_ROWS, spot] + both[TRACE_ROWS:, spot]
            there = near_ref[f : f + 1, spot] >= 0
            w = [outer[16 * v : 16 * v + 16] for v in range(FIELDS)]
            w[0] = jnp.where(there, w[0], 1.0)
            plus = side_term(w, f)
            minus = side_term([trace(fields_ref, c, v, f) for v in range(FIELDS)], f)
            for v in range(FIELDS):
                add_on_face(part_ref, c, v, f, 3.0 * (jnp.where(there, plus[v], 0.0) - minus[v]))


def ghost_terms(ghost, ask):
    face = (ask >> 9) ^ 1
    axis = face >> 1
    sign = jnp.where((face & 1) == 1, 3.0, -3.0)
    w = [ghost[16 * v : 16 * v + 16] for v in range(FIELDS)]
    u = [w[1 + c] / w[0] for c in range(3)]
    p = pressure_of(w, u)

    def along(x):
        return jnp.where(axis == 0, x[0], jnp.where(axis == 1, x[1], x[2]))

    un = along(u)
    flux = [along(w[1:4])]
    for c in range(3):
        flux.append(w[1 + c] * un + jnp.where(axis == c, p, 0.0))
    flux.append((w[4] + p) * un)
    return jnp.concatenate([sign * flux[v] - (3.0 * SPEED) * w[v] for v in range(FIELDS)], axis=0)


def ghost_rows(ghosts, ask_ref):
    parts = [split(ghost_terms(g, ask_ref[t])) for t, g in enumerate(ghosts)]
    high = jnp.concatenate([p[0] for p in parts], axis=1)
    low = jnp.concatenate([p[1] for p in parts], axis=1)
    return jnp.concatenate([high, low], axis=0)


def add_ghosts(sum_ref, lhs, hot_of, blocks=range(BLOCKS)):
    for f in range(6):
        both = dot(lhs, hot_of(f))
        for i, c in enumerate(blocks):
            spot = slice(128 * i, 128 * i + 128)
            term = both[0:TRACE_ROWS, spot] + both[TRACE_ROWS:, spot]
            for v in range(FIELDS):
                add_on_face(sum_ref, c, v, f, term[16 * v : 16 * v + 16])


def direct_kernel(part_ref, far_ref, ask_ref, a_ref, b_ref, sib_ref, sum_ref):
    lhs = ghost_rows([sib_ref[0], a_ref[2], a_ref[0], b_ref[1], b_ref[0]], ask_ref)
    sum_ref[...] = part_ref[...]
    add_ghosts(sum_ref, lhs, lambda f: one_hot_rows(5 * CAP, far_ref[f : f + 1, :] - 3 * CAP))


def metric_of(start_ref, c):
    return jnp.where(start_ref[c, ROWS : ROWS + 1, :] > 0.5, 2.0, 1.0)


def second_kernel(start_ref, part_ref, rest_ref, own_ask_ref, post_ref, ask_ref, hot_ref,
                  section_ref, swap_ref, sum_ref, got_ref):
    lhs = ghost_rows([post_ref[1], post_ref[0], post_ref[2]], own_ask_ref)
    sum_ref[...] = part_ref[...]
    add_ghosts(sum_ref, lhs, lambda f: rest_ref[f])
    for c in range(BLOCKS):
        section_ref[c] = start_ref[c, 0:ROWS, :] - (DT * metric_of(start_ref, c)) * sum_ref[c]
    reply(wide(section_ref, ROWS), ask_ref[4:8, :], hot_ref[...], got_ref, [swap_ref.at[t] for t in range(4)])


def last_kernel(start_ref, section_ref, part_ref, rest_ref, own_ask_ref, post_ref,
                state_hbm, rate_hbm, sum_ref, state_ref, rate_ref, sems):
    lhs = ghost_rows([post_ref[1], post_ref[0], post_ref[2]], own_ask_ref)
    sum_ref[...] = part_ref[...]
    copies = []
    for half in range(2):
        pair = (2 * half, 2 * half + 1)
        add_ghosts(sum_ref, lhs, lambda f: rest_ref[f, :, HALF * half : HALF * half + HALF], pair)
        for c in pair:
            rate = -metric_of(start_ref, c) * sum_ref[c]
            rate_ref[c] = rate
            state_ref[c] = 0.5 * start_ref[c, 0:ROWS, :] + 0.5 * (section_ref[c] + DT * rate)
            for i, (src, dst) in enumerate(((rate_ref, rate_hbm), (state_ref, state_hbm))):
                copy = pltpu.make_async_copy(src.at[c], dst.at[:, pl.ds(128 * c, 128)], sems.at[i, c])
                copy.start()
                copies.append(copy)
    for copy in copies:
        copy.wait()


VM = pl.BlockSpec(memory_space=pltpu.VMEM)
SM = pl.BlockSpec(memory_space=pltpu.SMEM)
HB = pl.BlockSpec(memory_space=pltpu.HBM)


def call(kernel, outs, args, specs=None, scratch=(), flops=10**6, outs_in=None):
    return pl.pallas_call(
        kernel,
        out_shape=[jax.ShapeDtypeStruct(s, d) for s, d in outs],
        in_specs=specs or [VM] * len(args),
        out_specs=[outs_in or VM] * len(outs),
        scratch_shapes=[pltpu.VMEM(*s) if isinstance(s, tuple) else s for s in scratch],
        compiler_params=pltpu.CompilerParams(vmem_limit_bytes=24 * 2**20),
        cost_estimate=pl.CostEstimate(flops=flops, bytes_accessed=2**20, transcendentals=0),
    )(*args)


def swap_cores(x):
    n = lax.axis_size(AXES)
    return lax.ppermute(x, AXES, [(i, i ^ 1) for i in range(n)])


def swap_chips(x):
    n = lax.axis_size(AXES)
    return lax.ppermute(x, AXES, [(i, (i + (1 if i % 2 else -1)) % n) for i in range(n)])


def outward(x, by):
    n = lax.axis_size(AXES)
    return lax.ppermute(x, AXES, [(i, (i + (by if i % 2 == 0 else -by)) % n) for i in range(n)])


def outward_pair(own, got):
    b = outward(jnp.concatenate([own[1], got[2:4]], axis=0), 4)
    a = outward(jnp.concatenate([own[0], got[0:2]], axis=0), 2)
    return a, b


def swap_back(a, b):
    return swap_cores(jnp.concatenate([a[1:2], a[3:4], b[2:3]], axis=0))


def body(state_old, level_old, morton_old, neighbours):
    me = lax.axis_index(AXES).astype(I32).reshape(1)
    inputs = [
        pltpu.with_memory_space_constraint(x, pltpu.HBM)
        for x in (
            neighbours,
            state_old.reshape(ROWS, OLD_CAP),
            level_old.reshape(1, OLD_CAP),
            morton_old.reshape(1, OLD_CAP),
        )
    ]
    own_ask, swap_ask, near, far, state, level, morton = call(
        open_kernel,
        [
            ((3, 1, CAP), I32),
            ((5, 1, CAP), I32),
            ((6, NEW_DEV), I32),
            ((6, NEW_DEV), I32),
            ((ROWS, OLD_CAP), F32),
            ((1, OLD_CAP), I32),
            ((1, OLD_CAP), I32),
        ],
        (me, *inputs),
        [SM, HB, HB, HB, HB],
        [((6, NEW_DEV), I32), pltpu.SemaphoreType.DMA((4,))],
    )
    got = swap_cores(swap_ask)
    relay = [SM, VM, VM, VM]
    moved = ((MOVED_ROWS, HALF), F32)
    (to_far,) = call(far_kernel, [moved], (me, state, level, morton), relay)
    got, to_far = lax.optimization_barrier((got, to_far))
    a, b = outward_pair((own_ask[0:2], own_ask[2:3]), got[1:5])
    from_far = swap_chips(to_far)
    a, morton = lax.optimization_barrier((a, morton))
    (to_sib,) = call(sib_kernel, [moved], (me, state, level, morton), relay, flops=10**9)
    from_sib = swap_cores(to_sib)
    (home,) = call(home_kernel, [((BLOCKS, MOVED_ROWS, 128), F32)], (me, state, level, morton), relay)
    post = swap_back(a, b)
    asked = jnp.concatenate(
        [post[1], post[0], post[2], got[0], a[2], a[0], b[1], b[0]], axis=0
    )

    rest_hot, reply_hot = call(
        hot_kernel,
        [((6, 3 * CAP, NEW_DEV), BF16), ((NEW_DEV, 4 * CAP), BF16)],
        (far, asked),
        flops=10**9,
    )
    swapped = ((4, TRACE_ROWS, CAP), F32)
    got_scratch = ((4, ROWS, CAP), F32)
    blocks = ((BLOCKS, ROWS, 128), F32)
    table = jnp.asarray(stacked_table())

    def neighbours_of(fields, swap):
        got = swap_cores(swap)
        *own, sib = call(
            own_kernel,
            [((2, TRACE_ROWS, CAP), F32), ((1, TRACE_ROWS, CAP), F32), ((1, TRACE_ROWS, CAP), F32)],
            (fields, asked),
            None,
            [got_scratch],
            flops=10**9,
        )
        a, b = outward_pair(own, got)
        (part,) = call(
            near_kernel,
            [blocks],
            (table, fields, near),
            None,
            [((FIELDS, 3 * DOFS, NEW_DEV), BF16)] * 2,
            flops=10**9,
        )
        sib, part = lax.optimization_barrier((sib, part))
        sib = swap_cores(sib)
        a, b, part = lax.optimization_barrier((a, b, part))
        post = swap_back(a, b)
        (part,) = call(direct_kernel, [blocks], (part, far, swap_ask, a, b, sib), flops=10**9)
        return part, rest_hot, own_ask, post

    start, swap = call(
        first_kernel,
        [((BLOCKS, MOVED_ROWS, 128), F32), swapped],
        (me, home, from_far, from_sib, asked, reply_hot),
        [SM, VM, VM, VM, VM, VM],
        [got_scratch],
    )
    ghosts = neighbours_of(start, swap)
    section, swap = call(
        second_kernel,
        [blocks, swapped],
        (start, *ghosts, asked, reply_hot),
        None,
        [blocks, got_scratch],
    )
    ghosts = neighbours_of(section, swap)
    new_state, rate = call(
        last_kernel,
        [((ROWS, NEW_DEV), F32)] * 2,
        (start, section, *ghosts),
        None,
        [blocks, blocks, blocks, pltpu.SemaphoreType.DMA((2, BLOCKS))],
        outs_in=HB,
    )
    shape = (FIELDS, DOFS, NEW_DEV)
    return new_state.reshape(shape), rate.reshape(shape)


def solution(mesh):
    wide = P(None, None, AXES)
    return jax.shard_map(
        body,
        mesh=mesh,
        in_specs=(wide, P(AXES), P(AXES), P(None, AXES)),
        out_specs=(wide, wide),
        check_vma=False,
    )
```

```python
import jax
import jax.numpy as jnp
import numpy as np
from jax import lax
from jax.experimental import pallas as pl
from jax.experimental.pallas import tpu as pltpu
from jax.sharding import PartitionSpec as P

FIELDS = 5
DOFS = 64
ROWS = FIELDS * DOFS
NEW_DEV = 512
HALF = NEW_DEV // 2
OLD_CAP = 1024
CAP = 128
TRACE_ROWS = FIELDS * 16
MOVED_ROWS = ROWS + 8
BLOCKS = NEW_DEV // 128

HEAT = 1.4
SPEED = 4.0
DT = 0.0002
AXES = ("px", "py")
F32 = jnp.float32
BF16 = jnp.bfloat16
I32 = jnp.int32

STEPS = (2, 3, 4, 1, -1, -2, -3, -4)


def derivative_table():
    points = np.array([-1.0, -1.0 / np.sqrt(5.0), 1.0 / np.sqrt(5.0), 1.0])
    weights = np.array(
        [1.0 / np.prod([points[c] - points[o] for o in range(4) if o != c]) for c in range(4)]
    )
    table = np.zeros((4, 4))
    for r in range(4):
        for c in range(4):
            if r != c:
                table[r, c] = weights[c] / weights[r] / (points[r] - points[c])
        table[r, r] = -np.sum(table[r])
    return table


def stacked_table():
    d = derivative_table().astype(np.float32).astype(np.float64)
    one = np.eye(4)
    full = np.concatenate(
        [
            np.kron(np.kron(d, one), one),
            np.kron(np.kron(one, d), one),
            np.kron(np.kron(one, one), d),
        ],
        axis=1,
    ).astype(np.float32)
    high = full.astype(jnp.bfloat16)
    low = (full - high.astype(np.float32)).astype(jnp.bfloat16)
    return np.concatenate([high, low], axis=0)


def split(x):
    high = x.astype(BF16)
    low = (x - high.astype(F32)).astype(BF16)
    return high, low


def dot(a, b):
    return lax.dot_general(a, b, (((1,), (0,)), ((), ())), preferred_element_type=F32)


def dot_nt(a, b):
    return lax.dot_general(a, b, (((1,), (1,)), ((), ())), preferred_element_type=F32)


def one_hot_rows(size, row):
    spots = lax.broadcasted_iota(I32, (size, row.shape[1]), 0)
    return jnp.where(spots == row, 1.0, 0.0).astype(BF16)


def relay_slots(me, morton):
    occupied = morton >= 0
    owner = morton >> 9
    slot = morton & (NEW_DEV - 1)
    gap = (owner - me) & 127
    even = (me & 1) == 0
    to_next = occupied & (gap == 1)
    to_prior = occupied & (gap == 127)
    home = jnp.where(occupied & (gap == 0), slot, -1)
    ahead = jnp.where(to_next, slot, -1)
    behind = jnp.where(to_prior, slot - HALF, -1)
    sib = jnp.where(even, ahead, behind)
    far = jnp.where(even, behind, ahead)
    return sib, far, home


def store_moved(ref, got):
    ref[0:ROWS, :] = got[0:ROWS] + got[ROWS : 2 * ROWS]
    ref[ROWS : ROWS + 8, :] = got[2 * ROWS : 2 * ROWS + 8]


def relay_rows(state, level):
    high, low = split(state)
    lev = jnp.broadcast_to(level.astype(F32), (16, OLD_CAP)).astype(BF16)
    return jnp.concatenate([high, low, lev], axis=0)


def open_kernel(me_ref, links_hbm, state_hbm, level_hbm, morton_hbm, own_ask_ref, swap_ask_ref, near_ref, far_ref,
                state_ref, level_ref, morton_ref, links_ref, sems):
    pairs = ((links_hbm, links_ref), (morton_hbm, morton_ref), (level_hbm, level_ref), (state_hbm, state_ref))
    copies = [pltpu.make_async_copy(src, dst, sems.at[i]) for i, (src, dst) in enumerate(pairs)]
    for copy in copies:
        copy.start()
    copies[0].wait()
    ask = requests(me_ref[0], links_ref[...], near_ref, far_ref)
    for t in range(8):
        if t < 3:
            own_ask_ref[t] = ask[t : t + 1]
        else:
            swap_ask_ref[t - 3] = ask[t : t + 1]
    for copy in copies[1:]:
        copy.wait()


def far_kernel(me_ref, state_ref, level_ref, morton_ref, far_ref):
    _, far, _ = relay_slots(me_ref[0], morton_ref[...])
    lhs = relay_rows(state_ref[...], level_ref[...])
    store_moved(far_ref, dot_nt(lhs, one_hot_rows(HALF, far)))


def sib_kernel(me_ref, state_ref, level_ref, morton_ref, sib_ref):
    sib, _, _ = relay_slots(me_ref[0], morton_ref[...])
    lhs = relay_rows(state_ref[...], level_ref[...])
    store_moved(sib_ref, dot_nt(lhs, one_hot_rows(HALF, sib)))


def home_kernel(me_ref, state_ref, level_ref, morton_ref, home_ref):
    _, _, home = relay_slots(me_ref[0], morton_ref[...])
    got = dot_nt(relay_rows(state_ref[...], level_ref[...]), one_hot_rows(NEW_DEV, home))
    for c in range(BLOCKS):
        store_moved(home_ref.at[c], got[:, 128 * c : 128 * c + 128])


def requests(me, links, near_ref, far_ref):
    owner = links >> 9
    slot = links & (NEW_DEV - 1)
    gap = ((owner - me + 192) & 127) - 64
    gap = jnp.where((me & 1) == 0, gap, -gap)
    near_ref[...] = jnp.where(gap == 0, slot, -1)
    b = lax.broadcasted_iota(I32, (8, NEW_DEV), 0)
    step_of = jnp.where(b < 3, b + 2, jnp.where(b == 3, 1, 3 - b))
    masks = [jnp.where(gap[f : f + 1, :] == step_of, 1.0, 0.0) for f in range(6)]
    k = lax.broadcasted_iota(I32, (NEW_DEV, NEW_DEV), 0)
    j = lax.broadcasted_iota(I32, (NEW_DEV, NEW_DEV), 1)
    upper = jnp.where(k <= j, 1.0, 0.0).astype(BF16)
    counts = dot(jnp.concatenate(masks, axis=0).astype(BF16), upper)
    offset = jnp.full((8, 1), -1.0, F32)
    bf = b.astype(F32)
    total = jnp.zeros((16, CAP), F32)
    for f in range(6):
        run = counts[8 * f : 8 * f + 8, :]
        here = gap[f : f + 1, :] != 0
        rank = jnp.sum(masks[f] * (run + offset), axis=0, keepdims=True)
        bucket = jnp.sum(masks[f] * bf, axis=0, keepdims=True)
        offset = offset + run[:, NEW_DEV - 1 : NEW_DEV]
        rank = jnp.where(here, rank.astype(I32), -1)
        far_ref[f : f + 1, :] = jnp.where(here, bucket.astype(I32) * CAP + rank, -1)
        s = slot[f : f + 1, :]
        low = (s & 255).astype(F32)
        high = ((s >> 8) + 2 * (f ^ 1)).astype(F32)
        lhs = jnp.concatenate([masks[f] * low, masks[f] * high], axis=0).astype(BF16)
        total = total + dot_nt(lhs, one_hot_rows(CAP, rank))
    return total[0:8].astype(I32) + 256 * total[8:16].astype(I32)


def lower_half(shape):
    return lax.broadcasted_iota(I32, shape, 0) < 4


def trace(ref, c, v, f):
    a, s = f // 2, f % 2
    at = v * DOFS
    if a == 0:
        return ref[c, at + 48 * s : at + 48 * s + 16, :]
    if a == 1:
        out = []
        for h in range(2):
            r = at + 32 * h + 8 * s
            x = ref[c, r : r + 8, :]
            y = ref[c, r + 16 : r + 24, :]
            low = lower_half(x.shape)
            if s == 0:
                out.append(jnp.where(low, x, pltpu.roll(y, 4, 0)))
            else:
                out.append(jnp.where(low, pltpu.roll(x, 4, 0), y))
        return jnp.concatenate(out, axis=0)
    return ref[c, pl.ds(at + 3 * s, 16, stride=4), :]


def add_on_face(ref, c, v, f, x):
    a, s = f // 2, f % 2
    at = v * DOFS
    if a == 0:
        ref[c, at + 48 * s : at + 48 * s + 16, :] += x
    elif a == 1:
        for h in range(2):
            y = x[8 * h : 8 * h + 8, :]
            low = lower_half(y.shape)
            keep = low if s == 0 else ~low
            turned = pltpu.roll(y, 4, 0)
            first, second = (y, turned) if s == 0 else (turned, y)
            r = at + 32 * h + 8 * s
            ref[c, r : r + 8, :] += jnp.where(keep, first, 0.0)
            ref[c, r + 16 : r + 24, :] += jnp.where(keep, second, 0.0)
    else:
        spot = (c, pl.ds(at + 3 * s, 16, stride=4), slice(None))
        ref[spot] = ref[spot] + x


def wide(ref, rows):
    return jnp.concatenate([ref[c, 0:rows, :] for c in range(ref.shape[0])], axis=1)


def pressure_of(w, u):
    return (HEAT - 1.0) * (w[4] - 0.5 * (w[1] * u[0] + w[2] * u[1] + w[3] * u[2]))


def axis_flux(w, u, p, a):
    un = u[a]
    out = [w[1 + a]]
    for c in range(3):
        m = w[1 + c] * un
        out.append(m + p if c == a else m)
    out.append((w[4] + p) * un)
    return out


def side_term(w, f):
    sign = 1.0 if f % 2 else -1.0
    u = [w[1 + c] / w[0] for c in range(3)]
    p = pressure_of(w, u)
    flux = axis_flux(w, u, p, f // 2)
    return [(sign * flux[v]) - SPEED * w[v] for v in range(FIELDS)]


def asked_code(ask):
    return jnp.concatenate([ask[t : t + 1, :] for t in range(ask.shape[0])], axis=1)


def reply(fields, ask, hot, got_ref, outs):
    chunks = ask.shape[0]
    high, low = split(fields)
    both = dot(jnp.concatenate([high, low], axis=0), hot)
    for t in range(chunks):
        spot = slice(CAP * t, CAP * t + CAP)
        got_ref[t] = both[0:ROWS, spot] + both[ROWS:, spot]
    for t in range(chunks):
        face = ask[t : t + 1, :] >> 9
        for v in range(FIELDS):
            x = trace(got_ref, t, v, 0)
            for f in range(1, 6):
                x = jnp.where(face == f, trace(got_ref, t, v, f), x)
            outs[t][16 * v : 16 * v + 16, :] = x


def hot_kernel(far_ref, ask_ref, rest_ref, reply_ref):
    for f in range(6):
        rest_ref[f] = one_hot_rows(3 * CAP, far_ref[f : f + 1, :])
    reply_ref[...] = one_hot_rows(NEW_DEV, asked_code(ask_ref[4:8, :]) & (NEW_DEV - 1))


def own_kernel(fields_ref, ask_ref, a_ref, b_ref, sib_ref, got_ref):
    ask = ask_ref[0:4, :]
    hot = one_hot_rows(NEW_DEV, asked_code(ask) & (NEW_DEV - 1))
    outs = [a_ref.at[0], a_ref.at[1], b_ref.at[0], sib_ref.at[0]]
    reply(wide(fields_ref, ROWS), ask, hot, got_ref, outs)


def first_kernel(me_ref, home_ref, prior_ref, next_ref, sib_ref, ask_ref, hot_ref, start_ref, swap_ref, got_ref):
    even = (me_ref[0] & 1) == 0
    for c in range(2):
        spot = slice(128 * c, 128 * c + 128)
        sib = sib_ref[:, spot]
        start_ref[c] = home_ref[c] + jnp.where(even, prior_ref[:, spot], sib)
        start_ref[c + 2] = home_ref[c + 2] + jnp.where(even, sib, next_ref[:, spot])
    reply(wide(start_ref, ROWS), ask_ref[4:8, :], hot_ref[...], got_ref, [swap_ref.at[t] for t in range(4)])


def near_kernel(table_ref, fields_ref, near_ref, part_ref, high_ref, low_ref):
    for c in range(BLOCKS):
        spot = slice(128 * c, 128 * c + 128)
        w = [fields_ref[c, DOFS * v : DOFS * v + DOFS, :] for v in range(FIELDS)]
        u = [w[1 + i] / w[0] for i in range(3)]
        p = pressure_of(w, u)
        for a in range(3):
            flux = axis_flux(w, u, p, a)
            for v in range(FIELDS):
                high, low = split(flux[v])
                high_ref[v, DOFS * a : DOFS * a + DOFS, spot] = high
                low_ref[v, DOFS * a : DOFS * a + DOFS, spot] = low
    table = table_ref[...]
    for v in range(FIELDS):
        x = dot(table, high_ref[v])
        x = x[0:DOFS] + x[DOFS:] + dot(table[0:DOFS], low_ref[v])
        for c in range(BLOCKS):
            part_ref[c, DOFS * v : DOFS * v + DOFS, :] = x[:, 128 * c : 128 * c + 128]
    for f in range(6):
        hot = one_hot_rows(NEW_DEV, near_ref[f : f + 1, :])
        across = jnp.concatenate(
            [
                jnp.concatenate([trace(fields_ref, c, v, f ^ 1) for v in range(FIELDS)], axis=0)
                for c in range(BLOCKS)
            ],
            axis=1,
        )
        high, low = split(across)
        both = dot(jnp.concatenate([high, low], axis=0), hot)
        for c in range(BLOCKS):
            spot = slice(128 * c, 128 * c + 128)
            outer = both[0:TRACE_ROWS, spot] + both[TRACE_ROWS:, spot]
            there = near_ref[f : f + 1, spot] >= 0
            w = [outer[16 * v : 16 * v + 16] for v in range(FIELDS)]
            w[0] = jnp.where(there, w[0], 1.0)
            plus = side_term(w, f)
            minus = side_term([trace(fields_ref, c, v, f) for v in range(FIELDS)], f)
            for v in range(FIELDS):
                add_on_face(part_ref, c, v, f, 3.0 * (jnp.where(there, plus[v], 0.0) - minus[v]))


def ghost_terms(ghost, ask):
    face = (ask >> 9) ^ 1
    axis = face >> 1
    sign = jnp.where((face & 1) == 1, 3.0, -3.0)
    w = [ghost[16 * v : 16 * v + 16] for v in range(FIELDS)]
    u = [w[1 + c] / w[0] for c in range(3)]
    p = pressure_of(w, u)

    def along(x):
        return jnp.where(axis == 0, x[0], jnp.where(axis == 1, x[1], x[2]))

    un = along(u)
    flux = [along(w[1:4])]
    for c in range(3):
        flux.append(w[1 + c] * un + jnp.where(axis == c, p, 0.0))
    flux.append((w[4] + p) * un)
    return jnp.concatenate([sign * flux[v] - (3.0 * SPEED) * w[v] for v in range(FIELDS)], axis=0)


def ghost_rows(ghosts, ask_ref):
    parts = [split(ghost_terms(g, ask_ref[t])) for t, g in enumerate(ghosts)]
    high = jnp.concatenate([p[0] for p in parts], axis=1)
    low = jnp.concatenate([p[1] for p in parts], axis=1)
    return jnp.concatenate([high, low], axis=0)


def add_ghosts(sum_ref, lhs, hot_of, blocks=range(BLOCKS)):
    for f in range(6):
        both = dot(lhs, hot_of(f))
        for i, c in enumerate(blocks):
            spot = slice(128 * i, 128 * i + 128)
            term = both[0:TRACE_ROWS, spot] + both[TRACE_ROWS:, spot]
            for v in range(FIELDS):
                add_on_face(sum_ref, c, v, f, term[16 * v : 16 * v + 16])


def direct_kernel(part_ref, far_ref, ask_ref, a_ref, b_ref, sib_ref, sum_ref):
    lhs = ghost_rows([sib_ref[0], a_ref[2], a_ref[0], b_ref[1], b_ref[0]], ask_ref)
    sum_ref[...] = part_ref[...]
    add_ghosts(sum_ref, lhs, lambda f: one_hot_rows(5 * CAP, far_ref[f : f + 1, :] - 3 * CAP))


def metric_of(start_ref, c):
    return jnp.where(start_ref[c, ROWS : ROWS + 1, :] > 0.5, 2.0, 1.0)


def second_kernel(start_ref, part_ref, rest_ref, own_ask_ref, post_ref, ask_ref, hot_ref,
                  section_ref, swap_ref, sum_ref, got_ref):
    lhs = ghost_rows([post_ref[1], post_ref[0], post_ref[2]], own_ask_ref)
    sum_ref[...] = part_ref[...]
    add_ghosts(sum_ref, lhs, lambda f: rest_ref[f])
    for c in range(BLOCKS):
        section_ref[c] = start_ref[c, 0:ROWS, :] - (DT * metric_of(start_ref, c)) * sum_ref[c]
    reply(wide(section_ref, ROWS), ask_ref[4:8, :], hot_ref[...], got_ref, [swap_ref.at[t] for t in range(4)])


def last_kernel(start_ref, section_ref, part_ref, rest_ref, own_ask_ref, post_ref,
                state_hbm, rate_hbm, sum_ref, state_ref, rate_ref, sems):
    lhs = ghost_rows([post_ref[1], post_ref[0], post_ref[2]], own_ask_ref)
    sum_ref[...] = part_ref[...]
    copies = []
    for half in range(2):
        pair = (2 * half, 2 * half + 1)
        add_ghosts(sum_ref, lhs, lambda f: rest_ref[f, :, HALF * half : HALF * half + HALF], pair)
        for c in pair:
            rate = -metric_of(start_ref, c) * sum_ref[c]
            rate_ref[c] = rate
            state_ref[c] = 0.5 * start_ref[c, 0:ROWS, :] + 0.5 * (section_ref[c] + DT * rate)
            for i, (src, dst) in enumerate(((rate_ref, rate_hbm), (state_ref, state_hbm))):
                copy = pltpu.make_async_copy(src.at[c], dst.at[:, pl.ds(128 * c, 128)], sems.at[i, c])
                copy.start()
                copies.append(copy)
    for copy in copies:
        copy.wait()


VM = pl.BlockSpec(memory_space=pltpu.VMEM)
SM = pl.BlockSpec(memory_space=pltpu.SMEM)
HB = pl.BlockSpec(memory_space=pltpu.HBM)


def call(kernel, outs, args, specs=None, scratch=(), flops=10**6, outs_in=None):
    return pl.pallas_call(
        kernel,
        out_shape=[jax.ShapeDtypeStruct(s, d) for s, d in outs],
        in_specs=specs or [VM] * len(args),
        out_specs=[outs_in or VM] * len(outs),
        scratch_shapes=[pltpu.VMEM(*s) if isinstance(s, tuple) else s for s in scratch],
        compiler_params=pltpu.CompilerParams(vmem_limit_bytes=24 * 2**20),
        cost_estimate=pl.CostEstimate(flops=flops, bytes_accessed=2**20, transcendentals=0),
    )(*args)


def swap_cores(x):
    n = lax.axis_size(AXES)
    return lax.ppermute(x, AXES, [(i, i ^ 1) for i in range(n)])


def to_next_chip(x):
    n = lax.axis_size(AXES)
    return lax.ppermute(x, AXES, [(i, (i + 1) % n) for i in range(1, n, 2)])


def to_prior_chip(x):
    n = lax.axis_size(AXES)
    return lax.ppermute(x, AXES, [(i, (i - 1) % n) for i in range(0, n, 2)])


def outward(x, by):
    n = lax.axis_size(AXES)
    return lax.ppermute(x, AXES, [(i, (i + (by if i % 2 == 0 else -by)) % n) for i in range(n)])


def outward_pair(own, got):
    b = outward(jnp.concatenate([own[1], got[2:4]], axis=0), 4)
    a = outward(jnp.concatenate([own[0], got[0:2]], axis=0), 2)
    return a, b


def swap_back(a, b):
    return swap_cores(jnp.concatenate([a[1:2], a[3:4], b[2:3]], axis=0))


def body(state_old, level_old, morton_old, neighbours):
    me = lax.axis_index(AXES).astype(I32).reshape(1)
    inputs = [
        pltpu.with_memory_space_constraint(x, pltpu.HBM)
        for x in (
            neighbours,
            state_old.reshape(ROWS, OLD_CAP),
            level_old.reshape(1, OLD_CAP),
            morton_old.reshape(1, OLD_CAP),
        )
    ]
    own_ask, swap_ask, near, far, state, level, morton = call(
        open_kernel,
        [
            ((3, 1, CAP), I32),
            ((5, 1, CAP), I32),
            ((6, NEW_DEV), I32),
            ((6, NEW_DEV), I32),
            ((ROWS, OLD_CAP), F32),
            ((1, OLD_CAP), I32),
            ((1, OLD_CAP), I32),
        ],
        (me, *inputs),
        [SM, HB, HB, HB, HB],
        [((6, NEW_DEV), I32), pltpu.SemaphoreType.DMA((4,))],
    )
    got = swap_cores(swap_ask)
    relay = [SM, VM, VM, VM]
    moved = ((MOVED_ROWS, HALF), F32)
    (to_far,) = call(far_kernel, [moved], (me, state, level, morton), relay)
    from_prior = to_next_chip(to_far)
    got, to_far = lax.optimization_barrier((got, to_far))
    a, b = outward_pair((own_ask[0:2], own_ask[2:3]), got[1:5])
    from_next = to_prior_chip(to_far)
    a, morton = lax.optimization_barrier((a, morton))
    (to_sib,) = call(sib_kernel, [moved], (me, state, level, morton), relay, flops=10**9)
    from_sib = swap_cores(to_sib)
    (home,) = call(home_kernel, [((BLOCKS, MOVED_ROWS, 128), F32)], (me, state, level, morton), relay)
    post = swap_back(a, b)
    asked = jnp.concatenate(
        [post[1], post[0], post[2], got[0], a[2], a[0], b[1], b[0]], axis=0
    )

    rest_hot, reply_hot = call(
        hot_kernel,
        [((6, 3 * CAP, NEW_DEV), BF16), ((NEW_DEV, 4 * CAP), BF16)],
        (far, asked),
        flops=10**9,
    )
    swapped = ((4, TRACE_ROWS, CAP), F32)
    got_scratch = ((4, ROWS, CAP), F32)
    blocks = ((BLOCKS, ROWS, 128), F32)
    table = jnp.asarray(stacked_table())

    def neighbours_of(fields, swap):
        got = swap_cores(swap)
        *own, sib = call(
            own_kernel,
            [((2, TRACE_ROWS, CAP), F32), ((1, TRACE_ROWS, CAP), F32), ((1, TRACE_ROWS, CAP), F32)],
            (fields, asked),
            None,
            [got_scratch],
            flops=10**9,
        )
        a, b = outward_pair(own, got)
        (part,) = call(
            near_kernel,
            [blocks],
            (table, fields, near),
            None,
            [((FIELDS, 3 * DOFS, NEW_DEV), BF16)] * 2,
            flops=10**9,
        )
        sib, part = lax.optimization_barrier((sib, part))
        sib = swap_cores(sib)
        a, b, part = lax.optimization_barrier((a, b, part))
        post = swap_back(a, b)
        (part,) = call(direct_kernel, [blocks], (part, far, swap_ask, a, b, sib), flops=10**9)
        return part, rest_hot, own_ask, post

    start, swap = call(
        first_kernel,
        [((BLOCKS, MOVED_ROWS, 128), F32), swapped],
        (me, home, from_prior, from_next, from_sib, asked, reply_hot),
        [SM, VM, VM, VM, VM, VM, VM],
        [got_scratch],
    )
    ghosts = neighbours_of(start, swap)
    section, swap = call(
        second_kernel,
        [blocks, swapped],
        (start, *ghosts, asked, reply_hot),
        None,
        [blocks, got_scratch],
    )
    ghosts = neighbours_of(section, swap)
    new_state, rate = call(
        last_kernel,
        [((ROWS, NEW_DEV), F32)] * 2,
        (start, section, *ghosts),
        None,
        [blocks, blocks, blocks, pltpu.SemaphoreType.DMA((2, BLOCKS))],
        outs_in=HB,
    )
    shape = (FIELDS, DOFS, NEW_DEV)
    return new_state.reshape(shape), rate.reshape(shape)


def solution(mesh):
    wide = P(None, None, AXES)
    return jax.shard_map(
        body,
        mesh=mesh,
        in_specs=(wide, P(AXES), P(AXES), P(None, AXES)),
        out_specs=(wide, wide),
        check_vma=False,
    )
```

```python
import jax
import jax.numpy as jnp
import numpy as np
from jax import lax
from jax.experimental import pallas as pl
from jax.experimental.pallas import tpu as pltpu
from jax.sharding import PartitionSpec as P

FIELDS = 5
DOFS = 64
ROWS = FIELDS * DOFS
NEW_DEV = 512
HALF = NEW_DEV // 2
OLD_CAP = 1024
CAP = 128
TRACE_ROWS = FIELDS * 16
MOVED_ROWS = ROWS + 8
BLOCKS = NEW_DEV // 128

HEAT = 1.4
SPEED = 4.0
DT = 0.0002
AXES = ("px", "py")
F32 = jnp.float32
BF16 = jnp.bfloat16
I32 = jnp.int32

STEPS = (2, 3, 4, 1, -1, -2, -3, -4)


def derivative_table():
    points = np.array([-1.0, -1.0 / np.sqrt(5.0), 1.0 / np.sqrt(5.0), 1.0])
    weights = np.array(
        [1.0 / np.prod([points[c] - points[o] for o in range(4) if o != c]) for c in range(4)]
    )
    table = np.zeros((4, 4))
    for r in range(4):
        for c in range(4):
            if r != c:
                table[r, c] = weights[c] / weights[r] / (points[r] - points[c])
        table[r, r] = -np.sum(table[r])
    return table


def stacked_table():
    d = derivative_table().astype(np.float32).astype(np.float64)
    one = np.eye(4)
    full = np.concatenate(
        [
            np.kron(np.kron(d, one), one),
            np.kron(np.kron(one, d), one),
            np.kron(np.kron(one, one), d),
        ],
        axis=1,
    ).astype(np.float32)
    high = full.astype(jnp.bfloat16)
    low = (full - high.astype(np.float32)).astype(jnp.bfloat16)
    return np.concatenate([high, low], axis=0)


def split(x):
    high = x.astype(BF16)
    low = (x - high.astype(F32)).astype(BF16)
    return high, low


def dot(a, b):
    return lax.dot_general(a, b, (((1,), (0,)), ((), ())), preferred_element_type=F32)


def dot_nt(a, b):
    return lax.dot_general(a, b, (((1,), (1,)), ((), ())), preferred_element_type=F32)


def one_hot_rows(size, row):
    spots = lax.broadcasted_iota(I32, (size, row.shape[1]), 0)
    return jnp.where(spots == row, 1.0, 0.0).astype(BF16)


def relay_slots(me, morton):
    occupied = morton >= 0
    owner = morton >> 9
    slot = morton & (NEW_DEV - 1)
    gap = (owner - me) & 127
    even = (me & 1) == 0
    to_next = occupied & (gap == 1)
    to_prior = occupied & (gap == 127)
    home = jnp.where(occupied & (gap == 0), slot, -1)
    ahead = jnp.where(to_next, slot, -1)
    behind = jnp.where(to_prior, slot - HALF, -1)
    sib = jnp.where(even, ahead, behind)
    far = jnp.where(even, behind, ahead)
    return sib, far, home


def store_moved(ref, got):
    ref[0:ROWS, :] = got[0:ROWS] + got[ROWS : 2 * ROWS]
    ref[ROWS : ROWS + 8, :] = got[2 * ROWS : 2 * ROWS + 8]


def relay_rows(state, level):
    high, low = split(state)
    lev = jnp.broadcast_to(level.astype(F32), (16, OLD_CAP)).astype(BF16)
    return jnp.concatenate([high, low, lev], axis=0)


def open_kernel(me_ref, links_hbm, state_hbm, level_hbm, morton_hbm, own_ask_ref, swap_ask_ref, near_ref, far_ref,
                state_ref, level_ref, morton_ref, links_ref, sems):
    pairs = ((links_hbm, links_ref), (morton_hbm, morton_ref), (level_hbm, level_ref), (state_hbm, state_ref))
    copies = [pltpu.make_async_copy(src, dst, sems.at[i]) for i, (src, dst) in enumerate(pairs)]
    for copy in copies:
        copy.start()
    copies[0].wait()
    ask = requests(me_ref[0], links_ref[...], near_ref, far_ref)
    for t in range(8):
        if t < 3:
            own_ask_ref[t] = ask[t : t + 1]
        else:
            swap_ask_ref[t - 3] = ask[t : t + 1]
    for copy in copies[1:]:
        copy.wait()


def far_kernel(me_ref, state_ref, level_ref, morton_ref, far_ref):
    _, far, _ = relay_slots(me_ref[0], morton_ref[...])
    lhs = relay_rows(state_ref[...], level_ref[...])
    store_moved(far_ref, dot_nt(lhs, one_hot_rows(HALF, far)))


def sib_kernel(me_ref, state_ref, level_ref, morton_ref, sib_ref):
    sib, _, _ = relay_slots(me_ref[0], morton_ref[...])
    lhs = relay_rows(state_ref[...], level_ref[...])
    store_moved(sib_ref, dot_nt(lhs, one_hot_rows(HALF, sib)))


def home_kernel(me_ref, state_ref, level_ref, morton_ref, home_ref):
    _, _, home = relay_slots(me_ref[0], morton_ref[...])
    got = dot_nt(relay_rows(state_ref[...], level_ref[...]), one_hot_rows(NEW_DEV, home))
    for c in range(BLOCKS):
        store_moved(home_ref.at[c], got[:, 128 * c : 128 * c + 128])


def requests(me, links, near_ref, far_ref):
    owner = links >> 9
    slot = links & (NEW_DEV - 1)
    gap = ((owner - me + 192) & 127) - 64
    gap = jnp.where((me & 1) == 0, gap, -gap)
    near_ref[...] = jnp.where(gap == 0, slot, -1)
    b = lax.broadcasted_iota(I32, (8, NEW_DEV), 0)
    step_of = jnp.where(b < 3, b + 2, jnp.where(b == 3, 1, 3 - b))
    masks = [jnp.where(gap[f : f + 1, :] == step_of, 1.0, 0.0) for f in range(6)]
    k = lax.broadcasted_iota(I32, (NEW_DEV, NEW_DEV), 0)
    j = lax.broadcasted_iota(I32, (NEW_DEV, NEW_DEV), 1)
    upper = jnp.where(k <= j, 1.0, 0.0).astype(BF16)
    counts = dot(jnp.concatenate(masks, axis=0).astype(BF16), upper)
    offset = jnp.full((8, 1), -1.0, F32)
    bf = b.astype(F32)
    total = jnp.zeros((16, CAP), F32)
    for f in range(6):
        run = counts[8 * f : 8 * f + 8, :]
        here = gap[f : f + 1, :] != 0
        rank = jnp.sum(masks[f] * (run + offset), axis=0, keepdims=True)
        bucket = jnp.sum(masks[f] * bf, axis=0, keepdims=True)
        offset = offset + run[:, NEW_DEV - 1 : NEW_DEV]
        rank = jnp.where(here, rank.astype(I32), -1)
        far_ref[f : f + 1, :] = jnp.where(here, bucket.astype(I32) * CAP + rank, -1)
        s = slot[f : f + 1, :]
        low = (s & 255).astype(F32)
        high = ((s >> 8) + 2 * (f ^ 1)).astype(F32)
        lhs = jnp.concatenate([masks[f] * low, masks[f] * high], axis=0).astype(BF16)
        total = total + dot_nt(lhs, one_hot_rows(CAP, rank))
    return total[0:8].astype(I32) + 256 * total[8:16].astype(I32)


def lower_half(shape):
    return lax.broadcasted_iota(I32, shape, 0) < 4


def trace(ref, c, v, f):
    a, s = f // 2, f % 2
    at = v * DOFS
    if a == 0:
        return ref[c, at + 48 * s : at + 48 * s + 16, :]
    if a == 1:
        out = []
        for h in range(2):
            r = at + 32 * h + 8 * s
            x = ref[c, r : r + 8, :]
            y = ref[c, r + 16 : r + 24, :]
            low = lower_half(x.shape)
            if s == 0:
                out.append(jnp.where(low, x, pltpu.roll(y, 4, 0)))
            else:
                out.append(jnp.where(low, pltpu.roll(x, 4, 0), y))
        return jnp.concatenate(out, axis=0)
    return ref[c, pl.ds(at + 3 * s, 16, stride=4), :]


def add_on_face(ref, c, v, f, x):
    a, s = f // 2, f % 2
    at = v * DOFS
    if a == 0:
        ref[c, at + 48 * s : at + 48 * s + 16, :] += x
    elif a == 1:
        for h in range(2):
            y = x[8 * h : 8 * h + 8, :]
            low = lower_half(y.shape)
            keep = low if s == 0 else ~low
            turned = pltpu.roll(y, 4, 0)
            first, second = (y, turned) if s == 0 else (turned, y)
            r = at + 32 * h + 8 * s
            ref[c, r : r + 8, :] += jnp.where(keep, first, 0.0)
            ref[c, r + 16 : r + 24, :] += jnp.where(keep, second, 0.0)
    else:
        spot = (c, pl.ds(at + 3 * s, 16, stride=4), slice(None))
        ref[spot] = ref[spot] + x


def wide(ref, rows):
    return jnp.concatenate([ref[c, 0:rows, :] for c in range(ref.shape[0])], axis=1)


def pressure_of(w, u):
    return (HEAT - 1.0) * (w[4] - 0.5 * (w[1] * u[0] + w[2] * u[1] + w[3] * u[2]))


def axis_flux(w, u, p, a):
    un = u[a]
    out = [w[1 + a]]
    for c in range(3):
        m = w[1 + c] * un
        out.append(m + p if c == a else m)
    out.append((w[4] + p) * un)
    return out


def side_term(w, f):
    sign = 1.0 if f % 2 else -1.0
    u = [w[1 + c] / w[0] for c in range(3)]
    p = pressure_of(w, u)
    flux = axis_flux(w, u, p, f // 2)
    return [(sign * flux[v]) - SPEED * w[v] for v in range(FIELDS)]


def asked_code(ask):
    return jnp.concatenate([ask[t : t + 1, :] for t in range(ask.shape[0])], axis=1)


def reply(fields, ask, hot, got_ref, outs):
    chunks = ask.shape[0]
    high, low = split(fields)
    both = dot(jnp.concatenate([high, low], axis=0), hot)
    for t in range(chunks):
        spot = slice(CAP * t, CAP * t + CAP)
        got_ref[t] = both[0:ROWS, spot] + both[ROWS:, spot]
    for t in range(chunks):
        face = ask[t : t + 1, :] >> 9
        for v in range(FIELDS):
            x = trace(got_ref, t, v, 0)
            for f in range(1, 6):
                x = jnp.where(face == f, trace(got_ref, t, v, f), x)
            outs[t][16 * v : 16 * v + 16, :] = x


def hot_kernel(far_ref, ask_ref, rest_ref, reply_ref):
    for f in range(6):
        rest_ref[f] = one_hot_rows(3 * CAP, far_ref[f : f + 1, :])
    reply_ref[...] = one_hot_rows(NEW_DEV, asked_code(ask_ref[4:8, :]) & (NEW_DEV - 1))


def own_kernel(fields_ref, ask_ref, a_ref, b_ref, sib_ref, got_ref):
    ask = ask_ref[0:4, :]
    hot = one_hot_rows(NEW_DEV, asked_code(ask) & (NEW_DEV - 1))
    outs = [a_ref.at[0], a_ref.at[1], b_ref.at[0], sib_ref.at[0]]
    reply(wide(fields_ref, ROWS), ask, hot, got_ref, outs)


def first_kernel(me_ref, home_ref, far_ref, sib_ref, ask_ref, hot_ref, start_ref, swap_ref, got_ref):
    even = (me_ref[0] & 1) == 0
    for c in range(2):
        spot = slice(128 * c, 128 * c + 128)
        sib = sib_ref[:, spot]
        far = far_ref[:, spot]
        start_ref[c] = home_ref[c] + jnp.where(even, far, sib)
        start_ref[c + 2] = home_ref[c + 2] + jnp.where(even, sib, far)
    reply(wide(start_ref, ROWS), ask_ref[4:8, :], hot_ref[...], got_ref, [swap_ref.at[t] for t in range(4)])


def near_kernel(table_ref, fields_ref, near_ref, part_ref, high_ref, low_ref):
    for c in range(BLOCKS):
        spot = slice(128 * c, 128 * c + 128)
        w = [fields_ref[c, DOFS * v : DOFS * v + DOFS, :] for v in range(FIELDS)]
        u = [w[1 + i] / w[0] for i in range(3)]
        p = pressure_of(w, u)
        for a in range(3):
            flux = axis_flux(w, u, p, a)
            for v in range(FIELDS):
                high, low = split(flux[v])
                high_ref[v, DOFS * a : DOFS * a + DOFS, spot] = high
                low_ref[v, DOFS * a : DOFS * a + DOFS, spot] = low
    table = table_ref[...]
    for v in range(FIELDS):
        x = dot(table, high_ref[v])
        x = x[0:DOFS] + x[DOFS:] + dot(table[0:DOFS], low_ref[v])
        for c in range(BLOCKS):
            part_ref[c, DOFS * v : DOFS * v + DOFS, :] = x[:, 128 * c : 128 * c + 128]
    for f in range(6):
        hot = one_hot_rows(NEW_DEV, near_ref[f : f + 1, :])
        across = jnp.concatenate(
            [
                jnp.concatenate([trace(fields_ref, c, v, f ^ 1) for v in range(FIELDS)], axis=0)
                for c in range(BLOCKS)
            ],
            axis=1,
        )
        high, low = split(across)
        both = dot(jnp.concatenate([high, low], axis=0), hot)
        for c in range(BLOCKS):
            spot = slice(128 * c, 128 * c + 128)
            outer = both[0:TRACE_ROWS, spot] + both[TRACE_ROWS:, spot]
            there = near_ref[f : f + 1, spot] >= 0
            w = [outer[16 * v : 16 * v + 16] for v in range(FIELDS)]
            w[0] = jnp.where(there, w[0], 1.0)
            plus = side_term(w, f)
            minus = side_term([trace(fields_ref, c, v, f) for v in range(FIELDS)], f)
            for v in range(FIELDS):
                add_on_face(part_ref, c, v, f, 3.0 * (jnp.where(there, plus[v], 0.0) - minus[v]))


def ghost_terms(ghost, ask):
    face = (ask >> 9) ^ 1
    axis = face >> 1
    sign = jnp.where((face & 1) == 1, 3.0, -3.0)
    w = [ghost[16 * v : 16 * v + 16] for v in range(FIELDS)]
    u = [w[1 + c] / w[0] for c in range(3)]
    p = pressure_of(w, u)

    def along(x):
        return jnp.where(axis == 0, x[0], jnp.where(axis == 1, x[1], x[2]))

    un = along(u)
    flux = [along(w[1:4])]
    for c in range(3):
        flux.append(w[1 + c] * un + jnp.where(axis == c, p, 0.0))
    flux.append((w[4] + p) * un)
    return jnp.concatenate([sign * flux[v] - (3.0 * SPEED) * w[v] for v in range(FIELDS)], axis=0)


def ghost_rows(ghosts, ask_ref):
    parts = [split(ghost_terms(g, ask_ref[t])) for t, g in enumerate(ghosts)]
    high = jnp.concatenate([p[0] for p in parts], axis=1)
    low = jnp.concatenate([p[1] for p in parts], axis=1)
    return jnp.concatenate([high, low], axis=0)


def add_ghosts(sum_ref, lhs, hot_of, blocks=range(BLOCKS)):
    for f in range(6):
        both = dot(lhs, hot_of(f))
        for i, c in enumerate(blocks):
            spot = slice(128 * i, 128 * i + 128)
            term = both[0:TRACE_ROWS, spot] + both[TRACE_ROWS:, spot]
            for v in range(FIELDS):
                add_on_face(sum_ref, c, v, f, term[16 * v : 16 * v + 16])


def direct_kernel(part_ref, far_ref, ask_ref, own_ref, got_ref, b_ref, sib_ref, sum_ref):
    lhs = ghost_rows([sib_ref[0], got_ref[0], own_ref[0], b_ref[1], b_ref[0]], ask_ref)
    sum_ref[...] = part_ref[...]
    add_ghosts(sum_ref, lhs, lambda f: one_hot_rows(5 * CAP, far_ref[f : f + 1, :] - 3 * CAP))


def metric_of(start_ref, c):
    return jnp.where(start_ref[c, ROWS : ROWS + 1, :] > 0.5, 2.0, 1.0)


def second_kernel(start_ref, part_ref, rest_ref, own_ask_ref, post_ref, ask_ref, hot_ref,
                  section_ref, swap_ref, sum_ref, got_ref):
    lhs = ghost_rows([post_ref[1], post_ref[0], post_ref[2]], own_ask_ref)
    sum_ref[...] = part_ref[...]
    add_ghosts(sum_ref, lhs, lambda f: rest_ref[f])
    for c in range(BLOCKS):
        section_ref[c] = start_ref[c, 0:ROWS, :] - (DT * metric_of(start_ref, c)) * sum_ref[c]
    reply(wide(section_ref, ROWS), ask_ref[4:8, :], hot_ref[...], got_ref, [swap_ref.at[t] for t in range(4)])


def last_kernel(start_ref, section_ref, part_ref, rest_ref, own_ask_ref, post_ref,
                state_hbm, rate_hbm, sum_ref, state_ref, rate_ref, sems):
    lhs = ghost_rows([post_ref[1], post_ref[0], post_ref[2]], own_ask_ref)
    sum_ref[...] = part_ref[...]
    copies = []
    for half in range(2):
        pair = (2 * half, 2 * half + 1)
        add_ghosts(sum_ref, lhs, lambda f: rest_ref[f, :, HALF * half : HALF * half + HALF], pair)
        for c in pair:
            rate = -metric_of(start_ref, c) * sum_ref[c]
            rate_ref[c] = rate
            state_ref[c] = 0.5 * start_ref[c, 0:ROWS, :] + 0.5 * (section_ref[c] + DT * rate)
            for i, (src, dst) in enumerate(((rate_ref, rate_hbm), (state_ref, state_hbm))):
                copy = pltpu.make_async_copy(src.at[c], dst.at[:, pl.ds(128 * c, 128)], sems.at[i, c])
                copy.start()
                copies.append(copy)
    for copy in copies:
        copy.wait()


VM = pl.BlockSpec(memory_space=pltpu.VMEM)
SM = pl.BlockSpec(memory_space=pltpu.SMEM)
HB = pl.BlockSpec(memory_space=pltpu.HBM)


def call(kernel, outs, args, specs=None, scratch=(), flops=10**6, outs_in=None):
    return pl.pallas_call(
        kernel,
        out_shape=[jax.ShapeDtypeStruct(s, d) for s, d in outs],
        in_specs=specs or [VM] * len(args),
        out_specs=[outs_in or VM] * len(outs),
        scratch_shapes=[pltpu.VMEM(*s) if isinstance(s, tuple) else s for s in scratch],
        compiler_params=pltpu.CompilerParams(vmem_limit_bytes=24 * 2**20),
        cost_estimate=pl.CostEstimate(flops=flops, bytes_accessed=2**20, transcendentals=0),
    )(*args)


def swap_cores(x):
    n = lax.axis_size(AXES)
    return lax.ppermute(x, AXES, [(i, i ^ 1) for i in range(n)])


def swap_chips(x):
    n = lax.axis_size(AXES)
    return lax.ppermute(x, AXES, [(i, (i + (1 if i % 2 else -1)) % n) for i in range(n)])


def outward(x, by):
    n = lax.axis_size(AXES)
    return lax.ppermute(x, AXES, [(i, (i + (by if i % 2 == 0 else -by)) % n) for i in range(n)])


def outward_pair(own, got):
    b = outward(jnp.concatenate([own[1], got[2:4]], axis=0), 4)
    a = outward(jnp.concatenate([own[0], got[0:2]], axis=0), 2)
    return a, b


def swap_back(a, b):
    return swap_cores(jnp.concatenate([a[1:2], a[3:4], b[2:3]], axis=0))


def body(state_old, level_old, morton_old, neighbours):
    me = lax.axis_index(AXES).astype(I32).reshape(1)
    inputs = [
        pltpu.with_memory_space_constraint(x, pltpu.HBM)
        for x in (
            neighbours,
            state_old.reshape(ROWS, OLD_CAP),
            level_old.reshape(1, OLD_CAP),
            morton_old.reshape(1, OLD_CAP),
        )
    ]
    own_ask, swap_ask, near, far, state, level, morton = call(
        open_kernel,
        [
            ((3, 1, CAP), I32),
            ((5, 1, CAP), I32),
            ((6, NEW_DEV), I32),
            ((6, NEW_DEV), I32),
            ((ROWS, OLD_CAP), F32),
            ((1, OLD_CAP), I32),
            ((1, OLD_CAP), I32),
        ],
        (me, *inputs),
        [SM, HB, HB, HB, HB],
        [((6, NEW_DEV), I32), pltpu.SemaphoreType.DMA((4,))],
    )
    got = swap_cores(swap_ask)
    relay = [SM, VM, VM, VM]
    moved = ((MOVED_ROWS, HALF), F32)
    (to_far,) = call(far_kernel, [moved], (me, state, level, morton), relay)
    got, to_far = lax.optimization_barrier((got, to_far))
    a, b = outward_pair((own_ask[0:2], own_ask[2:3]), got[1:5])
    from_far = swap_chips(to_far)
    a, morton = lax.optimization_barrier((a, morton))
    (to_sib,) = call(sib_kernel, [moved], (me, state, level, morton), relay, flops=10**9)
    from_sib = swap_cores(to_sib)
    (home,) = call(home_kernel, [((BLOCKS, MOVED_ROWS, 128), F32)], (me, state, level, morton), relay)
    post = swap_back(a, b)
    asked = jnp.concatenate(
        [post[1], post[0], post[2], got[0], a[2], a[0], b[1], b[0]], axis=0
    )

    rest_hot, reply_hot = call(
        hot_kernel,
        [((6, 3 * CAP, NEW_DEV), BF16), ((NEW_DEV, 4 * CAP), BF16)],
        (far, asked),
        flops=10**9,
    )
    swapped = ((4, TRACE_ROWS, CAP), F32)
    got_scratch = ((4, ROWS, CAP), F32)
    blocks = ((BLOCKS, ROWS, 128), F32)
    table = jnp.asarray(stacked_table())

    def neighbours_of(fields, swap):
        got = swap_cores(swap)
        *own, sib = call(
            own_kernel,
            [((2, TRACE_ROWS, CAP), F32), ((1, TRACE_ROWS, CAP), F32), ((1, TRACE_ROWS, CAP), F32)],
            (fields, asked),
            None,
            [got_scratch],
            flops=10**9,
        )
        a_own = outward(own[0], 2)
        b = outward(jnp.concatenate([own[1], got[2:4]], axis=0), 4)
        a_got = outward(got[0:2], 2)
        (part,) = call(
            near_kernel,
            [blocks],
            (table, fields, near),
            None,
            [((FIELDS, 3 * DOFS, NEW_DEV), BF16)] * 2,
            flops=10**9,
        )
        sib, part = lax.optimization_barrier((sib, part))
        sib = swap_cores(sib)
        a_own, a_got, b, part = lax.optimization_barrier((a_own, a_got, b, part))
        post = swap_cores(jnp.concatenate([a_own[1:2], a_got[1:2], b[2:3]], axis=0))
        (part,) = call(direct_kernel, [blocks], (part, far, swap_ask, a_own, a_got, b, sib), flops=10**9)
        return part, rest_hot, own_ask, post

    start, swap = call(
        first_kernel,
        [((BLOCKS, MOVED_ROWS, 128), F32), swapped],
        (me, home, from_far, from_sib, asked, reply_hot),
        [SM, VM, VM, VM, VM, VM],
        [got_scratch],
    )
    ghosts = neighbours_of(start, swap)
    section, swap = call(
        second_kernel,
        [blocks, swapped],
        (start, *ghosts, asked, reply_hot),
        None,
        [blocks, got_scratch],
    )
    ghosts = neighbours_of(section, swap)
    new_state, rate = call(
        last_kernel,
        [((ROWS, NEW_DEV), F32)] * 2,
        (start, section, *ghosts),
        None,
        [blocks, blocks, blocks, pltpu.SemaphoreType.DMA((2, BLOCKS))],
        outs_in=HB,
    )
    shape = (FIELDS, DOFS, NEW_DEV)
    return new_state.reshape(shape), rate.reshape(shape)


def solution(mesh):
    wide = P(None, None, AXES)
    return jax.shard_map(
        body,
        mesh=mesh,
        in_specs=(wide, P(AXES), P(AXES), P(None, AXES)),
        out_specs=(wide, wide),
        check_vma=False,
    )
```

```python
import jax
import jax.numpy as jnp
import numpy as np
from jax import lax
from jax.experimental import pallas as pl
from jax.experimental.pallas import tpu as pltpu
from jax.sharding import PartitionSpec as P

FIELDS = 5
DOFS = 64
ROWS = FIELDS * DOFS
NEW_DEV = 512
HALF = NEW_DEV // 2
OLD_CAP = 1024
CAP = 128
TRACE_ROWS = FIELDS * 16
MOVED_ROWS = ROWS + 8
BLOCKS = NEW_DEV // 128

HEAT = 1.4
SPEED = 4.0
DT = 0.0002
AXES = ("px", "py")
F32 = jnp.float32
BF16 = jnp.bfloat16
I32 = jnp.int32

STEPS = (2, 3, 4, 1, -1, -2, -3, -4)


def derivative_table():
    points = np.array([-1.0, -1.0 / np.sqrt(5.0), 1.0 / np.sqrt(5.0), 1.0])
    weights = np.array(
        [1.0 / np.prod([points[c] - points[o] for o in range(4) if o != c]) for c in range(4)]
    )
    table = np.zeros((4, 4))
    for r in range(4):
        for c in range(4):
            if r != c:
                table[r, c] = weights[c] / weights[r] / (points[r] - points[c])
        table[r, r] = -np.sum(table[r])
    return table


def stacked_table():
    d = derivative_table().astype(np.float32).astype(np.float64)
    one = np.eye(4)
    full = np.concatenate(
        [
            np.kron(np.kron(d, one), one),
            np.kron(np.kron(one, d), one),
            np.kron(np.kron(one, one), d),
        ],
        axis=1,
    ).astype(np.float32)
    high = full.astype(jnp.bfloat16)
    low = (full - high.astype(np.float32)).astype(jnp.bfloat16)
    return np.concatenate([high, low], axis=0)


def split(x):
    high = x.astype(BF16)
    low = (x - high.astype(F32)).astype(BF16)
    return high, low


def dot(a, b):
    return lax.dot_general(a, b, (((1,), (0,)), ((), ())), preferred_element_type=F32)


def dot_nt(a, b):
    return lax.dot_general(a, b, (((1,), (1,)), ((), ())), preferred_element_type=F32)


def one_hot_rows(size, row):
    spots = lax.broadcasted_iota(I32, (size, row.shape[1]), 0)
    return jnp.where(spots == row, 1.0, 0.0).astype(BF16)


def relay_slots(me, morton):
    occupied = morton >= 0
    owner = morton >> 9
    slot = morton & (NEW_DEV - 1)
    gap = (owner - me) & 127
    even = (me & 1) == 0
    to_next = occupied & (gap == 1)
    to_prior = occupied & (gap == 127)
    home = jnp.where(occupied & (gap == 0), slot, -1)
    ahead = jnp.where(to_next, slot, -1)
    behind = jnp.where(to_prior, slot - HALF, -1)
    sib = jnp.where(even, ahead, behind)
    far = jnp.where(even, behind, ahead)
    return sib, far, home


def store_moved(ref, got):
    ref[0:ROWS, :] = got[0:ROWS] + got[ROWS : 2 * ROWS]
    ref[ROWS : ROWS + 8, :] = got[2 * ROWS : 2 * ROWS + 8]


def relay_rows(state, level):
    high, low = split(state)
    lev = jnp.broadcast_to(level.astype(F32), (16, OLD_CAP)).astype(BF16)
    return jnp.concatenate([high, low, lev], axis=0)


def open_kernel(me_ref, links_hbm, state_hbm, level_hbm, morton_hbm, own_ask_ref, swap_ask_ref, near_ref, far_ref,
                state_ref, level_ref, morton_ref, links_ref, sems):
    pairs = ((links_hbm, links_ref), (morton_hbm, morton_ref), (level_hbm, level_ref), (state_hbm, state_ref))
    copies = [pltpu.make_async_copy(src, dst, sems.at[i]) for i, (src, dst) in enumerate(pairs)]
    for copy in copies:
        copy.start()
    copies[0].wait()
    ask = requests(me_ref[0], links_ref[...], near_ref, far_ref)
    for t in range(8):
        if t < 3:
            own_ask_ref[t] = ask[t : t + 1]
        else:
            swap_ask_ref[t - 3] = ask[t : t + 1]
    for copy in copies[1:]:
        copy.wait()


def far_kernel(me_ref, state_ref, level_ref, morton_ref, far_ref):
    _, far, _ = relay_slots(me_ref[0], morton_ref[...])
    lhs = relay_rows(state_ref[...], level_ref[...])
    store_moved(far_ref, dot_nt(lhs, one_hot_rows(HALF, far)))


def sib_kernel(me_ref, state_ref, level_ref, morton_ref, sib_ref):
    sib, _, _ = relay_slots(me_ref[0], morton_ref[...])
    lhs = relay_rows(state_ref[...], level_ref[...])
    store_moved(sib_ref, dot_nt(lhs, one_hot_rows(HALF, sib)))


def home_kernel(me_ref, state_ref, level_ref, morton_ref, home_ref):
    _, _, home = relay_slots(me_ref[0], morton_ref[...])
    got = dot_nt(relay_rows(state_ref[...], level_ref[...]), one_hot_rows(NEW_DEV, home))
    for c in range(BLOCKS):
        store_moved(home_ref.at[c], got[:, 128 * c : 128 * c + 128])


def requests(me, links, near_ref, far_ref):
    owner = links >> 9
    slot = links & (NEW_DEV - 1)
    gap = ((owner - me + 192) & 127) - 64
    gap = jnp.where((me & 1) == 0, gap, -gap)
    near_ref[...] = jnp.where(gap == 0, slot, -1)
    b = lax.broadcasted_iota(I32, (8, NEW_DEV), 0)
    step_of = jnp.where(b < 3, b + 2, jnp.where(b == 3, 1, 3 - b))
    masks = [jnp.where(gap[f : f + 1, :] == step_of, 1.0, 0.0) for f in range(6)]
    k = lax.broadcasted_iota(I32, (NEW_DEV, NEW_DEV), 0)
    j = lax.broadcasted_iota(I32, (NEW_DEV, NEW_DEV), 1)
    upper = jnp.where(k <= j, 1.0, 0.0).astype(BF16)
    counts = dot(jnp.concatenate(masks, axis=0).astype(BF16), upper)
    offset = jnp.full((8, 1), -1.0, F32)
    bf = b.astype(F32)
    total = jnp.zeros((16, CAP), F32)
    for f in range(6):
        run = counts[8 * f : 8 * f + 8, :]
        here = gap[f : f + 1, :] != 0
        rank = jnp.sum(masks[f] * (run + offset), axis=0, keepdims=True)
        bucket = jnp.sum(masks[f] * bf, axis=0, keepdims=True)
        offset = offset + run[:, NEW_DEV - 1 : NEW_DEV]
        rank = jnp.where(here, rank.astype(I32), -1)
        far_ref[f : f + 1, :] = jnp.where(here, bucket.astype(I32) * CAP + rank, -1)
        s = slot[f : f + 1, :]
        low = (s & 255).astype(F32)
        high = ((s >> 8) + 2 * (f ^ 1)).astype(F32)
        lhs = jnp.concatenate([masks[f] * low, masks[f] * high], axis=0).astype(BF16)
        total = total + dot_nt(lhs, one_hot_rows(CAP, rank))
    return total[0:8].astype(I32) + 256 * total[8:16].astype(I32)


def lower_half(shape):
    return lax.broadcasted_iota(I32, shape, 0) < 4


def trace(ref, c, v, f):
    a, s = f // 2, f % 2
    at = v * DOFS
    if a == 0:
        return ref[c, at + 48 * s : at + 48 * s + 16, :]
    if a == 1:
        out = []
        for h in range(2):
            r = at + 32 * h + 8 * s
            x = ref[c, r : r + 8, :]
            y = ref[c, r + 16 : r + 24, :]
            low = lower_half(x.shape)
            if s == 0:
                out.append(jnp.where(low, x, pltpu.roll(y, 4, 0)))
            else:
                out.append(jnp.where(low, pltpu.roll(x, 4, 0), y))
        return jnp.concatenate(out, axis=0)
    return ref[c, pl.ds(at + 3 * s, 16, stride=4), :]


def add_on_face(ref, c, v, f, x):
    a, s = f // 2, f % 2
    at = v * DOFS
    if a == 0:
        ref[c, at + 48 * s : at + 48 * s + 16, :] += x
    elif a == 1:
        for h in range(2):
            y = x[8 * h : 8 * h + 8, :]
            low = lower_half(y.shape)
            keep = low if s == 0 else ~low
            turned = pltpu.roll(y, 4, 0)
            first, second = (y, turned) if s == 0 else (turned, y)
            r = at + 32 * h + 8 * s
            ref[c, r : r + 8, :] += jnp.where(keep, first, 0.0)
            ref[c, r + 16 : r + 24, :] += jnp.where(keep, second, 0.0)
    else:
        spot = (c, pl.ds(at + 3 * s, 16, stride=4), slice(None))
        ref[spot] = ref[spot] + x


def wide(ref, rows):
    return jnp.concatenate([ref[c, 0:rows, :] for c in range(ref.shape[0])], axis=1)


def pressure_of(w, u):
    return (HEAT - 1.0) * (w[4] - 0.5 * (w[1] * u[0] + w[2] * u[1] + w[3] * u[2]))


def axis_flux(w, u, p, a):
    un = u[a]
    out = [w[1 + a]]
    for c in range(3):
        m = w[1 + c] * un
        out.append(m + p if c == a else m)
    out.append((w[4] + p) * un)
    return out


def side_term(w, f):
    sign = 1.0 if f % 2 else -1.0
    u = [w[1 + c] / w[0] for c in range(3)]
    p = pressure_of(w, u)
    flux = axis_flux(w, u, p, f // 2)
    return [(sign * flux[v]) - SPEED * w[v] for v in range(FIELDS)]


def asked_code(ask):
    return jnp.concatenate([ask[t : t + 1, :] for t in range(ask.shape[0])], axis=1)


def gather(fields, hot):
    high, low = split(fields)
    both = dot(jnp.concatenate([high, low], axis=0), hot)
    return both[0:ROWS] + both[ROWS:]


def pick_faces(got_ref, ask, outs):
    for t in range(ask.shape[0]):
        face = ask[t : t + 1, :] >> 9
        for v in range(FIELDS):
            x = trace(got_ref, t, v, 0)
            for f in range(1, 6):
                x = jnp.where(face == f, trace(got_ref, t, v, f), x)
            outs[t][16 * v : 16 * v + 16, :] = x


def reply(fields, ask, hot, got_ref, outs):
    got = gather(fields, hot)
    for t in range(ask.shape[0]):
        got_ref[t] = got[:, CAP * t : CAP * t + CAP]
    pick_faces(got_ref, ask, outs)


def hot_kernel(me_ref, far_ref, ask_ref, home_ref, sib_ref, rest_ref, reply_ref, base_ref, pre_ref):
    even = (me_ref[0] & 1) == 0
    for c in range(2):
        sib = sib_ref[:, 128 * c : 128 * c + 128]
        base_ref[c] = home_ref[c] + jnp.where(even, 0.0, sib)
        base_ref[c + 2] = home_ref[c + 2] + jnp.where(even, sib, 0.0)
    hot = one_hot_rows(NEW_DEV, asked_code(ask_ref[4:8, :]) & (NEW_DEV - 1))
    reply_ref[...] = hot
    got = gather(wide(base_ref, ROWS), hot)
    for t in range(4):
        pre_ref[t] = got[:, CAP * t : CAP * t + CAP]
    for f in range(6):
        rest_ref[f] = one_hot_rows(3 * CAP, far_ref[f : f + 1, :])


def own_kernel(fields_ref, ask_ref, a_ref, b_ref, sib_ref, got_ref):
    ask = ask_ref[0:4, :]
    hot = one_hot_rows(NEW_DEV, asked_code(ask) & (NEW_DEV - 1))
    outs = [a_ref.at[0], a_ref.at[1], b_ref.at[0], sib_ref.at[0]]
    reply(wide(fields_ref, ROWS), ask, hot, got_ref, outs)


def first_kernel(me_ref, base_ref, pre_ref, far_ref, ask_ref, hot_ref, start_ref, swap_ref, got_ref):
    odd = me_ref[0] & 1
    got = gather(far_ref[0:ROWS, :], hot_ref[pl.ds(pl.multiple_of(odd * HALF, HALF), HALF), :])
    for t in range(4):
        got_ref[t] = pre_ref[t] + got[:, CAP * t : CAP * t + CAP]
    pick_faces(got_ref, ask_ref[4:8, :], [swap_ref.at[t] for t in range(4)])
    for c in range(2):
        far = far_ref[:, 128 * c : 128 * c + 128]
        start_ref[c] = base_ref[c] + jnp.where(odd == 0, far, 0.0)
        start_ref[c + 2] = base_ref[c + 2] + jnp.where(odd == 0, 0.0, far)


def near_kernel(table_ref, fields_ref, near_ref, part_ref, high_ref, low_ref):
    for c in range(BLOCKS):
        spot = slice(128 * c, 128 * c + 128)
        w = [fields_ref[c, DOFS * v : DOFS * v + DOFS, :] for v in range(FIELDS)]
        u = [w[1 + i] / w[0] for i in range(3)]
        p = pressure_of(w, u)
        for a in range(3):
            flux = axis_flux(w, u, p, a)
            for v in range(FIELDS):
                high, low = split(flux[v])
                high_ref[v, DOFS * a : DOFS * a + DOFS, spot] = high
                low_ref[v, DOFS * a : DOFS * a + DOFS, spot] = low
    table = table_ref[...]
    for v in range(FIELDS):
        x = dot(table, high_ref[v])
        x = x[0:DOFS] + x[DOFS:] + dot(table[0:DOFS], low_ref[v])
        for c in range(BLOCKS):
            part_ref[c, DOFS * v : DOFS * v + DOFS, :] = x[:, 128 * c : 128 * c + 128]
    for f in range(6):
        hot = one_hot_rows(NEW_DEV, near_ref[f : f + 1, :])
        across = jnp.concatenate(
            [
                jnp.concatenate([trace(fields_ref, c, v, f ^ 1) for v in range(FIELDS)], axis=0)
                for c in range(BLOCKS)
            ],
            axis=1,
        )
        high, low = split(across)
        both = dot(jnp.concatenate([high, low], axis=0), hot)
        for c in range(BLOCKS):
            spot = slice(128 * c, 128 * c + 128)
            outer = both[0:TRACE_ROWS, spot] + both[TRACE_ROWS:, spot]
            there = near_ref[f : f + 1, spot] >= 0
            w = [outer[16 * v : 16 * v + 16] for v in range(FIELDS)]
            w[0] = jnp.where(there, w[0], 1.0)
            plus = side_term(w, f)
            minus = side_term([trace(fields_ref, c, v, f) for v in range(FIELDS)], f)
            for v in range(FIELDS):
                add_on_face(part_ref, c, v, f, 3.0 * (jnp.where(there, plus[v], 0.0) - minus[v]))


def ghost_terms(ghost, ask):
    face = (ask >> 9) ^ 1
    axis = face >> 1
    sign = jnp.where((face & 1) == 1, 3.0, -3.0)
    w = [ghost[16 * v : 16 * v + 16] for v in range(FIELDS)]
    u = [w[1 + c] / w[0] for c in range(3)]
    p = pressure_of(w, u)

    def along(x):
        return jnp.where(axis == 0, x[0], jnp.where(axis == 1, x[1], x[2]))

    un = along(u)
    flux = [along(w[1:4])]
    for c in range(3):
        flux.append(w[1 + c] * un + jnp.where(axis == c, p, 0.0))
    flux.append((w[4] + p) * un)
    return jnp.concatenate([sign * flux[v] - (3.0 * SPEED) * w[v] for v in range(FIELDS)], axis=0)


def ghost_rows(ghosts, ask_ref):
    parts = [split(ghost_terms(g, ask_ref[t])) for t, g in enumerate(ghosts)]
    high = jnp.concatenate([p[0] for p in parts], axis=1)
    low = jnp.concatenate([p[1] for p in parts], axis=1)
    return jnp.concatenate([high, low], axis=0)


def add_ghosts(sum_ref, lhs, hot_of, blocks=range(BLOCKS)):
    for f in range(6):
        both = dot(lhs, hot_of(f))
        for i, c in enumerate(blocks):
            spot = slice(128 * i, 128 * i + 128)
            term = both[0:TRACE_ROWS, spot] + both[TRACE_ROWS:, spot]
            for v in range(FIELDS):
                add_on_face(sum_ref, c, v, f, term[16 * v : 16 * v + 16])


def direct_kernel(part_ref, far_ref, ask_ref, own_ref, got_ref, b_ref, sib_ref, sum_ref):
    lhs = ghost_rows([sib_ref[0], got_ref[0], own_ref[0], b_ref[1], b_ref[0]], ask_ref)
    sum_ref[...] = part_ref[...]
    add_ghosts(sum_ref, lhs, lambda f: one_hot_rows(5 * CAP, far_ref[f : f + 1, :] - 3 * CAP))


def metric_of(start_ref, c):
    return jnp.where(start_ref[c, ROWS : ROWS + 1, :] > 0.5, 2.0, 1.0)


def second_kernel(start_ref, part_ref, rest_ref, own_ask_ref, post_ref, ask_ref, hot_ref,
                  section_ref, swap_ref, sum_ref, got_ref):
    lhs = ghost_rows([post_ref[1], post_ref[0], post_ref[2]], own_ask_ref)
    sum_ref[...] = part_ref[...]
    add_ghosts(sum_ref, lhs, lambda f: rest_ref[f])
    for c in range(BLOCKS):
        section_ref[c] = start_ref[c, 0:ROWS, :] - (DT * metric_of(start_ref, c)) * sum_ref[c]
    reply(wide(section_ref, ROWS), ask_ref[4:8, :], hot_ref[...], got_ref, [swap_ref.at[t] for t in range(4)])


def last_kernel(start_ref, section_ref, part_ref, rest_ref, own_ask_ref, post_ref,
                state_hbm, rate_hbm, sum_ref, state_ref, rate_ref, sems):
    lhs = ghost_rows([post_ref[1], post_ref[0], post_ref[2]], own_ask_ref)
    sum_ref[...] = part_ref[...]
    copies = []
    for half in range(2):
        pair = (2 * half, 2 * half + 1)
        add_ghosts(sum_ref, lhs, lambda f: rest_ref[f, :, HALF * half : HALF * half + HALF], pair)
        for c in pair:
            rate = -metric_of(start_ref, c) * sum_ref[c]
            rate_ref[c] = rate
            state_ref[c] = 0.5 * start_ref[c, 0:ROWS, :] + 0.5 * (section_ref[c] + DT * rate)
            for i, (src, dst) in enumerate(((rate_ref, rate_hbm), (state_ref, state_hbm))):
                copy = pltpu.make_async_copy(src.at[c], dst.at[:, pl.ds(128 * c, 128)], sems.at[i, c])
                copy.start()
                copies.append(copy)
    for copy in copies:
        copy.wait()


VM = pl.BlockSpec(memory_space=pltpu.VMEM)
SM = pl.BlockSpec(memory_space=pltpu.SMEM)
HB = pl.BlockSpec(memory_space=pltpu.HBM)


def call(kernel, outs, args, specs=None, scratch=(), flops=10**6, outs_in=None):
    return pl.pallas_call(
        kernel,
        out_shape=[jax.ShapeDtypeStruct(s, d) for s, d in outs],
        in_specs=specs or [VM] * len(args),
        out_specs=[outs_in or VM] * len(outs),
        scratch_shapes=[pltpu.VMEM(*s) if isinstance(s, tuple) else s for s in scratch],
        compiler_params=pltpu.CompilerParams(vmem_limit_bytes=24 * 2**20),
        cost_estimate=pl.CostEstimate(flops=flops, bytes_accessed=2**20, transcendentals=0),
    )(*args)


def swap_cores(x):
    n = lax.axis_size(AXES)
    return lax.ppermute(x, AXES, [(i, i ^ 1) for i in range(n)])


def swap_chips(x):
    n = lax.axis_size(AXES)
    return lax.ppermute(x, AXES, [(i, (i + (1 if i % 2 else -1)) % n) for i in range(n)])


def outward(x, by):
    n = lax.axis_size(AXES)
    return lax.ppermute(x, AXES, [(i, (i + (by if i % 2 == 0 else -by)) % n) for i in range(n)])


def outward_pair(own, got):
    b = outward(jnp.concatenate([own[1], got[2:4]], axis=0), 4)
    a = outward(jnp.concatenate([own[0], got[0:2]], axis=0), 2)
    return a, b


def swap_back(a, b):
    return swap_cores(jnp.concatenate([a[1:2], a[3:4], b[2:3]], axis=0))


def body(state_old, level_old, morton_old, neighbours):
    me = lax.axis_index(AXES).astype(I32).reshape(1)
    inputs = [
        pltpu.with_memory_space_constraint(x, pltpu.HBM)
        for x in (
            neighbours,
            state_old.reshape(ROWS, OLD_CAP),
            level_old.reshape(1, OLD_CAP),
            morton_old.reshape(1, OLD_CAP),
        )
    ]
    own_ask, swap_ask, near, far, state, level, morton = call(
        open_kernel,
        [
            ((3, 1, CAP), I32),
            ((5, 1, CAP), I32),
            ((6, NEW_DEV), I32),
            ((6, NEW_DEV), I32),
            ((ROWS, OLD_CAP), F32),
            ((1, OLD_CAP), I32),
            ((1, OLD_CAP), I32),
        ],
        (me, *inputs),
        [SM, HB, HB, HB, HB],
        [((6, NEW_DEV), I32), pltpu.SemaphoreType.DMA((4,))],
    )
    got = swap_cores(swap_ask)
    relay = [SM, VM, VM, VM]
    moved = ((MOVED_ROWS, HALF), F32)
    (to_far,) = call(far_kernel, [moved], (me, state, level, morton), relay)
    got, to_far = lax.optimization_barrier((got, to_far))
    a, b = outward_pair((own_ask[0:2], own_ask[2:3]), got[1:5])
    from_far = swap_chips(to_far)
    a, morton = lax.optimization_barrier((a, morton))
    (to_sib,) = call(sib_kernel, [moved], (me, state, level, morton), relay, flops=10**9)
    from_sib = swap_cores(to_sib)
    (home,) = call(home_kernel, [((BLOCKS, MOVED_ROWS, 128), F32)], (me, state, level, morton), relay)
    post = swap_back(a, b)
    asked = jnp.concatenate(
        [post[1], post[0], post[2], got[0], a[2], a[0], b[1], b[0]], axis=0
    )

    rest_hot, reply_hot, base, pre = call(
        hot_kernel,
        [
            ((6, 3 * CAP, NEW_DEV), BF16),
            ((NEW_DEV, 4 * CAP), BF16),
            ((BLOCKS, MOVED_ROWS, 128), F32),
            ((4, ROWS, CAP), F32),
        ],
        (me, far, asked, home, from_sib),
        [SM, VM, VM, VM, VM],
        flops=10**9,
    )
    swapped = ((4, TRACE_ROWS, CAP), F32)
    got_scratch = ((4, ROWS, CAP), F32)
    blocks = ((BLOCKS, ROWS, 128), F32)
    table = jnp.asarray(stacked_table())

    def neighbours_of(fields, swap):
        got = swap_cores(swap)
        *own, sib = call(
            own_kernel,
            [((2, TRACE_ROWS, CAP), F32), ((1, TRACE_ROWS, CAP), F32), ((1, TRACE_ROWS, CAP), F32)],
            (fields, asked),
            None,
            [got_scratch],
            flops=10**9,
        )
        a_own = outward(own[0], 2)
        b = outward(jnp.concatenate([own[1], got[2:4]], axis=0), 4)
        a_got = outward(got[0:2], 2)
        (part,) = call(
            near_kernel,
            [blocks],
            (table, fields, near),
            None,
            [((FIELDS, 3 * DOFS, NEW_DEV), BF16)] * 2,
            flops=10**9,
        )
        sib, part = lax.optimization_barrier((sib, part))
        sib = swap_cores(sib)
        a_own, a_got, b, part = lax.optimization_barrier((a_own, a_got, b, part))
        post = swap_cores(jnp.concatenate([a_own[1:2], a_got[1:2], b[2:3]], axis=0))
        (part,) = call(direct_kernel, [blocks], (part, far, swap_ask, a_own, a_got, b, sib), flops=10**9)
        return part, rest_hot, own_ask, post

    start, swap = call(
        first_kernel,
        [((BLOCKS, MOVED_ROWS, 128), F32), swapped],
        (me, base, pre, from_far, asked, reply_hot),
        [SM, VM, VM, VM, VM, VM],
        [got_scratch],
    )
    ghosts = neighbours_of(start, swap)
    section, swap = call(
        second_kernel,
        [blocks, swapped],
        (start, *ghosts, asked, reply_hot),
        None,
        [blocks, got_scratch],
    )
    ghosts = neighbours_of(section, swap)
    new_state, rate = call(
        last_kernel,
        [((ROWS, NEW_DEV), F32)] * 2,
        (start, section, *ghosts),
        None,
        [blocks, blocks, blocks, pltpu.SemaphoreType.DMA((2, BLOCKS))],
        outs_in=HB,
    )
    shape = (FIELDS, DOFS, NEW_DEV)
    return new_state.reshape(shape), rate.reshape(shape)


def solution(mesh):
    wide = P(None, None, AXES)
    return jax.shard_map(
        body,
        mesh=mesh,
        in_specs=(wide, P(AXES), P(AXES), P(None, AXES)),
        out_specs=(wide, wide),
        check_vma=False,
    )
```

```python
import jax
import jax.numpy as jnp
import numpy as np
from jax import lax
from jax.experimental import pallas as pl
from jax.experimental.pallas import tpu as pltpu
from jax.sharding import PartitionSpec as P

FIELDS = 5
DOFS = 64
ROWS = FIELDS * DOFS
NEW_DEV = 512
HALF = NEW_DEV // 2
OLD_CAP = 1024
CAP = 128
TRACE_ROWS = FIELDS * 16
MOVED_ROWS = ROWS + 8
BLOCKS = NEW_DEV // 128

HEAT = 1.4
SPEED = 4.0
DT = 0.0002
AXES = ("px", "py")
F32 = jnp.float32
BF16 = jnp.bfloat16
I32 = jnp.int32

STEPS = (2, 3, 4, 1, -1, -2, -3, -4)


def derivative_table():
    points = np.array([-1.0, -1.0 / np.sqrt(5.0), 1.0 / np.sqrt(5.0), 1.0])
    weights = np.array(
        [1.0 / np.prod([points[c] - points[o] for o in range(4) if o != c]) for c in range(4)]
    )
    table = np.zeros((4, 4))
    for r in range(4):
        for c in range(4):
            if r != c:
                table[r, c] = weights[c] / weights[r] / (points[r] - points[c])
        table[r, r] = -np.sum(table[r])
    return table


def stacked_table():
    d = derivative_table().astype(np.float32).astype(np.float64)
    one = np.eye(4)
    full = np.concatenate(
        [
            np.kron(np.kron(d, one), one),
            np.kron(np.kron(one, d), one),
            np.kron(np.kron(one, one), d),
        ],
        axis=1,
    ).astype(np.float32)
    high = full.astype(jnp.bfloat16)
    low = (full - high.astype(np.float32)).astype(jnp.bfloat16)
    return np.concatenate([high, low], axis=0)


def split(x):
    high = x.astype(BF16)
    low = (x - high.astype(F32)).astype(BF16)
    return high, low


def dot(a, b):
    return lax.dot_general(a, b, (((1,), (0,)), ((), ())), preferred_element_type=F32)


def dot_nt(a, b):
    return lax.dot_general(a, b, (((1,), (1,)), ((), ())), preferred_element_type=F32)


def one_hot_rows(size, row):
    spots = lax.broadcasted_iota(I32, (size, row.shape[1]), 0)
    return jnp.where(spots == row, 1.0, 0.0).astype(BF16)


def relay_slots(me, morton):
    occupied = morton >= 0
    owner = morton >> 9
    slot = morton & (NEW_DEV - 1)
    gap = (owner - me) & 127
    even = (me & 1) == 0
    to_next = occupied & (gap == 1)
    to_prior = occupied & (gap == 127)
    home = jnp.where(occupied & (gap == 0), slot, -1)
    ahead = jnp.where(to_next, slot, -1)
    behind = jnp.where(to_prior, slot - HALF, -1)
    sib = jnp.where(even, ahead, behind)
    far = jnp.where(even, behind, ahead)
    return sib, far, home


def store_moved(ref, got):
    ref[0:ROWS, :] = got[0:ROWS] + got[ROWS : 2 * ROWS]
    ref[ROWS : ROWS + 8, :] = got[2 * ROWS : 2 * ROWS + 8]


def relay_rows(state, level):
    high, low = split(state)
    lev = jnp.broadcast_to(level.astype(F32), (16, OLD_CAP)).astype(BF16)
    return jnp.concatenate([high, low, lev], axis=0)


def open_kernel(me_ref, links_hbm, state_hbm, level_hbm, morton_hbm, own_ask_ref, swap_ask_ref, near_ref, far_ref,
                state_ref, level_ref, morton_ref, links_ref, sems):
    pairs = ((links_hbm, links_ref), (morton_hbm, morton_ref), (level_hbm, level_ref), (state_hbm, state_ref))
    copies = [pltpu.make_async_copy(src, dst, sems.at[i]) for i, (src, dst) in enumerate(pairs)]
    for copy in copies:
        copy.start()
    copies[0].wait()
    ask = requests(me_ref[0], links_ref[...], near_ref, far_ref)
    for t in range(8):
        if t < 3:
            own_ask_ref[t] = ask[t : t + 1]
        else:
            swap_ask_ref[t - 3] = ask[t : t + 1]
    for copy in copies[1:]:
        copy.wait()


def far_kernel(me_ref, state_ref, level_ref, morton_ref, far_ref):
    _, far, _ = relay_slots(me_ref[0], morton_ref[...])
    lhs = relay_rows(state_ref[...], level_ref[...])
    store_moved(far_ref, dot_nt(lhs, one_hot_rows(HALF, far)))


def sib_kernel(me_ref, state_ref, level_ref, morton_ref, sib_ref):
    sib, _, _ = relay_slots(me_ref[0], morton_ref[...])
    lhs = relay_rows(state_ref[...], level_ref[...])
    store_moved(sib_ref, dot_nt(lhs, one_hot_rows(HALF, sib)))


def home_kernel(me_ref, state_ref, level_ref, morton_ref, home_ref):
    _, _, home = relay_slots(me_ref[0], morton_ref[...])
    got = dot_nt(relay_rows(state_ref[...], level_ref[...]), one_hot_rows(NEW_DEV, home))
    for c in range(BLOCKS):
        store_moved(home_ref.at[c], got[:, 128 * c : 128 * c + 128])


def requests(me, links, near_ref, far_ref):
    owner = links >> 9
    slot = links & (NEW_DEV - 1)
    gap = ((owner - me + 192) & 127) - 64
    gap = jnp.where((me & 1) == 0, gap, -gap)
    near_ref[...] = jnp.where(gap == 0, slot, -1)
    b = lax.broadcasted_iota(I32, (8, NEW_DEV), 0)
    step_of = jnp.where(b < 3, b + 2, jnp.where(b == 3, 1, 3 - b))
    masks = [jnp.where(gap[f : f + 1, :] == step_of, 1.0, 0.0) for f in range(6)]
    k = lax.broadcasted_iota(I32, (128, 128), 0)
    j = lax.broadcasted_iota(I32, (128, 128), 1)
    upper = jnp.where(k <= j, 1.0, 0.0).astype(BF16)
    every = jnp.concatenate(masks, axis=0)
    blocks = [every[:, 128 * q : 128 * q + 128] for q in range(BLOCKS)]
    inside = dot(jnp.concatenate(blocks, axis=0).astype(BF16), upper)
    before = jnp.zeros((48, 1), F32)
    counts = []
    for q in range(BLOCKS):
        counts.append(inside[48 * q : 48 * q + 48] + before)
        before = counts[-1][:, 127:128]
    counts = jnp.concatenate(counts, axis=1)
    offset = jnp.full((8, 1), -1.0, F32)
    bf = b.astype(F32)
    total = jnp.zeros((16, CAP), F32)
    for f in range(6):
        run = counts[8 * f : 8 * f + 8, :]
        here = gap[f : f + 1, :] != 0
        rank = jnp.sum(masks[f] * (run + offset), axis=0, keepdims=True)
        bucket = jnp.sum(masks[f] * bf, axis=0, keepdims=True)
        offset = offset + run[:, NEW_DEV - 1 : NEW_DEV]
        rank = jnp.where(here, rank.astype(I32), -1)
        far_ref[f : f + 1, :] = jnp.where(here, bucket.astype(I32) * CAP + rank, -1)
        s = slot[f : f + 1, :]
        low = (s & 255).astype(F32)
        high = ((s >> 8) + 2 * (f ^ 1)).astype(F32)
        lhs = jnp.concatenate([masks[f] * low, masks[f] * high], axis=0).astype(BF16)
        total = total + dot_nt(lhs, one_hot_rows(CAP, rank))
    return total[0:8].astype(I32) + 256 * total[8:16].astype(I32)


def lower_half(shape):
    return lax.broadcasted_iota(I32, shape, 0) < 4


def trace(ref, c, v, f):
    a, s = f // 2, f % 2
    at = v * DOFS
    if a == 0:
        return ref[c, at + 48 * s : at + 48 * s + 16, :]
    if a == 1:
        out = []
        for h in range(2):
            r = at + 32 * h + 8 * s
            x = ref[c, r : r + 8, :]
            y = ref[c, r + 16 : r + 24, :]
            low = lower_half(x.shape)
            if s == 0:
                out.append(jnp.where(low, x, pltpu.roll(y, 4, 0)))
            else:
                out.append(jnp.where(low, pltpu.roll(x, 4, 0), y))
        return jnp.concatenate(out, axis=0)
    return ref[c, pl.ds(at + 3 * s, 16, stride=4), :]


def add_on_face(ref, c, v, f, x):
    a, s = f // 2, f % 2
    at = v * DOFS
    if a == 0:
        ref[c, at + 48 * s : at + 48 * s + 16, :] += x
    elif a == 1:
        for h in range(2):
            y = x[8 * h : 8 * h + 8, :]
            low = lower_half(y.shape)
            keep = low if s == 0 else ~low
            turned = pltpu.roll(y, 4, 0)
            first, second = (y, turned) if s == 0 else (turned, y)
            r = at + 32 * h + 8 * s
            ref[c, r : r + 8, :] += jnp.where(keep, first, 0.0)
            ref[c, r + 16 : r + 24, :] += jnp.where(keep, second, 0.0)
    else:
        spot = (c, pl.ds(at + 3 * s, 16, stride=4), slice(None))
        ref[spot] = ref[spot] + x


def wide(ref, rows):
    return jnp.concatenate([ref[c, 0:rows, :] for c in range(ref.shape[0])], axis=1)


def pressure_of(w, u):
    return (HEAT - 1.0) * (w[4] - 0.5 * (w[1] * u[0] + w[2] * u[1] + w[3] * u[2]))


def axis_flux(w, u, p, a):
    un = u[a]
    out = [w[1 + a]]
    for c in range(3):
        m = w[1 + c] * un
        out.append(m + p if c == a else m)
    out.append((w[4] + p) * un)
    return out


def side_term(w, f):
    sign = 1.0 if f % 2 else -1.0
    u = [w[1 + c] / w[0] for c in range(3)]
    p = pressure_of(w, u)
    flux = axis_flux(w, u, p, f // 2)
    return [(sign * flux[v]) - SPEED * w[v] for v in range(FIELDS)]


def asked_code(ask):
    return jnp.concatenate([ask[t : t + 1, :] for t in range(ask.shape[0])], axis=1)


def gather(fields, hot):
    high, low = split(fields)
    both = dot(jnp.concatenate([high, low], axis=0), hot)
    return both[0:ROWS] + both[ROWS:]


def pick_faces(got_ref, ask, outs):
    for t in range(ask.shape[0]):
        face = ask[t : t + 1, :] >> 9
        for v in range(FIELDS):
            x = trace(got_ref, t, v, 0)
            for f in range(1, 6):
                x = jnp.where(face == f, trace(got_ref, t, v, f), x)
            outs[t][16 * v : 16 * v + 16, :] = x


def reply(fields, ask, hot, got_ref, outs):
    got = gather(fields, hot)
    for t in range(ask.shape[0]):
        got_ref[t] = got[:, CAP * t : CAP * t + CAP]
    pick_faces(got_ref, ask, outs)


def hot_kernel(me_ref, far_ref, ask_ref, home_ref, sib_ref, rest_ref, reply_ref, base_ref, pre_ref):
    even = (me_ref[0] & 1) == 0
    for c in range(2):
        sib = sib_ref[:, 128 * c : 128 * c + 128]
        base_ref[c] = home_ref[c] + jnp.where(even, 0.0, sib)
        base_ref[c + 2] = home_ref[c + 2] + jnp.where(even, sib, 0.0)
    hot = one_hot_rows(NEW_DEV, asked_code(ask_ref[4:8, :]) & (NEW_DEV - 1))
    reply_ref[...] = hot
    got = gather(wide(base_ref, ROWS), hot)
    for t in range(4):
        pre_ref[t] = got[:, CAP * t : CAP * t + CAP]
    for f in range(6):
        rest_ref[f] = one_hot_rows(3 * CAP, far_ref[f : f + 1, :])


def own_kernel(fields_ref, ask_ref, a_ref, b_ref, sib_ref, got_ref):
    ask = ask_ref[0:4, :]
    hot = one_hot_rows(NEW_DEV, asked_code(ask) & (NEW_DEV - 1))
    outs = [a_ref.at[0], a_ref.at[1], b_ref.at[0], sib_ref.at[0]]
    reply(wide(fields_ref, ROWS), ask, hot, got_ref, outs)


def first_kernel(me_ref, base_ref, pre_ref, far_ref, ask_ref, hot_ref, start_ref, swap_ref, got_ref):
    odd = me_ref[0] & 1
    got = gather(far_ref[0:ROWS, :], hot_ref[pl.ds(pl.multiple_of(odd * HALF, HALF), HALF), :])
    for t in range(4):
        got_ref[t] = pre_ref[t] + got[:, CAP * t : CAP * t + CAP]
    pick_faces(got_ref, ask_ref[4:8, :], [swap_ref.at[t] for t in range(4)])
    for c in range(2):
        far = far_ref[:, 128 * c : 128 * c + 128]
        start_ref[c] = base_ref[c] + jnp.where(odd == 0, far, 0.0)
        start_ref[c + 2] = base_ref[c + 2] + jnp.where(odd == 0, 0.0, far)


def near_kernel(table_ref, fields_ref, near_ref, part_ref, high_ref, low_ref):
    for c in range(BLOCKS):
        spot = slice(128 * c, 128 * c + 128)
        w = [fields_ref[c, DOFS * v : DOFS * v + DOFS, :] for v in range(FIELDS)]
        u = [w[1 + i] / w[0] for i in range(3)]
        p = pressure_of(w, u)
        for a in range(3):
            flux = axis_flux(w, u, p, a)
            for v in range(FIELDS):
                high, low = split(flux[v])
                high_ref[v, DOFS * a : DOFS * a + DOFS, spot] = high
                low_ref[v, DOFS * a : DOFS * a + DOFS, spot] = low
    table = table_ref[...]
    for v in range(FIELDS):
        x = dot(table, high_ref[v])
        x = x[0:DOFS] + x[DOFS:] + dot(table[0:DOFS], low_ref[v])
        for c in range(BLOCKS):
            part_ref[c, DOFS * v : DOFS * v + DOFS, :] = x[:, 128 * c : 128 * c + 128]
    for f in range(6):
        hot = one_hot_rows(NEW_DEV, near_ref[f : f + 1, :])
        across = jnp.concatenate(
            [
                jnp.concatenate([trace(fields_ref, c, v, f ^ 1) for v in range(FIELDS)], axis=0)
                for c in range(BLOCKS)
            ],
            axis=1,
        )
        high, low = split(across)
        both = dot(jnp.concatenate([high, low], axis=0), hot)
        for c in range(BLOCKS):
            spot = slice(128 * c, 128 * c + 128)
            outer = both[0:TRACE_ROWS, spot] + both[TRACE_ROWS:, spot]
            there = near_ref[f : f + 1, spot] >= 0
            w = [outer[16 * v : 16 * v + 16] for v in range(FIELDS)]
            w[0] = jnp.where(there, w[0], 1.0)
            plus = side_term(w, f)
            minus = side_term([trace(fields_ref, c, v, f) for v in range(FIELDS)], f)
            for v in range(FIELDS):
                add_on_face(part_ref, c, v, f, 3.0 * (jnp.where(there, plus[v], 0.0) - minus[v]))


def ghost_terms(ghost, ask):
    face = (ask >> 9) ^ 1
    axis = face >> 1
    sign = jnp.where((face & 1) == 1, 3.0, -3.0)
    w = [ghost[16 * v : 16 * v + 16] for v in range(FIELDS)]
    u = [w[1 + c] / w[0] for c in range(3)]
    p = pressure_of(w, u)

    def along(x):
        return jnp.where(axis == 0, x[0], jnp.where(axis == 1, x[1], x[2]))

    un = along(u)
    flux = [along(w[1:4])]
    for c in range(3):
        flux.append(w[1 + c] * un + jnp.where(axis == c, p, 0.0))
    flux.append((w[4] + p) * un)
    return jnp.concatenate([sign * flux[v] - (3.0 * SPEED) * w[v] for v in range(FIELDS)], axis=0)


def ghost_rows(ghosts, ask_ref):
    parts = [split(ghost_terms(g, ask_ref[t])) for t, g in enumerate(ghosts)]
    high = jnp.concatenate([p[0] for p in parts], axis=1)
    low = jnp.concatenate([p[1] for p in parts], axis=1)
    return jnp.concatenate([high, low], axis=0)


def add_ghosts(part_ref, sum_ref, lhs, hot_of, blocks=range(BLOCKS)):
    for c in blocks:
        for v in range(FIELDS):
            rows = slice(DOFS * v + 16, DOFS * v + 48)
            sum_ref[c, rows, :] = part_ref[c, rows, :]
    for f in range(6):
        both = dot(lhs, hot_of(f))
        for i, c in enumerate(blocks):
            spot = slice(128 * i, 128 * i + 128)
            term = both[0:TRACE_ROWS, spot] + both[TRACE_ROWS:, spot]
            for v in range(FIELDS):
                x = term[16 * v : 16 * v + 16]
                if f < 2:
                    rows = slice(DOFS * v + 48 * f, DOFS * v + 48 * f + 16)
                    sum_ref[c, rows, :] = part_ref[c, rows, :] + x
                else:
                    add_on_face(sum_ref, c, v, f, x)


def direct_kernel(part_ref, far_ref, ask_ref, own_ref, got_ref, b_ref, sib_ref, sum_ref):
    lhs = ghost_rows([sib_ref[0], got_ref[0], own_ref[0], b_ref[1], b_ref[0]], ask_ref)
    add_ghosts(part_ref, sum_ref, lhs, lambda f: one_hot_rows(5 * CAP, far_ref[f : f + 1, :] - 3 * CAP))


def metric_of(start_ref, c):
    return jnp.where(start_ref[c, ROWS : ROWS + 1, :] > 0.5, 2.0, 1.0)


def second_kernel(start_ref, part_ref, rest_ref, own_ask_ref, post_ref, ask_ref, hot_ref,
                  section_ref, swap_ref, sum_ref, got_ref):
    lhs = ghost_rows([post_ref[1], post_ref[0], post_ref[2]], own_ask_ref)
    add_ghosts(part_ref, sum_ref, lhs, lambda f: rest_ref[f])
    for c in range(BLOCKS):
        section_ref[c] = start_ref[c, 0:ROWS, :] - (DT * metric_of(start_ref, c)) * sum_ref[c]
    reply(wide(section_ref, ROWS), ask_ref[4:8, :], hot_ref[...], got_ref, [swap_ref.at[t] for t in range(4)])


def last_kernel(start_ref, section_ref, part_ref, rest_ref, own_ask_ref, post_ref,
                state_hbm, rate_hbm, sum_ref, state_ref, rate_ref, sems):
    lhs = ghost_rows([post_ref[1], post_ref[0], post_ref[2]], own_ask_ref)
    copies = []
    for half in range(2):
        pair = (2 * half, 2 * half + 1)
        add_ghosts(part_ref, sum_ref, lhs, lambda f: rest_ref[f, :, HALF * half : HALF * half + HALF], pair)
        for c in pair:
            rate = -metric_of(start_ref, c) * sum_ref[c]
            rate_ref[c] = rate
            state_ref[c] = 0.5 * start_ref[c, 0:ROWS, :] + 0.5 * (section_ref[c] + DT * rate)
            for i, (src, dst) in enumerate(((rate_ref, rate_hbm), (state_ref, state_hbm))):
                copy = pltpu.make_async_copy(src.at[c], dst.at[:, pl.ds(128 * c, 128)], sems.at[i, c])
                copy.start()
                copies.append(copy)
    for copy in copies:
        copy.wait()


VM = pl.BlockSpec(memory_space=pltpu.VMEM)
SM = pl.BlockSpec(memory_space=pltpu.SMEM)
HB = pl.BlockSpec(memory_space=pltpu.HBM)


def call(kernel, outs, args, specs=None, scratch=(), flops=10**6, outs_in=None):
    return pl.pallas_call(
        kernel,
        out_shape=[jax.ShapeDtypeStruct(s, d) for s, d in outs],
        in_specs=specs or [VM] * len(args),
        out_specs=[outs_in or VM] * len(outs),
        scratch_shapes=[pltpu.VMEM(*s) if isinstance(s, tuple) else s for s in scratch],
        compiler_params=pltpu.CompilerParams(vmem_limit_bytes=24 * 2**20),
        cost_estimate=pl.CostEstimate(flops=flops, bytes_accessed=2**20, transcendentals=0),
    )(*args)


def swap_cores(x):
    n = lax.axis_size(AXES)
    return lax.ppermute(x, AXES, [(i, i ^ 1) for i in range(n)])


def swap_chips(x):
    n = lax.axis_size(AXES)
    return lax.ppermute(x, AXES, [(i, (i + (1 if i % 2 else -1)) % n) for i in range(n)])


def outward(x, by):
    n = lax.axis_size(AXES)
    return lax.ppermute(x, AXES, [(i, (i + (by if i % 2 == 0 else -by)) % n) for i in range(n)])


def outward_pair(own, got):
    b = outward(jnp.concatenate([own[1], got[2:4]], axis=0), 4)
    a = outward(jnp.concatenate([own[0], got[0:2]], axis=0), 2)
    return a, b


def swap_back(a, b):
    return swap_cores(jnp.concatenate([a[1:2], a[3:4], b[2:3]], axis=0))


def body(state_old, level_old, morton_old, neighbours):
    me = lax.axis_index(AXES).astype(I32).reshape(1)
    inputs = [
        pltpu.with_memory_space_constraint(x, pltpu.HBM)
        for x in (
            neighbours,
            state_old.reshape(ROWS, OLD_CAP),
            level_old.reshape(1, OLD_CAP),
            morton_old.reshape(1, OLD_CAP),
        )
    ]
    own_ask, swap_ask, near, far, state, level, morton = call(
        open_kernel,
        [
            ((3, 1, CAP), I32),
            ((5, 1, CAP), I32),
            ((6, NEW_DEV), I32),
            ((6, NEW_DEV), I32),
            ((ROWS, OLD_CAP), F32),
            ((1, OLD_CAP), I32),
            ((1, OLD_CAP), I32),
        ],
        (me, *inputs),
        [SM, HB, HB, HB, HB],
        [((6, NEW_DEV), I32), pltpu.SemaphoreType.DMA((4,))],
    )
    got = swap_cores(swap_ask)
    relay = [SM, VM, VM, VM]
    moved = ((MOVED_ROWS, HALF), F32)
    (to_far,) = call(far_kernel, [moved], (me, state, level, morton), relay)
    got, to_far = lax.optimization_barrier((got, to_far))
    a, b = outward_pair((own_ask[0:2], own_ask[2:3]), got[1:5])
    from_far = swap_chips(to_far)
    a, morton = lax.optimization_barrier((a, morton))
    (to_sib,) = call(sib_kernel, [moved], (me, state, level, morton), relay, flops=10**9)
    from_sib = swap_cores(to_sib)
    (home,) = call(home_kernel, [((BLOCKS, MOVED_ROWS, 128), F32)], (me, state, level, morton), relay)
    post = swap_back(a, b)
    asked = jnp.concatenate(
        [post[1], post[0], post[2], got[0], a[2], a[0], b[1], b[0]], axis=0
    )

    rest_hot, reply_hot, base, pre = call(
        hot_kernel,
        [
            ((6, 3 * CAP, NEW_DEV), BF16),
            ((NEW_DEV, 4 * CAP), BF16),
            ((BLOCKS, MOVED_ROWS, 128), F32),
            ((4, ROWS, CAP), F32),
        ],
        (me, far, asked, home, from_sib),
        [SM, VM, VM, VM, VM],
        flops=10**9,
    )
    swapped = ((4, TRACE_ROWS, CAP), F32)
    got_scratch = ((4, ROWS, CAP), F32)
    blocks = ((BLOCKS, ROWS, 128), F32)
    table = jnp.asarray(stacked_table())

    def neighbours_of(fields, swap):
        got = swap_cores(swap)
        *own, sib = call(
            own_kernel,
            [((2, TRACE_ROWS, CAP), F32), ((1, TRACE_ROWS, CAP), F32), ((1, TRACE_ROWS, CAP), F32)],
            (fields, asked),
            None,
            [got_scratch],
            flops=10**9,
        )
        a_own = outward(own[0], 2)
        b = outward(jnp.concatenate([own[1], got[2:4]], axis=0), 4)
        a_got = outward(got[0:2], 2)
        (part,) = call(
            near_kernel,
            [blocks],
            (table, fields, near),
            None,
            [((FIELDS, 3 * DOFS, NEW_DEV), BF16)] * 2,
            flops=10**9,
        )
        sib, part = lax.optimization_barrier((sib, part))
        sib = swap_cores(sib)
        a_own, a_got, b, part = lax.optimization_barrier((a_own, a_got, b, part))
        post = swap_cores(jnp.concatenate([a_own[1:2], a_got[1:2], b[2:3]], axis=0))
        (part,) = call(direct_kernel, [blocks], (part, far, swap_ask, a_own, a_got, b, sib), flops=10**9)
        return part, rest_hot, own_ask, post

    start, swap = call(
        first_kernel,
        [((BLOCKS, MOVED_ROWS, 128), F32), swapped],
        (me, base, pre, from_far, asked, reply_hot),
        [SM, VM, VM, VM, VM, VM],
        [got_scratch],
    )
    ghosts = neighbours_of(start, swap)
    section, swap = call(
        second_kernel,
        [blocks, swapped],
        (start, *ghosts, asked, reply_hot),
        None,
        [blocks, got_scratch],
    )
    ghosts = neighbours_of(section, swap)
    new_state, rate = call(
        last_kernel,
        [((ROWS, NEW_DEV), F32)] * 2,
        (start, section, *ghosts),
        None,
        [blocks, blocks, blocks, pltpu.SemaphoreType.DMA((2, BLOCKS))],
        outs_in=HB,
    )
    shape = (FIELDS, DOFS, NEW_DEV)
    return new_state.reshape(shape), rate.reshape(shape)


def solution(mesh):
    wide = P(None, None, AXES)
    return jax.shard_map(
        body,
        mesh=mesh,
        in_specs=(wide, P(AXES), P(AXES), P(None, AXES)),
        out_specs=(wide, wide),
        check_vma=False,
    )
```

```python
import jax
import jax.numpy as jnp
import numpy as np
from jax import lax
from jax.experimental import pallas as pl
from jax.experimental.pallas import tpu as pltpu
from jax.sharding import PartitionSpec as P

FIELDS = 5
DOFS = 64
ROWS = FIELDS * DOFS
NEW_DEV = 512
HALF = NEW_DEV // 2
OLD_CAP = 1024
CAP = 128
TRACE_ROWS = FIELDS * 16
MOVED_ROWS = ROWS + 8
BLOCKS = NEW_DEV // 128

HEAT = 1.4
SPEED = 4.0
DT = 0.0002
AXES = ("px", "py")
F32 = jnp.float32
BF16 = jnp.bfloat16
I32 = jnp.int32

STEPS = (2, 3, 4, 1, -1, -2, -3, -4)


def derivative_table():
    points = np.array([-1.0, -1.0 / np.sqrt(5.0), 1.0 / np.sqrt(5.0), 1.0])
    weights = np.array(
        [1.0 / np.prod([points[c] - points[o] for o in range(4) if o != c]) for c in range(4)]
    )
    table = np.zeros((4, 4))
    for r in range(4):
        for c in range(4):
            if r != c:
                table[r, c] = weights[c] / weights[r] / (points[r] - points[c])
        table[r, r] = -np.sum(table[r])
    return table


def stacked_table():
    d = derivative_table().astype(np.float32).astype(np.float64)
    one = np.eye(4)
    full = np.concatenate(
        [
            np.kron(np.kron(d, one), one),
            np.kron(np.kron(one, d), one),
            np.kron(np.kron(one, one), d),
        ],
        axis=1,
    ).astype(np.float32)
    high = full.astype(jnp.bfloat16)
    low = (full - high.astype(np.float32)).astype(jnp.bfloat16)
    return np.concatenate([high, low], axis=0)


def split(x):
    high = x.astype(BF16)
    low = (x - high.astype(F32)).astype(BF16)
    return high, low


def dot(a, b):
    return lax.dot_general(a, b, (((1,), (0,)), ((), ())), preferred_element_type=F32)


def dot_nt(a, b):
    return lax.dot_general(a, b, (((1,), (1,)), ((), ())), preferred_element_type=F32)


def one_hot_rows(size, row):
    spots = lax.broadcasted_iota(I32, (size, row.shape[1]), 0)
    return jnp.where(spots == row, 1.0, 0.0).astype(BF16)


def relay_slots(me, morton):
    occupied = morton >= 0
    owner = morton >> 9
    slot = morton & (NEW_DEV - 1)
    gap = (owner - me) & 127
    even = (me & 1) == 0
    to_next = occupied & (gap == 1)
    to_prior = occupied & (gap == 127)
    home = jnp.where(occupied & (gap == 0), slot, -1)
    ahead = jnp.where(to_next, slot, -1)
    behind = jnp.where(to_prior, slot - HALF, -1)
    sib = jnp.where(even, ahead, behind)
    far = jnp.where(even, behind, ahead)
    return sib, far, home


def store_moved(ref, got):
    ref[0:ROWS, :] = got[0:ROWS] + got[ROWS : 2 * ROWS]
    ref[ROWS : ROWS + 8, :] = got[2 * ROWS : 2 * ROWS + 8]


def relay_rows(state, level):
    high, low = split(state)
    lev = jnp.broadcast_to(level.astype(F32), (16, OLD_CAP)).astype(BF16)
    return jnp.concatenate([high, low, lev], axis=0)


def open_kernel(me_ref, links_hbm, state_hbm, level_hbm, morton_hbm, own_ask_ref, swap_ask_ref, near_ref, far_ref,
                state_ref, level_ref, morton_ref, links_ref, sems):
    pairs = ((links_hbm, links_ref), (morton_hbm, morton_ref), (level_hbm, level_ref), (state_hbm, state_ref))
    copies = [pltpu.make_async_copy(src, dst, sems.at[i]) for i, (src, dst) in enumerate(pairs)]
    for copy in copies:
        copy.start()
    copies[0].wait()
    ask = requests(me_ref[0], links_ref[...], near_ref, far_ref)
    for t in range(8):
        if t < 3:
            own_ask_ref[t] = ask[t : t + 1]
        else:
            swap_ask_ref[t - 3] = ask[t : t + 1]
    for copy in copies[1:]:
        copy.wait()


def far_kernel(me_ref, state_ref, level_ref, morton_ref, far_ref):
    _, far, _ = relay_slots(me_ref[0], morton_ref[...])
    lhs = relay_rows(state_ref[...], level_ref[...])
    store_moved(far_ref, dot_nt(lhs, one_hot_rows(HALF, far)))


def sib_kernel(me_ref, state_ref, level_ref, morton_ref, sib_ref):
    sib, _, _ = relay_slots(me_ref[0], morton_ref[...])
    lhs = relay_rows(state_ref[...], level_ref[...])
    store_moved(sib_ref, dot_nt(lhs, one_hot_rows(HALF, sib)))


def home_kernel(me_ref, state_ref, level_ref, morton_ref, home_ref):
    _, _, home = relay_slots(me_ref[0], morton_ref[...])
    got = dot_nt(relay_rows(state_ref[...], level_ref[...]), one_hot_rows(NEW_DEV, home))
    for c in range(BLOCKS):
        store_moved(home_ref.at[c], got[:, 128 * c : 128 * c + 128])


def requests(me, links, near_ref, far_ref):
    owner = links >> 9
    slot = links & (NEW_DEV - 1)
    gap = ((owner - me + 192) & 127) - 64
    gap = jnp.where((me & 1) == 0, gap, -gap)
    near_ref[...] = jnp.where(gap == 0, slot, -1)
    b = lax.broadcasted_iota(I32, (8, NEW_DEV), 0)
    step_of = jnp.where(b < 3, b + 2, jnp.where(b == 3, 1, 3 - b))
    masks = [jnp.where(gap[f : f + 1, :] == step_of, 1.0, 0.0) for f in range(6)]
    k = lax.broadcasted_iota(I32, (NEW_DEV, NEW_DEV), 0)
    j = lax.broadcasted_iota(I32, (NEW_DEV, NEW_DEV), 1)
    upper = jnp.where(k <= j, 1.0, 0.0).astype(BF16)
    counts = dot(jnp.concatenate(masks, axis=0).astype(BF16), upper)
    offset = jnp.full((8, 1), -1.0, F32)
    bf = b.astype(F32)
    total = jnp.zeros((16, CAP), F32)
    for f in range(6):
        run = counts[8 * f : 8 * f + 8, :]
        here = gap[f : f + 1, :] != 0
        rank = jnp.sum(masks[f] * (run + offset), axis=0, keepdims=True)
        bucket = jnp.sum(masks[f] * bf, axis=0, keepdims=True)
        offset = offset + run[:, NEW_DEV - 1 : NEW_DEV]
        rank = jnp.where(here, rank.astype(I32), -1)
        far_ref[f : f + 1, :] = jnp.where(here, bucket.astype(I32) * CAP + rank, -1)
        s = slot[f : f + 1, :]
        low = (s & 255).astype(F32)
        high = ((s >> 8) + 2 * (f ^ 1)).astype(F32)
        lhs = jnp.concatenate([masks[f] * low, masks[f] * high], axis=0).astype(BF16)
        total = total + dot_nt(lhs, one_hot_rows(CAP, rank))
    return total[0:8].astype(I32) + 256 * total[8:16].astype(I32)


def lower_half(shape):
    return lax.broadcasted_iota(I32, shape, 0) < 4


def trace(ref, c, v, f):
    a, s = f // 2, f % 2
    at = v * DOFS
    if a == 0:
        return ref[c, at + 48 * s : at + 48 * s + 16, :]
    if a == 1:
        out = []
        for h in range(2):
            r = at + 32 * h + 8 * s
            x = ref[c, r : r + 8, :]
            y = ref[c, r + 16 : r + 24, :]
            low = lower_half(x.shape)
            if s == 0:
                out.append(jnp.where(low, x, pltpu.roll(y, 4, 0)))
            else:
                out.append(jnp.where(low, pltpu.roll(x, 4, 0), y))
        return jnp.concatenate(out, axis=0)
    return ref[c, pl.ds(at + 3 * s, 16, stride=4), :]


def add_on_face(ref, c, v, f, x):
    a, s = f // 2, f % 2
    at = v * DOFS
    if a == 0:
        ref[c, at + 48 * s : at + 48 * s + 16, :] += x
    elif a == 1:
        for h in range(2):
            y = x[8 * h : 8 * h + 8, :]
            low = lower_half(y.shape)
            keep = low if s == 0 else ~low
            turned = pltpu.roll(y, 4, 0)
            first, second = (y, turned) if s == 0 else (turned, y)
            r = at + 32 * h + 8 * s
            ref[c, r : r + 8, :] += jnp.where(keep, first, 0.0)
            ref[c, r + 16 : r + 24, :] += jnp.where(keep, second, 0.0)
    else:
        spot = (c, pl.ds(at + 3 * s, 16, stride=4), slice(None))
        ref[spot] = ref[spot] + x


def wide(ref, rows):
    return jnp.concatenate([ref[c, 0:rows, :] for c in range(ref.shape[0])], axis=1)


def pressure_of(w, u):
    return (HEAT - 1.0) * (w[4] - 0.5 * (w[1] * u[0] + w[2] * u[1] + w[3] * u[2]))


def axis_flux(w, u, p, a):
    un = u[a]
    out = [w[1 + a]]
    for c in range(3):
        m = w[1 + c] * un
        out.append(m + p if c == a else m)
    out.append((w[4] + p) * un)
    return out


def side_term(w, f):
    sign = 1.0 if f % 2 else -1.0
    u = [w[1 + c] / w[0] for c in range(3)]
    p = pressure_of(w, u)
    flux = axis_flux(w, u, p, f // 2)
    return [(sign * flux[v]) - SPEED * w[v] for v in range(FIELDS)]


def asked_code(ask):
    return jnp.concatenate([ask[t : t + 1, :] for t in range(ask.shape[0])], axis=1)


def gather(fields, hot):
    high, low = split(fields)
    both = dot(jnp.concatenate([high, low], axis=0), hot)
    return both[0:ROWS] + both[ROWS:]


def pick_faces(got_ref, ask, outs):
    for t in range(ask.shape[0]):
        face = ask[t : t + 1, :] >> 9
        for v in range(FIELDS):
            x = trace(got_ref, t, v, 0)
            for f in range(1, 6):
                x = jnp.where(face == f, trace(got_ref, t, v, f), x)
            outs[t][16 * v : 16 * v + 16, :] = x


def reply(fields, ask, hot, got_ref, outs):
    got = gather(fields, hot)
    for t in range(ask.shape[0]):
        got_ref[t] = got[:, CAP * t : CAP * t + CAP]
    pick_faces(got_ref, ask, outs)


def hot_kernel(me_ref, far_ref, ask_ref, home_ref, sib_ref, rest_ref, reply_ref, base_ref, pre_ref):
    even = (me_ref[0] & 1) == 0
    for c in range(2):
        sib = sib_ref[:, 128 * c : 128 * c + 128]
        base_ref[c] = home_ref[c] + jnp.where(even, 0.0, sib)
        base_ref[c + 2] = home_ref[c + 2] + jnp.where(even, sib, 0.0)
    hot = one_hot_rows(NEW_DEV, asked_code(ask_ref[4:8, :]) & (NEW_DEV - 1))
    reply_ref[...] = hot
    got = gather(wide(base_ref, ROWS), hot)
    for t in range(4):
        pre_ref[t] = got[:, CAP * t : CAP * t + CAP]
    for f in range(6):
        rest_ref[f] = one_hot_rows(3 * CAP, far_ref[f : f + 1, :])


def own_kernel(fields_ref, ask_ref, a_ref, b_ref, sib_ref, got_ref):
    ask = ask_ref[0:4, :]
    hot = one_hot_rows(NEW_DEV, asked_code(ask) & (NEW_DEV - 1))
    outs = [a_ref.at[0], a_ref.at[1], b_ref.at[0], sib_ref.at[0]]
    reply(wide(fields_ref, ROWS), ask, hot, got_ref, outs)


def first_kernel(me_ref, base_ref, pre_ref, far_ref, ask_ref, hot_ref, start_ref, swap_ref, got_ref):
    odd = me_ref[0] & 1
    got = gather(far_ref[0:ROWS, :], hot_ref[pl.ds(pl.multiple_of(odd * HALF, HALF), HALF), :])
    for t in range(4):
        got_ref[t] = pre_ref[t] + got[:, CAP * t : CAP * t + CAP]
    pick_faces(got_ref, ask_ref[4:8, :], [swap_ref.at[t] for t in range(4)])
    for c in range(2):
        far = far_ref[:, 128 * c : 128 * c + 128]
        start_ref[c] = base_ref[c] + jnp.where(odd == 0, far, 0.0)
        start_ref[c + 2] = base_ref[c + 2] + jnp.where(odd == 0, 0.0, far)


def near_kernel(table_ref, fields_ref, near_ref, part_ref, high_ref, low_ref):
    for c in range(BLOCKS):
        spot = slice(128 * c, 128 * c + 128)
        w = [fields_ref[c, DOFS * v : DOFS * v + DOFS, :] for v in range(FIELDS)]
        u = [w[1 + i] / w[0] for i in range(3)]
        p = pressure_of(w, u)
        for a in range(3):
            flux = axis_flux(w, u, p, a)
            for v in range(FIELDS):
                high, low = split(flux[v])
                high_ref[v, DOFS * a : DOFS * a + DOFS, spot] = high
                low_ref[v, DOFS * a : DOFS * a + DOFS, spot] = low
    table = table_ref[...]
    for v in range(FIELDS):
        x = dot(table, high_ref[v])
        x = x[0:DOFS] + x[DOFS:] + dot(table[0:DOFS], low_ref[v])
        for c in range(BLOCKS):
            part_ref[c, DOFS * v : DOFS * v + DOFS, :] = x[:, 128 * c : 128 * c + 128]
    for f in range(6):
        hot = one_hot_rows(NEW_DEV, near_ref[f : f + 1, :])
        across = jnp.concatenate(
            [
                jnp.concatenate([trace(fields_ref, c, v, f ^ 1) for v in range(FIELDS)], axis=0)
                for c in range(BLOCKS)
            ],
            axis=1,
        )
        high, low = split(across)
        both = dot(jnp.concatenate([high, low], axis=0), hot)
        for c in range(BLOCKS):
            spot = slice(128 * c, 128 * c + 128)
            outer = both[0:TRACE_ROWS, spot] + both[TRACE_ROWS:, spot]
            there = near_ref[f : f + 1, spot] >= 0
            w = [outer[16 * v : 16 * v + 16] for v in range(FIELDS)]
            w[0] = jnp.where(there, w[0], 1.0)
            plus = side_term(w, f)
            minus = side_term([trace(fields_ref, c, v, f) for v in range(FIELDS)], f)
            for v in range(FIELDS):
                add_on_face(part_ref, c, v, f, 3.0 * (jnp.where(there, plus[v], 0.0) - minus[v]))


def ghost_terms(ghost, ask):
    face = (ask >> 9) ^ 1
    axis = face >> 1
    sign = jnp.where((face & 1) == 1, 3.0, -3.0)
    w = [ghost[16 * v : 16 * v + 16] for v in range(FIELDS)]
    u = [w[1 + c] / w[0] for c in range(3)]
    p = pressure_of(w, u)

    def along(x):
        return jnp.where(axis == 0, x[0], jnp.where(axis == 1, x[1], x[2]))

    un = along(u)
    flux = [along(w[1:4])]
    for c in range(3):
        flux.append(w[1 + c] * un + jnp.where(axis == c, p, 0.0))
    flux.append((w[4] + p) * un)
    return jnp.concatenate([sign * flux[v] - (3.0 * SPEED) * w[v] for v in range(FIELDS)], axis=0)


def ghost_rows(ghosts, ask_ref):
    parts = [split(ghost_terms(g, ask_ref[t])) for t, g in enumerate(ghosts)]
    high = jnp.concatenate([p[0] for p in parts], axis=1)
    low = jnp.concatenate([p[1] for p in parts], axis=1)
    return jnp.concatenate([high, low], axis=0)


def add_ghosts(sum_ref, lhs, hot_of, blocks=range(BLOCKS)):
    for f in range(6):
        both = dot(lhs, hot_of(f))
        for i, c in enumerate(blocks):
            spot = slice(128 * i, 128 * i + 128)
            term = both[0:TRACE_ROWS, spot] + both[TRACE_ROWS:, spot]
            for v in range(FIELDS):
                add_on_face(sum_ref, c, v, f, term[16 * v : 16 * v + 16])


def direct_kernel(part_ref, far_ref, ask_ref, a_ref, b_ref, sib_ref, sum_ref):
    lhs = ghost_rows([sib_ref[0], a_ref[2], a_ref[0], b_ref[1], b_ref[0]], ask_ref)
    sum_ref[...] = part_ref[...]
    add_ghosts(sum_ref, lhs, lambda f: one_hot_rows(5 * CAP, far_ref[f : f + 1, :] - 3 * CAP))


def metric_of(start_ref, c):
    return jnp.where(start_ref[c, ROWS : ROWS + 1, :] > 0.5, 2.0, 1.0)


def second_kernel(start_ref, part_ref, rest_ref, own_ask_ref, post_ref, ask_ref, hot_ref,
                  section_ref, swap_ref, sum_ref, got_ref):
    lhs = ghost_rows([post_ref[1], post_ref[0], post_ref[2]], own_ask_ref)
    sum_ref[...] = part_ref[...]
    add_ghosts(sum_ref, lhs, lambda f: rest_ref[f])
    for c in range(BLOCKS):
        section_ref[c] = start_ref[c, 0:ROWS, :] - (DT * metric_of(start_ref, c)) * sum_ref[c]
    reply(wide(section_ref, ROWS), ask_ref[4:8, :], hot_ref[...], got_ref, [swap_ref.at[t] for t in range(4)])


def last_kernel(start_ref, section_ref, part_ref, rest_ref, own_ask_ref, post_ref,
                state_hbm, rate_hbm, sum_ref, state_ref, rate_ref, sems):
    lhs = ghost_rows([post_ref[1], post_ref[0], post_ref[2]], own_ask_ref)
    sum_ref[...] = part_ref[...]
    copies = []
    for half in range(2):
        pair = (2 * half, 2 * half + 1)
        add_ghosts(sum_ref, lhs, lambda f: rest_ref[f, :, HALF * half : HALF * half + HALF], pair)
        for c in pair:
            rate = -metric_of(start_ref, c) * sum_ref[c]
            rate_ref[c] = rate
            state_ref[c] = 0.5 * start_ref[c, 0:ROWS, :] + 0.5 * (section_ref[c] + DT * rate)
            for i, (src, dst) in enumerate(((rate_ref, rate_hbm), (state_ref, state_hbm))):
                copy = pltpu.make_async_copy(src.at[c], dst.at[:, pl.ds(128 * c, 128)], sems.at[i, c])
                copy.start()
                copies.append(copy)
    for copy in copies:
        copy.wait()


VM = pl.BlockSpec(memory_space=pltpu.VMEM)
SM = pl.BlockSpec(memory_space=pltpu.SMEM)
HB = pl.BlockSpec(memory_space=pltpu.HBM)


def call(kernel, outs, args, specs=None, scratch=(), flops=10**6, outs_in=None):
    return pl.pallas_call(
        kernel,
        out_shape=[jax.ShapeDtypeStruct(s, d) for s, d in outs],
        in_specs=specs or [VM] * len(args),
        out_specs=[outs_in or VM] * len(outs),
        scratch_shapes=[pltpu.VMEM(*s) if isinstance(s, tuple) else s for s in scratch],
        compiler_params=pltpu.CompilerParams(vmem_limit_bytes=24 * 2**20),
        cost_estimate=pl.CostEstimate(flops=flops, bytes_accessed=2**20, transcendentals=0),
    )(*args)


def swap_cores(x):
    n = lax.axis_size(AXES)
    return lax.ppermute(x, AXES, [(i, i ^ 1) for i in range(n)])


def swap_chips(x):
    n = lax.axis_size(AXES)
    return lax.ppermute(x, AXES, [(i, (i + (1 if i % 2 else -1)) % n) for i in range(n)])


def outward(x, by):
    n = lax.axis_size(AXES)
    return lax.ppermute(x, AXES, [(i, (i + (by if i % 2 == 0 else -by)) % n) for i in range(n)])


def outward_pair(own, got):
    b = outward(jnp.concatenate([own[1], got[2:4]], axis=0), 4)
    a = outward(jnp.concatenate([own[0], got[0:2]], axis=0), 2)
    return a, b


def swap_back(a, b):
    return swap_cores(jnp.concatenate([a[1:2], a[3:4], b[2:3]], axis=0))


def body(state_old, level_old, morton_old, neighbours):
    me = lax.axis_index(AXES).astype(I32).reshape(1)
    inputs = [
        pltpu.with_memory_space_constraint(x, pltpu.HBM)
        for x in (
            neighbours,
            state_old.reshape(ROWS, OLD_CAP),
            level_old.reshape(1, OLD_CAP),
            morton_old.reshape(1, OLD_CAP),
        )
    ]
    own_ask, swap_ask, near, far, state, level, morton = call(
        open_kernel,
        [
            ((3, 1, CAP), I32),
            ((5, 1, CAP), I32),
            ((6, NEW_DEV), I32),
            ((6, NEW_DEV), I32),
            ((ROWS, OLD_CAP), F32),
            ((1, OLD_CAP), I32),
            ((1, OLD_CAP), I32),
        ],
        (me, *inputs),
        [SM, HB, HB, HB, HB],
        [((6, NEW_DEV), I32), pltpu.SemaphoreType.DMA((4,))],
    )
    got = swap_cores(swap_ask)
    relay = [SM, VM, VM, VM]
    moved = ((MOVED_ROWS, HALF), F32)
    (to_far,) = call(far_kernel, [moved], (me, state, level, morton), relay)
    got, to_far = lax.optimization_barrier((got, to_far))
    a, b = outward_pair((own_ask[0:2], own_ask[2:3]), got[1:5])
    from_far = swap_chips(to_far)
    a, morton = lax.optimization_barrier((a, morton))
    (to_sib,) = call(sib_kernel, [moved], (me, state, level, morton), relay, flops=10**9)
    from_sib = swap_cores(to_sib)
    (home,) = call(home_kernel, [((BLOCKS, MOVED_ROWS, 128), F32)], (me, state, level, morton), relay)
    post = swap_back(a, b)
    asked = jnp.concatenate(
        [post[1], post[0], post[2], got[0], a[2], a[0], b[1], b[0]], axis=0
    )

    rest_hot, reply_hot, base, pre = call(
        hot_kernel,
        [
            ((6, 3 * CAP, NEW_DEV), BF16),
            ((NEW_DEV, 4 * CAP), BF16),
            ((BLOCKS, MOVED_ROWS, 128), F32),
            ((4, ROWS, CAP), F32),
        ],
        (me, far, asked, home, from_sib),
        [SM, VM, VM, VM, VM],
        flops=10**9,
    )
    swapped = ((4, TRACE_ROWS, CAP), F32)
    got_scratch = ((4, ROWS, CAP), F32)
    blocks = ((BLOCKS, ROWS, 128), F32)
    table = jnp.asarray(stacked_table())

    def neighbours_of(fields, swap):
        got = swap_cores(swap)
        *own, sib = call(
            own_kernel,
            [((2, TRACE_ROWS, CAP), F32), ((1, TRACE_ROWS, CAP), F32), ((1, TRACE_ROWS, CAP), F32)],
            (fields, asked),
            None,
            [got_scratch],
            flops=10**9,
        )
        a, b = outward_pair(own, got)
        (part,) = call(
            near_kernel,
            [blocks],
            (table, fields, near),
            None,
            [((FIELDS, 3 * DOFS, NEW_DEV), BF16)] * 2,
            flops=10**9,
        )
        sib, part = lax.optimization_barrier((sib, part))
        sib = swap_cores(sib)
        a, b, part = lax.optimization_barrier((a, b, part))
        post = swap_back(a, b)
        (part,) = call(direct_kernel, [blocks], (part, far, swap_ask, a, b, sib), flops=10**9)
        return part, rest_hot, own_ask, post

    start, swap = call(
        first_kernel,
        [((BLOCKS, MOVED_ROWS, 128), F32), swapped],
        (me, base, pre, from_far, asked, reply_hot),
        [SM, VM, VM, VM, VM, VM],
        [got_scratch],
    )
    ghosts = neighbours_of(start, swap)
    section, swap = call(
        second_kernel,
        [blocks, swapped],
        (start, *ghosts, asked, reply_hot),
        None,
        [blocks, got_scratch],
    )
    ghosts = neighbours_of(section, swap)
    new_state, rate = call(
        last_kernel,
        [((ROWS, NEW_DEV), F32)] * 2,
        (start, section, *ghosts),
        None,
        [blocks, blocks, blocks, pltpu.SemaphoreType.DMA((2, BLOCKS))],
        outs_in=HB,
    )
    shape = (FIELDS, DOFS, NEW_DEV)
    return new_state.reshape(shape), rate.reshape(shape)


def solution(mesh):
    wide = P(None, None, AXES)
    return jax.shard_map(
        body,
        mesh=mesh,
        in_specs=(wide, P(AXES), P(AXES), P(None, AXES)),
        out_specs=(wide, wide),
        check_vma=False,
    )
```
